128 devices in a mesh: dp: 16 (over x, y_hi, core), llm: 8 (over z, y_lo).
Axes of the slice: x: 4, y: 4 (y_hi: 2, y_lo: 2; y = y_hi * 2 + y_lo), z: 4, core: 2. Of those that a mesh axis runs over, the one named last changes fastest.
Arguments:
- token_grads: bfloat16 [8192, 8192], P(('dp', 'llm')), may hold values from -6 to 6
- token_dest: int32 [8192, 1], P(('dp', 'llm')), may hold values from 0 to 15; in each aligned block of 64 rows (0 to 63, 64 to 127, ...) at most 8 rows name the same one
- merger_down: bfloat16 [5120, 8192], P('llm'), may hold values from -0.078125 to 0.078125
- merger_up: bfloat16 [5120, 5120], P(None, 'llm'), may hold values from -0.078125 to 0.078125
- merger_pre: bfloat16 [8192, 5120], P('dp', 'llm'), may hold values from -6 to 6
- layer_input: bfloat16 [65536, 1280], P(('dp', 'llm')), may hold values from -6 to 6
- window_ids: int32 [128, 512], P(('dp', 'llm')), may hold values from 0 to 15, never falling along the last dimension, each value on 1 to 64 neighbouring positions
- norm_gain: float32 [1280], replicated, may hold values from 0.25 to 1.75
- merge_gain: float32 [1280], replicated, may hold values from 0.25 to 1.75
- qkv_weight: bfloat16 [1280, 1920], P('dp'), may hold values from -1.5 to 1.5
- proj_weight: bfloat16 [640, 1280], P('dp'), may hold values from -0.25 to 0.25
Outputs:
- layer_grad: bfloat16 [65536, 1280], P(('dp', 'llm'))
- qkv_grad: float32 [1280, 1920], P('dp')
- proj_grad: float32 [640, 1280], P('dp')
The draws below stay inside these ranges and needn't reach their ends.
Inputs may be any that keep to these rules, and one draw needn't show every extreme that they name: `token_dest`: among the 64 tokens of one device, at most 8 name the same vision group. `window_ids`: windows are runs of consecutive patch slots of one vision device, each at most 64 long.
All inputs are finite; a program needn't handle non-finite values.
Results may differ from the reference program's by a relative error of at most 0.035.
The reference program's roundings to bfloat16 on the way (of `pre_grad`, `merged` and `cotangent`) count: a program that leaves them out, or rounds other values in their place, can miss the bound.
Values may be sent and summed in bfloat16 or wider, within the bound.
A program may use at most 128 MiB of HBM per device.

```python
import math
import jax
import jax.numpy as jnp
import numpy as np
from jax import lax

D_LLM = 8192
D_VIT = 1280
MRG_HID = 5120
HEAD_DIM = 80
HEADS = 8
MERGE = 4
WIN = 64
TOK_DEV = 64
CAP = 8
TOKENS = 8192
PCAP = 512
NWIN = 16
ATT = 640
N_DP = 16
N_LLM = 8


def draw_layer_input(key, part):
    key = jax.random.fold_in(key, 11)
    row_total = N_DP * N_LLM * PCAP
    values = jax.random.normal(key, (row_total, D_VIT), jnp.float32)
    return jnp.clip(values, -6.0, 6.0).astype(jnp.bfloat16)


def draw_qkv_weight(key, part):
    key = jax.random.fold_in(key, 23)
    values = jax.random.normal(key, (D_VIT, 3 * HEADS * HEAD_DIM), jnp.float32)
    values = jnp.clip(values, -6.0, 6.0) * D_VIT ** (-0.5)
    return jnp.clip(values, -1.5, 1.5).astype(jnp.bfloat16)


def level_of(rng, dims, split, low, high):
    level, own = 1.0, jax.random.fold_in(rng, 6)
    for position, parts in split:
        heights = jnp.exp(jax.random.uniform(jax.random.fold_in(own, position), (parts,), jnp.float32, low / len(split), high / len(split)))
        level = level * jnp.repeat(heights, dims[position] // parts).reshape([-1 if axis == position else 1 for axis in range(len(dims))])
    return level


def profile(number_of, total, limit, skew):
    portions = [(1 << 20) // math.isqrt(standing ** skew) + 1 for standing in range(2, number_of + 1)]
    spare, holding = total - limit - (number_of - 1), [1] * (number_of - 1)
    while spare > 0:
        movable = [i for i in range(number_of - 1) if holding[i] < limit]
        mass, remaining = sum([portions[i] for i in movable]), spare
        for i in movable:
            extra = min(limit - holding[i], max(1, remaining * portions[i] // mass), spare)
            holding[i] = holding[i] + extra
            spare = spare - extra
    return np.array([limit] + holding)


def uneven_parts(key, number_of, total, reach, slope):
    if number_of == 2:
        one = jax.random.randint(key, (), max(1, total - reach), min(reach, total - 1) + 1)
        return jnp.stack([one, total - one])
    tallies = jnp.asarray(profile(number_of, total, reach, slope), jnp.int32)
    twos = (number_of - 1) // 2
    donor, sink = tallies[1:1 + 2 * twos:2], tallies[2:2 + 2 * twos:2]
    room = jnp.minimum(donor - 1, reach - sink)
    shifted = jax.random.randint(jax.random.fold_in(key, 1), (twos,), 0, 1 << 20) % (room + 1)
    tallies = tallies.at[1:1 + 2 * twos:2].set(donor - shifted).at[2:2 + 2 * twos:2].set(sink + shifted)
    return tallies[jax.random.permutation(jax.random.fold_in(key, 2), number_of)]


def shared_out(stream_key, own, number, rows, count, top, bound, slope):
    order = jax.random.permutation(stream_key, count)
    packed, ordinary = shares(count, rows * top, bound, slope, True), shares(count, rows * top, bound, slope, False)
    places = jnp.arange(count)

    def named(sizes, rotation):
        used = int((sizes > 0).sum())
        fixed = max(1, used // 4)
        shifted = fixed + (places - fixed + rotation * (used - fixed)) % max(1, count - fixed)
        return jnp.zeros((count,), jnp.int32).at[order[jnp.where(places < fixed, places, shifted)]].set(jnp.asarray(sizes, jnp.int32))

    sizes = jnp.where(number % 4 == 0, named(packed, number // 4), named(ordinary, number - number // 4 - 1))
    mixed = jax.random.permutation(jax.random.fold_in(own, 3), count)
    giver, sink = mixed[0:count // 2 * 2:2], mixed[1:count // 2 * 2:2]
    room = jnp.minimum(sizes[giver] - 1, bound - sizes[sink]) // 2
    room = jnp.where((giver == order[0]) | (sink == order[0]) | (sizes[sink] == 0), 0, jnp.maximum(room, 0))
    shifted = jax.random.randint(jax.random.fold_in(own, 4), (count // 2,), 0, 1 << 20) % (room + 1)
    sizes = sizes.at[giver].add(-shifted).at[sink].add(shifted)
    members = jnp.searchsorted(jnp.cumsum(sizes), jnp.arange(rows * top), side="right").astype(jnp.int32)
    table = members.reshape(top, rows).T
    table = table[jax.random.permutation(jax.random.fold_in(own, 1), rows)]
    rotation = jax.random.randint(jax.random.fold_in(own, 2), (rows, 1), 0, top)
    return jnp.take_along_axis(table, (jnp.arange(top)[None, :] + rotation) % top, axis=1)


def shares(number_of, total, bound, slope, full):
    portions = [(1 << 20) // math.isqrt(grade ** slope) + 1 for grade in range(1, number_of + 1)]
    largest = bound if full else min(bound, max(-(-total // number_of), total * portions[0] // sum(portions)))
    least = 1 if total - largest >= number_of - 1 else 0
    given, spare = [largest] + [least] * (number_of - 1), total - largest - least * (number_of - 1)
    while spare > 0:
        candidates = [i for i in range(1, number_of) if given[i] < largest] or [i for i in range(1, number_of) if given[i] < bound]
        mass, left = sum([portions[i] for i in candidates]), spare
        for i in candidates:
            extra = min(bound - given[i], max(1, left * portions[i] // mass), spare)
            given[i] = given[i] + extra
            spare = spare - extra
    return np.array(given)


def scatter_about(key, shape, scale, reach, split=(), kind=jnp.bfloat16):
    array = jax.random.normal(key, shape, jnp.float32) * scale
    if len(split) > 0:
        array = level_of(key, shape, split, -0.22, 0.18) * array
    return jnp.clip(array, min=-reach, max=reach).astype(kind)


def setup_inputs(seed: int = 0) -> dict:
    streams_of = jax.random.split(jax.random.key(seed), 12)
    token_grads = scatter_about(streams_of[0], (TOKENS, D_LLM), 1.0, 6.0, ((0, 128),))
    token_dest_keys = jax.random.split(jax.random.fold_in(streams_of[1], 1), TOKENS // TOK_DEV)
    token_dest_turns = jax.random.permutation(jax.random.fold_in(streams_of[1], 3), TOKENS // TOK_DEV)
    token_dest = jax.vmap(lambda own, number: shared_out(jax.random.fold_in(streams_of[1], 2), own, number, TOK_DEV, N_DP, 1, CAP, 2))(token_dest_keys, token_dest_turns).reshape((TOKENS, 1))
    merger_down = scatter_about(streams_of[2], (MRG_HID, D_LLM), MRG_HID ** -0.5, 0.078125, ((0, 8),))
    merger_up = scatter_about(streams_of[3], (MERGE * D_VIT, MRG_HID), (MERGE * D_VIT) ** -0.5, 0.078125, ((1, 8),))
    merger_pre = scatter_about(streams_of[4], (TOKENS, MRG_HID), 1.0, 6.0, ((0, 16), (1, 8)))
    layer_input = draw_layer_input(jax.random.fold_in(streams_of[11], 71), 0)
    window_ids = jax.vmap(lambda own: jnp.searchsorted(jnp.cumsum(uneven_parts(own, NWIN, PCAP, WIN, 1)), jnp.arange(PCAP), side="right"))(jax.random.split(streams_of[6], (N_DP * N_LLM))).reshape((N_DP * N_LLM, PCAP)).astype(jnp.int32)
    norm_gain = jnp.clip(1.0 + 0.15 * jax.random.normal(streams_of[7], (D_VIT,), jnp.float32), 0.25, 1.75)
    merge_gain = jnp.clip(1.0 + 0.15 * jax.random.normal(streams_of[8], (D_VIT,), jnp.float32), 0.25, 1.75)
    qkv_weight = draw_qkv_weight(jax.random.fold_in(streams_of[11], 71), 0)
    proj_weight = scatter_about(streams_of[10], (ATT, D_VIT), ATT ** -0.5, 0.25, ((0, 16),))
    return {"token_grads": token_grads, "token_dest": token_dest, "merger_down": merger_down, "merger_up": merger_up, "merger_pre": merger_pre, "layer_input": layer_input, "window_ids": window_ids, "norm_gain": norm_gain, "merge_gain": merge_gain, "qkv_weight": qkv_weight, "proj_weight": proj_weight}


EPSILON = 1e-06

def gelu_slope(values):
    return 0.5 * (1.0 + jax.scipy.special.erf(values * 0.7071067811865476)) + values * jnp.exp(-0.5 * values * values) * 0.3989422804014327

def rms_scale(values, scaling):
    return values * lax.rsqrt(lax.optimization_barrier(jnp.mean(values * values, axis=-1, keepdims=True)) + EPSILON) * scaling

def vision_forward(layer_in, packed_weight, output_weight, windows, norm_gain, merge_gain):
    patches = layer_in.shape[0]
    head_count = output_weight.shape[0] // HEAD_DIM
    widened = layer_in.astype(jnp.float32)
    normed = rms_scale(widened, norm_gain).astype(jnp.bfloat16)
    projected = jnp.dot(normed, packed_weight, preferred_element_type=jnp.float32).astype(jnp.bfloat16)
    triple = projected.reshape(patches, 3, head_count, HEAD_DIM).astype(jnp.float32)
    scores = jnp.einsum('qhd,khd->hqk', triple[:, 0], triple[:, 1]) * HEAD_DIM ** (-0.5)
    same_window = windows[:, None] == windows[None, :]
    scores = jnp.where(same_window[None], scores, -1e+30)
    attention = jax.nn.softmax(scores, axis=-1).astype(jnp.bfloat16)
    combined = jnp.einsum('hqk,khd->qhd', attention.astype(jnp.float32), triple[:, 2])
    combined = combined.reshape(patches, head_count * HEAD_DIM).astype(jnp.bfloat16)
    output = widened + jnp.dot(combined, output_weight, preferred_element_type=jnp.float32)
    return rms_scale(output, merge_gain)

def vision_backward(layer_in, packed_weight, output_weight, windows, norm_gain, merge_gain, cotangent):

    def forward(layer_arg, packed_arg, output_arg):
        return vision_forward(layer_arg, packed_arg, output_arg, windows, norm_gain, merge_gain)
    _, pullback = jax.vjp(forward, layer_in, packed_weight, output_weight)
    return pullback(cotangent.astype(jnp.float32))

def reference(token_grads, token_dest, merger_down, merger_up, merger_pre, layer_input, window_ids, norm_gain, merge_gain, qkv_weight, proj_weight):
    device_count = N_DP * N_LLM
    groups = token_grads.reshape(N_DP, TOK_DEV * N_LLM, D_LLM)
    saved_pre = merger_pre.reshape(N_DP, TOK_DEV * N_LLM, MRG_HID)

    def merger_group(arrays):
        grads_here, saved_here = arrays
        hidden_grad = lax.dot_general(grads_here, merger_down, (((1,), (1,)), ((), ())), preferred_element_type=jnp.float32)
        pre_grad = (hidden_grad * gelu_slope(saved_here.astype(jnp.float32))).astype(jnp.bfloat16)
        summed = lax.dot_general(pre_grad, merger_up, (((1,), (1,)), ((), ())), preferred_element_type=jnp.float32)
        return summed.astype(jnp.bfloat16)
    merged = lax.map(merger_group, (groups, saved_pre)).reshape(TOKENS, MERGE * D_VIT)
    targets = token_dest[:, 0].reshape(device_count, TOK_DEV)
    onehot = (targets[:, :, None] == jnp.arange(N_DP, dtype=jnp.int32)[None, None, :]).astype(jnp.int32)
    slot_rank = lax.optimization_barrier(jnp.sum((jnp.cumsum(onehot, axis=1) - onehot) * onehot, axis=2))
    device_ids = jnp.arange(device_count, dtype=jnp.int32)[:, None]
    vision_ids = targets * N_LLM + device_ids % N_LLM
    slot_index = device_ids // N_LLM * CAP + slot_rank
    flat_index = (vision_ids * (N_DP * CAP) + slot_index).reshape(-1).astype(jnp.int32)
    cotangents = jnp.zeros((device_count * N_DP * CAP, MERGE * D_VIT), jnp.bfloat16).at[flat_index].set(merged)
    cotangents = cotangents.reshape(device_count, PCAP, D_VIT)

    def vision_step(totals, stacked):
        layer_in, windows, cotangent = stacked
        layer_grad, packed_term, output_term = vision_backward(layer_in, qkv_weight, proj_weight, windows, norm_gain, merge_gain, cotangent)
        return ((totals[0] + packed_term.astype(jnp.float32), totals[1] + output_term.astype(jnp.float32)), layer_grad)
    starting = (jnp.zeros(qkv_weight.shape, jnp.float32), jnp.zeros(proj_weight.shape, jnp.float32))
    totals, layer_grads = lax.scan(vision_step, starting, (layer_input.reshape(device_count, PCAP, D_VIT), window_ids, cotangents))
    return (layer_grads.reshape(device_count * PCAP, D_VIT), totals[0] / device_count, totals[1] / device_count)
```

```python
import jax
import jax.numpy as jnp
from jax import lax
from jax.experimental import pallas as pl
from jax.experimental.pallas import tpu as pltpu
from jax.sharding import PartitionSpec as P

MESH = pl.DeviceIdType.MESH
HEAD_DIM = 80
CAP = 8
EPSILON = 1e-06
BF16 = jnp.bfloat16
F32 = jnp.float32

NT = (((1,), (1,)), ((), ()))
TN = (((0,), (0,)), ((), ()))

N_TOK = 8
N_FEAT = 8


def gelu_slope(values):
    return (
        0.5 * (1.0 + lax.erf(values * 0.7071067811865476))
        + values * jnp.exp(-0.5 * values * values) * 0.3989422804014327
    )


def rms_scale(values, scaling):
    return values * lax.rsqrt(jnp.mean(values * values, axis=-1, keepdims=True) + EPSILON) * scaling


def place():
    d, l = lax.axis_index("dp"), lax.axis_index("llm")
    return d // 4, (d // 2) % 2, d % 2, l // 2, l % 2


def at(x, yh, c, z, yl):
    return (x * 2 + yh) * 2 + c, z * 2 + yl


def remote(src, dst, send, recv, device):
    return pltpu.make_async_remote_copy(
        src_ref=src, dst_ref=dst, send_sem=send, recv_sem=recv, device_id=device, device_id_type=MESH
    )


def greet(devices):
    barrier = pltpu.get_barrier_semaphore()
    for device in devices:
        pl.semaphore_signal(barrier, inc=1, device_id=device, device_id_type=MESH)
    pl.semaphore_wait(barrier, len(devices))


def merger_kernel(
    tok, dest, down, up, pre, qw, ow,
    cot, wq, wo,
    G, down_v, up_v, slope, acc, pg, pre2,
    S, R, own, T, T0, ZR, M, OUT, A,
    loc, zs, zr, ys, yr, ps, pr, ws, wr, xs, xr, cs, cr, rys, ryr, rzs, rzr, as_, ar,
):
    x, yh, c, z, yl = place()
    d = (x * 2 + yh) * 2 + c
    l = z * 2 + yl
    zp = [at(x, yh, c, (z + s) % 4, yl) for s in (1, 2, 3)]
    p1 = at(x, yh, c, z, 1 - yl)
    p2 = at(x, 1 - yh, c, z, 1 - yl)
    yhp = at(x, 1 - yh, c, z, yl)
    xp = [at((x + s) % 4, yh, c, z, yl) for s in (1, 2, 3)]
    core = at(x, yh, 1 - c, z, yl)
    dps = [((d + s) % 16, l) for s in range(1, 16)]

    cp_tok = pltpu.make_async_copy(tok, G.at[0, pl.ds(0, 64)], loc.at[0])
    cp_down = pltpu.make_async_copy(down, down_v, loc.at[1])
    cp_up = pltpu.make_async_copy(up, up_v, loc.at[2])
    cp_tok.start()
    cp_down.start()
    cp_up.start()
    greet(zp + [p1, p2] + dps)
    cp_tok.wait()

    W = G.shape[2] // N_TOK

    def col(k):
        return pl.ds(pl.multiple_of(k * W, W), W)

    def z_copy(k, i):
        return remote(
            G.at[0, pl.ds(0, 64), col(k)], G.at[3 - i, pl.ds(0, 64), col(k)], zs.at[k, i], zr.at[k, i], zp[i]
        )

    def y_copy(k, i):
        return remote(
            G.at[:, pl.ds(32 * i, 32), col(k)],
            G.at[:, pl.ds(64 + 32 * i, 32), col(k)],
            ys.at[k, i],
            yr.at[k, i],
            (p1, p2)[i],
        )

    for k in range(2):
        for i in (0, 2, 1):
            z_copy(k, i).start()

    def pre_copy(zz):
        rows = pl.ds(pl.multiple_of((2 * zz + 1 - yl) * 64 + 32, 32), 32)
        return remote(pre.at[rows], pre2.at[pl.ds(32 * zz, 32)], ps.at[zz], pr.at[zz], yhp)

    for zz in range(4):
        pre_copy(zz).start()

    def w_copies(source, index, sends, recvs, device):
        first = wq.at[index] if source is None else source[0]
        second = wo.at[index] if source is None else source[1]
        return [
            remote(first, wq.at[index], sends.at[0], recvs.at[0], device),
            remote(second, wo.at[index], sends.at[1], recvs.at[1], device),
        ]

    def flipped(dd):
        return dd + 2 - 4 * ((dd // 2) % 2)

    wq[d] = qw[...]
    wo[d] = ow[...]
    d2 = flipped(d)
    for cp in w_copies((qw, ow), d, ws.at[0], wr.at[0], p2):
        cp.start()
    for i in (0, 2, 1):
        for cp in w_copies((qw, ow), d, xs.at[0, i], xr.at[0, i], xp[i]):
            cp.start()
    for cp in w_copies((qw, ow), d, cs.at[0], cr.at[0], core):
        cp.start()

    for zz in range(4):
        pre_copy(zz).wait_recv()
    for r in range(4):
        zz = (z + r) % 4
        mine = pre[pl.ds(pl.multiple_of((2 * zz + yl) * 64, 64), 64), :]
        first = pre[pl.ds(pl.multiple_of((2 * zz + 1 - yl) * 64, 64), 32), :]
        second = pre2[pl.ds(pl.multiple_of(zz * 32, 32), 32), :]
        slope[r, 0:64, :] = gelu_slope(mine.astype(F32))
        slope[r, 64:96, :] = gelu_slope(first.astype(F32))
        slope[r, 96:128, :] = gelu_slope(second.astype(F32))
    acc[...] = jnp.zeros_like(acc)

    def multiply(k):
        for i in range(2):
            y_copy(k, i).wait_recv()
        tile = G[:, :, col(k)].reshape(512, W)
        acc[...] += lax.dot_general(tile, down_v[:, col(k)], NT, preferred_element_type=F32)

    cp_down.wait()

    def gather_step(k, carry):
        @pl.when(k + 2 < N_TOK)
        def _():
            for i in (0, 2, 1):
                z_copy(k + 2, i).start()

        for i in range(3):
            z_copy(k, i).wait_recv()
        for i in range(2):
            y_copy(k, i).start()

        @pl.when(k == 1)
        def _():
            for cp in w_copies((qw, ow), d2, ws.at[0], wr.at[0], p2):
                cp.wait_recv()
            for i in (0, 2, 1):
                for cp in w_copies(None, d2, xs.at[1, i], xr.at[1, i], xp[i]):
                    cp.start()
            for cp in w_copies(None, d2, cs.at[1], cr.at[1], core):
                cp.start()

        @pl.when(k >= 1)
        def _():
            multiply(k - 1)

        return carry

    lax.fori_loop(0, N_TOK, gather_step, 0)
    multiply(N_TOK - 1)

    def x_arrive(h):
        for i in range(3):
            other = ((x + i + 1) % 4 * 2 + yh) * 2 + c
            other = flipped(other) if h else other
            for cp in w_copies(None, other, xs.at[h, 2 - i], xr.at[h, 2 - i], xp[2 - i]):
                cp.wait_recv()
            for cp in w_copies(None, other, cs.at[2 + 3 * h + i], cr.at[2 + 3 * h + i], core):
                cp.start()

    x_arrive(0)

    pg[...] = (acc[...] * slope[...].reshape(512, slope.shape[2])).astype(BF16)
    cp_up.wait()

    token = dest[...]
    hot = (lax.broadcasted_iota(jnp.int32, (16, 64), 0) == token).astype(F32)
    before = (
        lax.broadcasted_iota(jnp.int32, (64, 64), 0) < lax.broadcasted_iota(jnp.int32, (64, 64), 1)
    ).astype(F32)
    rank = jnp.sum(jnp.dot(hot, before, preferred_element_type=F32) * hot, axis=0, keepdims=True)
    target = token * 16 + rank.astype(jnp.int32)
    row = lax.broadcasted_iota(jnp.int32, (256, 64), 0)
    placing = jnp.concatenate(
        [(row == target).astype(F32), (row == target + 8).astype(F32)], axis=1
    ).astype(BF16)

    V = M.shape[2]

    def ry_copy(f, i):
        return remote(S.at[f, i], R.at[f, i], rys.at[f, i], ryr.at[f, i], (p1, p2)[i])

    def rz_copy(f, i):
        return remote(T.at[f, i], ZR.at[f, i], rzs.at[f, i], rzr.at[f, i], zp[i])

    def a_copy(j, s):
        dd = (d + s) % 16
        return remote(
            OUT.at[j, pl.ds(pl.multiple_of(dd * 16, 16), 16)],
            A.at[j, pl.ds(pl.multiple_of(d * 16, 16), 16)],
            as_.at[j],
            ar.at[j],
            dps[s - 1],
        )

    def sum_step(i, carry):
        @pl.when(i < N_FEAT)
        def _():
            rows = pl.ds(pl.multiple_of(i * V, V), V)
            part = lax.dot_general(pg[...], up_v[rows, :], NT, preferred_element_type=F32)
            part = part.reshape(4, 128, V)
            S[i, 0] = part[:, 64:96, :].astype(BF16)
            S[i, 1] = part[:, 96:128, :].astype(BF16)
            for h in range(2):
                ry_copy(i, h).start()
            own[i % 2] = part[:, 0:64, :]

        @pl.when((i >= 1) & (i < N_FEAT + 1))
        def _():
            f = i - 1
            for h in range(2):
                ry_copy(f, h).wait_recv()
            total = own[f % 2] + jnp.concatenate([R[f, 0].astype(F32), R[f, 1].astype(F32)], axis=1)
            T[f] = total[1:4].astype(BF16)
            T0[f % 2] = total[0]
            for h in (0, 2, 1):
                rz_copy(f, h).start()

        @pl.when(i >= 2)
        def _():
            f = i - 2
            for h in range(3):
                rz_copy(f, h).wait_recv()
            M[f] = (
                T0[f % 2] + ZR[f, 0].astype(F32) + ZR[f, 1].astype(F32) + ZR[f, 2].astype(F32)
            ).astype(BF16)

            @pl.when(f % 2 == 1)
            def _():
                j = f // 2
                both = jnp.concatenate([M[f - 1], M[f]], axis=0)
                OUT[j] = jnp.dot(placing, both, preferred_element_type=F32).astype(BF16)
                for s in range(1, 16):
                    a_copy(j, s).start()
                here = pl.ds(pl.multiple_of(d * 16, 16), 16)
                A[j, here, :] = OUT[j, here, :]

        return carry

    lax.fori_loop(0, N_FEAT + 2, sum_step, 0)

    x_arrive(1)

    fifteen = pl.ds(0, 240)
    for j in range(4):
        pltpu.make_async_copy(A.at[j, fifteen], A.at[j, fifteen], ar.at[j]).wait()
    out_row = lax.broadcasted_iota(jnp.int32, (128, 256), 0)
    in_row = lax.broadcasted_iota(jnp.int32, (128, 256), 1)
    wanted = (out_row % 4) * 64 + (out_row // 32) * 16 + (out_row // 4) % 8
    for h in range(2):
        order = (in_row == wanted + 8 * h).astype(F32).astype(BF16)
        for g in range(4):
            stacked = A[:, 64 * g : 64 * g + 64, :].reshape(256, V)
            cot[128 * g : 128 * g + 128, V * h : V * h + V] = jnp.dot(
                order, stacked, preferred_element_type=F32
            ).astype(BF16)

    cidx = [d, d2]
    for h in range(2):
        for i in range(3):
            other = ((x + i + 1) % 4 * 2 + yh) * 2 + c
            cidx.append(flipped(other) if h else other)
    for n, index in enumerate(cidx):
        for cp in w_copies(None, index, cs.at[n], cr.at[n], core):
            cp.wait_send()
        theirs = index + 1 - 2 * c
        for cp in w_copies(None, theirs, cs.at[n], cr.at[n], core):
            cp.wait_recv()
    for cp in w_copies((qw, ow), d, ws.at[0], wr.at[0], p2):
        cp.wait_send()
    for h in range(2):
        for i in range(3):
            for cp in w_copies(None, d2 if h else d, xs.at[h, i], xr.at[h, i], xp[i]):
                cp.wait_send()
    for zz in range(4):
        pre_copy(zz).wait_send()

    def drain(k, carry):
        for i in range(3):
            z_copy(k, i).wait_send()
        for i in range(2):
            y_copy(k, i).wait_send()
        return carry

    lax.fori_loop(0, N_TOK, drain, 0)

    def drain2(f, carry):
        for i in range(2):
            ry_copy(f, i).wait_send()
        for i in range(3):
            rz_copy(f, i).wait_send()
        return carry

    lax.fori_loop(0, N_FEAT, drain2, 0)
    for j in range(4):
        pltpu.make_async_copy(OUT.at[j, fifteen], OUT.at[j, fifteen], as_.at[j]).wait()


def merger(tok, dest, down, up, pre, qw, ow):
    vm = pl.BlockSpec(memory_space=pltpu.VMEM)
    hbm = pl.BlockSpec(memory_space=pl.ANY)
    dma = pltpu.SemaphoreType.DMA
    hid = pre.shape[1]
    feat = up.shape[0]
    V = feat // N_FEAT
    return pl.pallas_call(
        merger_kernel,
        name="merger",
        out_shape=(
            jax.ShapeDtypeStruct((512, feat // 4), BF16),
            jax.ShapeDtypeStruct((16,) + qw.shape, BF16),
            jax.ShapeDtypeStruct((16,) + ow.shape, BF16),
        ),
        in_specs=[hbm, vm, hbm, hbm, vm, vm, vm],
        out_specs=(vm, vm, vm),
        scratch_shapes=[
            pltpu.VMEM((4, 128, tok.shape[1]), BF16),
            pltpu.VMEM(down.shape, BF16),
            pltpu.VMEM(up.shape, BF16),
            pltpu.VMEM((4, 128, hid), F32),
            pltpu.VMEM((512, hid), F32),
            pltpu.VMEM((512, hid), BF16),
            pltpu.VMEM((128, hid), BF16),
            pltpu.VMEM((N_FEAT, 2, 4, 32, V), BF16),
            pltpu.VMEM((N_FEAT, 2, 4, 32, V), BF16),
            pltpu.VMEM((2, 4, 64, V), F32),
            pltpu.VMEM((N_FEAT, 3, 64, V), BF16),
            pltpu.VMEM((2, 64, V), F32),
            pltpu.VMEM((N_FEAT, 3, 64, V), BF16),
            pltpu.VMEM((N_FEAT, 64, V), BF16),
            pltpu.VMEM((4, 256, V), BF16),
            pltpu.VMEM((4, 256, V), BF16),
            dma((3,)),
            dma((N_TOK, 3)), dma((N_TOK, 3)), dma((N_TOK, 2)), dma((N_TOK, 2)),
            dma((4,)), dma((4,)),
            dma((1, 2)), dma((1, 2)),
            dma((2, 3, 2)), dma((2, 3, 2)),
            dma((8, 2)), dma((8, 2)),
            dma((N_FEAT, 2)), dma((N_FEAT, 2)),
            dma((N_FEAT, 3)), dma((N_FEAT, 3)),
            dma((4,)), dma((4,)),
        ],
        compiler_params=pltpu.CompilerParams(
            collective_id=1, has_side_effects=True, vmem_limit_bytes=60 << 20
        ),
        cost_estimate=pl.CostEstimate(flops=9 * 10**9, bytes_accessed=40 * 10**6, transcendentals=0),
    )(tok, dest, down, up, pre, qw, ow)


def reduce_kernel(
    g, out,
    C, S, XR, ZR, E1, E2, XR2, ZR2, E, YR, F, FR,
    cs, cr, xs, xr, zs, zr, x2s, x2r, z2s, z2r, ys, yr, fs, fr,
):
    x, yh, c, z, yl = place()
    zp = [at(x, yh, c, (z + s) % 4, yl) for s in (1, 2, 3)]
    xp = [at((x + s) % 4, yh, c, z, yl) for s in (1, 2, 3)]
    core = at(x, yh, 1 - c, z, yl)
    p1 = at(x, yh, c, z, 1 - yl)
    p2 = at(x, 1 - yh, c, z, 1 - yl)
    yhp = at(x, 1 - yh, c, z, yl)
    greet(zp + xp + [core, p1, p2, yhp])

    def core_copy(p):
        return remote(g.at[1 - c, p], C.at[p], cs.at[p], cr.at[p], core)

    for p in (2, 0, 3, 1):
        core_copy(p).start()

    def x_copy(p, i):
        return remote(S.at[p, (x + i + 1) % 4], XR.at[i, p], xs.at[p, i], xr.at[p, i], xp[i])

    def z_copy(i):
        t = (z + i + 1) % 4
        return remote(
            S.at[2 + t % 2, :, t // 2], ZR.at[i], zs.at[i], zr.at[i], zp[i]
        )

    def summed(p):
        core_copy(p).wait_recv()
        S[p] = (g[c, p].astype(F32) + C[p].astype(F32)).astype(BF16)

    summed(2)
    summed(0)
    for i in (0, 2, 1):
        x_copy(0, i).start()
    summed(3)
    for i in (0, 2, 1):
        z_copy(i).start()
    summed(1)
    for i in (0, 2, 1):
        x_copy(1, i).start()

    for i in range(3):
        z_copy(i).wait_recv()
    mine = S[2 + z % 2, :, z // 2].astype(F32)
    for i in range(3):
        mine = mine + ZR[i].astype(F32)
    E2[...] = mine.astype(BF16)

    def x2_copy(i):
        return remote(E2.at[(x + i + 1) % 4], XR2.at[i], x2s.at[i], x2r.at[i], xp[i])

    for i in (0, 2, 1):
        x2_copy(i).start()
    for p in range(2):
        for i in range(3):
            x_copy(p, i).wait_recv()
        mine = S[p, x].astype(F32)
        for i in range(3):
            mine = mine + XR[i, p].astype(F32)
        E1[0, p] = mine[0].astype(BF16)
        E1[1, p] = mine[1].astype(BF16)

    def z2_copy(i):
        t = (z + i + 1) % 4
        return remote(E1.at[t // 2, t % 2], ZR2.at[i], z2s.at[i], z2r.at[i], zp[i])

    for i in (0, 2, 1):
        z2_copy(i).start()
    for i in range(3):
        x2_copy(i).wait_recv()
    mine = E2[x].astype(F32)
    for i in range(3):
        mine = mine + XR2[i].astype(F32)
    E[1] = mine.astype(BF16)
    for i in range(3):
        z2_copy(i).wait_recv()
    mine = E1[z // 2, z % 2].astype(F32)
    for i in range(3):
        mine = mine + ZR2[i].astype(F32)
    E[0] = mine.astype(BF16)

    def y_copy(i):
        return remote(E, YR.at[i], ys.at[i], yr.at[i], (p1, p2, yhp)[i])

    owner = yh == z // 2

    @pl.when(owner)
    def _():
        y_copy(0).start()
        for i in range(3):
            y_copy(i).wait_recv()
        F[...] = (
            (E[...].astype(F32) + YR[0].astype(F32) + YR[1].astype(F32) + YR[2].astype(F32)) * (1.0 / 128.0)
        ).astype(BF16)
        y_copy(0).wait_send()

    @pl.when(jnp.logical_not(owner))
    def _():
        for i in (1, 2):
            y_copy(i).start()
        for i in (1, 2):
            y_copy(i).wait_send()

    def f_copy(i):
        return remote(F, FR.at[z % 2], fs.at[i], fr.at[z % 2], zp[i])

    @pl.when(owner)
    def _():
        for i in range(3):
            f_copy(i).start()
        FR[z % 2] = F[...]

    def f_wait(slot):
        pltpu.make_async_copy(FR.at[slot], FR.at[slot], fr.at[slot]).wait()

    @pl.when(owner)
    def _():
        f_wait(1 - z % 2)
        for i in range(3):
            f_copy(i).wait_send()

    @pl.when(jnp.logical_not(owner))
    def _():
        f_wait(0)
        f_wait(1)

    for t in range(2):
        for p in range(2):
            out[2 * p + t] = FR[t, p].astype(F32)

    for p in range(4):
        core_copy(p).wait_send()
    for i in range(3):
        for p in range(2):
            x_copy(p, i).wait_send()
        z_copy(i).wait_send()
        x2_copy(i).wait_send()
        z2_copy(i).wait_send()


def reduce_grads(g):
    vm = pl.BlockSpec(memory_space=pltpu.VMEM)
    dma = pltpu.SemaphoreType.DMA
    rows, cols = g.shape[4:]
    t = (rows, cols)
    return pl.pallas_call(
        reduce_kernel,
        name="reduce",
        out_shape=jax.ShapeDtypeStruct((4,) + t, F32),
        in_specs=[vm],
        out_specs=vm,
        scratch_shapes=[
            pltpu.VMEM((4, 4, 2) + t, BF16),
            pltpu.VMEM((4, 4, 2) + t, BF16),
            pltpu.VMEM((3, 2, 2) + t, BF16),
            pltpu.VMEM((3, 4) + t, BF16),
            pltpu.VMEM((2, 2) + t, BF16),
            pltpu.VMEM((4,) + t, BF16),
            pltpu.VMEM((3,) + t, BF16),
            pltpu.VMEM((3,) + t, BF16),
            pltpu.VMEM((2,) + t, BF16),
            pltpu.VMEM((3, 2) + t, BF16),
            pltpu.VMEM((2,) + t, BF16),
            pltpu.VMEM((2, 2) + t, BF16),
            dma((4,)), dma((4,)),
            dma((2, 3)), dma((2, 3)),
            dma((3,)), dma((3,)),
            dma((3,)), dma((3,)),
            dma((3,)), dma((3,)),
            dma((3,)), dma((3,)),
            dma((3,)), dma((2,)),
        ],
        compiler_params=pltpu.CompilerParams(
            collective_id=2, has_side_effects=True, vmem_limit_bytes=60 << 20
        ),
        cost_estimate=pl.CostEstimate(flops=10**7, bytes_accessed=40 * 10**6, transcendentals=0),
    )(g)


def vision_forward(layer_in, packed_weight, output_weight, windows, norm_gain, merge_gain):
    patches = layer_in.shape[0]
    head_count = output_weight.shape[0] // HEAD_DIM
    widened = layer_in.astype(F32)
    normed = rms_scale(widened, norm_gain).astype(BF16)
    projected = jnp.dot(normed, packed_weight, preferred_element_type=F32).astype(BF16)
    triple = projected.reshape(patches, 3, head_count, HEAD_DIM).astype(F32)
    scores = jnp.einsum("qhd,khd->hqk", triple[:, 0], triple[:, 1]) * HEAD_DIM ** (-0.5)
    same_window = windows[:, None] == windows[None, :]
    scores = jnp.where(same_window[None], scores, -1e30)
    attention = jax.nn.softmax(scores, axis=-1).astype(BF16)
    combined = jnp.einsum("hqk,khd->qhd", attention.astype(F32), triple[:, 2])
    combined = combined.reshape(patches, head_count * HEAD_DIM).astype(BF16)
    output = widened + jnp.dot(combined, output_weight, preferred_element_type=F32)
    return rms_scale(output, merge_gain)


def vision_backward(
    layer_in, packed_weight, output_weight, windows, norm_gain, merge_gain, cotangent
):

    def forward(layer_arg, packed_arg, output_arg):
        return vision_forward(layer_arg, packed_arg, output_arg, windows, norm_gain, merge_gain)

    _, pullback = jax.vjp(forward, layer_in, packed_weight, output_weight)
    return pullback(cotangent.astype(F32))


def local(
    token_grads,
    token_dest,
    merger_down,
    merger_up,
    merger_pre,
    layer_input,
    window_ids,
    norm_gain,
    merge_gain,
    qkv_weight,
    proj_weight,
):
    cotangent, packed_full, output_full = merger(
        token_grads, token_dest.reshape(1, 64), merger_down, merger_up, merger_pre, qkv_weight, proj_weight
    )
    packed_full = packed_full.reshape(1280, 1920)
    output_full = output_full.reshape(640, 1280)
    layer_grad, packed_term, output_term = vision_backward(
        layer_input, packed_full, output_full, window_ids[0], norm_gain, merge_gain, cotangent
    )
    packed_term = packed_term.reshape(4, 2, 2, 80, 3, 640).transpose(2, 4, 0, 1, 3, 5)
    output_term = output_term.reshape(4, 2, 2, 40, 2, 640).transpose(2, 0, 1, 4, 3, 5)
    output_term = output_term.reshape(2, 1, 4, 2, 80, 640)
    sums = reduce_grads(jnp.concatenate([packed_term, output_term], axis=1))
    packed_sum = jnp.concatenate([sums[0], sums[1], sums[2]], axis=1)
    output_sum = jnp.concatenate([sums[3, :40], sums[3, 40:]], axis=1)
    return (layer_grad, packed_sum, output_sum)


def solution(mesh):
    return jax.shard_map(
        local,
        mesh=mesh,
        in_specs=(
            P(("dp", "llm"), None),
            P(("dp", "llm"), None),
            P("llm", None),
            P(None, "llm"),
            P("dp", "llm"),
            P(("dp", "llm"), None),
            P(("dp", "llm"), None),
            P(),
            P(),
            P("dp", None),
            P("dp", None),
        ),
        out_specs=(P(("dp", "llm"), None), P("dp", None), P("dp", None)),
        check_vma=False,
    )
```

```python
import jax
import jax.numpy as jnp
from jax import lax
from jax.experimental import pallas as pl
from jax.experimental.pallas import tpu as pltpu
from jax.sharding import PartitionSpec as P

MESH = pl.DeviceIdType.MESH
HEAD_DIM = 80
CAP = 8
EPSILON = 1e-06
BF16 = jnp.bfloat16
F32 = jnp.float32

NT = (((1,), (1,)), ((), ()))
TN = (((0,), (0,)), ((), ()))

N_TOK = 8
N_FEAT = 8


def gelu_slope(values):
    return (
        0.5 * (1.0 + lax.erf(values * 0.7071067811865476))
        + values * jnp.exp(-0.5 * values * values) * 0.3989422804014327
    )


def rms_scale(values, scaling):
    return values * lax.rsqrt(jnp.mean(values * values, axis=-1, keepdims=True) + EPSILON) * scaling


KEYS = (0, 64, 192, 256)


def head_lanes(h):
    start = 128 * jnp.minimum(5 * h // 8, 3)
    lane = lax.broadcasted_iota(jnp.int32, (1, 256), 1) + start
    mask = ((lane >= HEAD_DIM * h) & (lane < HEAD_DIM * h + HEAD_DIM)).astype(F32).astype(BF16)
    return pl.ds(pl.multiple_of(start, 128), 256), mask


def place():
    d, l = lax.axis_index("dp"), lax.axis_index("llm")
    return d // 4, (d // 2) % 2, d % 2, l // 2, l % 2


def at(x, yh, c, z, yl):
    return (x * 2 + yh) * 2 + c, z * 2 + yl


def remote(src, dst, send, recv, device):
    return pltpu.make_async_remote_copy(
        src_ref=src, dst_ref=dst, send_sem=send, recv_sem=recv, device_id=device, device_id_type=MESH
    )


def greet(devices):
    barrier = pltpu.get_barrier_semaphore()
    for device in devices:
        pl.semaphore_signal(barrier, inc=1, device_id=device, device_id_type=MESH)
    pl.semaphore_wait(barrier, len(devices))


def merger_kernel(
    tok, dest, down, up, pre, qw, ow, xin, win, ng, mg,
    cot_o, wq_o, wo_o, normt_o, proj_o, prob_o, combt_o, n2_o, r2_o,
    G, down_v, slope, acc, pg, pre2,
    S, R, own, T, T0, ZR, M, OUT, A,
    cot, wq, wo, wo2, norm, normt, proj, prob, combt, n2, r2, bias,
    loc, dsem, outs, zs, zr, ys, yr, ps, pr, ws, wr, xs, xr, cs, cr, rys, ryr, rzs, rzr, as_, ar,
):
    x, yh, c, z, yl = place()
    d = (x * 2 + yh) * 2 + c
    l = z * 2 + yl
    zp = [at(x, yh, c, (z + s) % 4, yl) for s in (1, 2, 3)]
    p1 = at(x, yh, c, z, 1 - yl)
    p2 = at(x, 1 - yh, c, z, 1 - yl)
    yhp = at(x, 1 - yh, c, z, yl)
    xp = [at((x + s) % 4, yh, c, z, yl) for s in (1, 2, 3)]
    core = at(x, yh, 1 - c, z, yl)
    dps = [((d + s) % 16, l) for s in range(1, 16)]

    cp_tok = pltpu.make_async_copy(tok, G.at[0, pl.ds(0, 64)], loc.at[0])
    cp_tok.start()
    for k in range(4):
        pltpu.make_async_copy(down.at[:, pl.ds(1024 * k, 1024)], down_v.at[k], dsem.at[k]).start()
    greet(zp + [p1, p2] + dps)
    cp_tok.wait()

    W = G.shape[2] // N_TOK

    def col(k):
        return pl.ds(pl.multiple_of(k * W, W), W)

    def down_copy(k):
        return pltpu.make_async_copy(down.at[:, col(k)], down_v.at[k % 4], dsem.at[k % 4])

    V = M.shape[2]

    def up_copy(f):
        rows = pl.ds(pl.multiple_of(f * V, V), V)
        return pltpu.make_async_copy(up.at[rows], down_v.at[f % 4, :, pl.ds(0, V)], dsem.at[f % 4])

    def z_copy(k, i):
        return remote(
            G.at[0, pl.ds(0, 64), col(k)], G.at[3 - i, pl.ds(0, 64), col(k)], zs.at[k, i], zr.at[k, i], zp[i]
        )

    def y_copy(k, i):
        return remote(
            G.at[:, pl.ds(32 * i, 32), col(k)],
            G.at[:, pl.ds(64 + 32 * i, 32), col(k)],
            ys.at[k, i],
            yr.at[k, i],
            (p1, p2)[i],
        )

    for k in range(2):
        for i in (0, 2, 1):
            z_copy(k, i).start()

    def pre_copy(zz):
        rows = pl.ds(pl.multiple_of((2 * zz + 1 - yl) * 64 + 32, 32), 32)
        return remote(pre.at[rows], pre2.at[pl.ds(32 * zz, 32)], ps.at[zz], pr.at[zz], yhp)

    for zz in range(4):
        pre_copy(zz).start()

    def w_copies(source, index, sends, recvs, device):
        first = wq.at[index] if source is None else source[0]
        second = wo.at[index] if source is None else source[1]
        return [
            remote(first, wq.at[index], sends.at[0], recvs.at[0], device),
            remote(second, wo.at[index], sends.at[1], recvs.at[1], device),
        ]

    def flipped(dd):
        return dd + 2 - 4 * ((dd // 2) % 2)

    wq[d] = qw[...]
    wo[d] = ow[...]
    d2 = flipped(d)
    for cp in w_copies((qw, ow), d, ws.at[0], wr.at[0], p2):
        cp.start()
    for i in (0, 2, 1):
        for cp in w_copies((qw, ow), d, xs.at[0, i], xr.at[0, i], xp[i]):
            cp.start()
    for cp in w_copies((qw, ow), d, cs.at[0], cr.at[0], core):
        cp.start()

    def emit(n, source, target):
        return pltpu.make_async_copy(source, target, outs.at[n])

    def slope_step(k):
        r = k // 2
        zz = (z + r) % 4

        @pl.when(k % 2 == 0)
        def _():
            mine = pre[pl.ds(pl.multiple_of((2 * zz + yl) * 64, 64), 64), :]
            slope[r, 0:64, :] = gelu_slope(mine.astype(F32))

        @pl.when(k % 2 == 1)
        def _():
            first = pre[pl.ds(pl.multiple_of((2 * zz + 1 - yl) * 64, 64), 32), :]
            second = pre2[pl.ds(pl.multiple_of(zz * 32, 32), 32), :]
            slope[r, 64:96, :] = gelu_slope(first.astype(F32))
            slope[r, 96:128, :] = gelu_slope(second.astype(F32))

    def norm_step(k):
        rows = pl.ds(pl.multiple_of(k * 64, 64), 64)
        norm[rows, :] = rms_scale(xin[rows, :].astype(F32), ng[...]).astype(BF16)

    def bias_step():
        for b in range(4):
            queries = jnp.broadcast_to(win[:, 128 * b : 128 * b + 128].astype(F32), (128, 128)).T
            for h in range(2):
                keys = win[:, KEYS[b] + 128 * h : KEYS[b] + 128 * h + 128].astype(F32)
                bias[b, :, 128 * h : 128 * h + 128] = jnp.where(queries == keys, 0.0, -1e30)

    def qkv_step(p, carry):
        cols = pl.ds(pl.multiple_of(p * 640, 128), 640)
        weight = wq[:, :, cols].reshape(1280, 640)
        proj[p] = jnp.dot(norm[...], weight, preferred_element_type=F32).astype(BF16)
        return carry

    def head_step(h):
        lanes, mask = head_lanes(h)
        for b in range(4):
            rows, keys = pl.ds(128 * b, 128), pl.ds(KEYS[b], 256)
            scores = lax.dot_general(
                proj[0, rows, lanes] * mask, proj[1, keys, lanes], NT, preferred_element_type=F32
            )
            scores = scores * HEAD_DIM ** (-0.5) + bias[b]
            powers = jnp.exp(scores - jnp.max(scores, axis=-1, keepdims=True))
            share = (powers / jnp.sum(powers, axis=-1, keepdims=True)).astype(BF16)
            prob[h, b] = share
            combf[rows, lanes] += jnp.dot(share, proj[2, keys, lanes] * mask, preferred_element_type=F32)

    def output_step():
        comb = combf[...].astype(BF16)
        combt[...] = combf[...].T.astype(BF16)
        emit(6, combt, combt_o).start()
        for t in range(4):
            rows = pl.ds(128 * t, 128)
            value = xin[rows, :].astype(F32) + jnp.dot(
                comb[128 * t : 128 * t + 128], wo2[...], preferred_element_type=F32
            )
            factor = lax.rsqrt(jnp.mean(value * value, axis=-1, keepdims=True) + EPSILON)
            n2[rows, :] = value * factor
            r2[rows, :] = factor
        emit(7, n2, n2_o).start()
        emit(8, r2, r2_o).start()

    for zz in range(4):
        pre_copy(zz).wait_recv()
    acc[...] = jnp.zeros_like(acc)

    def multiply(k):
        for i in range(2):
            y_copy(k, i).wait_recv()
        tile = G[:, :, col(k)].reshape(512, W)
        down_copy(k).wait()
        acc[...] += lax.dot_general(tile, down_v[k % 4], NT, preferred_element_type=F32)

        @pl.when(k + 4 < N_TOK)
        def _():
            down_copy(k + 4).start()

        @pl.when(k >= 4)
        def _():
            up_copy(k - 4).start()


    def gather_step(k, carry):
        @pl.when(k + 2 < N_TOK)
        def _():
            for i in (0, 2, 1):
                z_copy(k + 2, i).start()

        for i in range(3):
            z_copy(k, i).wait_recv()
        for i in range(2):
            y_copy(k, i).start()

        @pl.when(k == 1)
        def _():
            for cp in w_copies((qw, ow), d2, ws.at[0], wr.at[0], p2):
                cp.wait_recv()
            for i in (0, 2, 1):
                for cp in w_copies(None, d2, xs.at[1, i], xr.at[1, i], xp[i]):
                    cp.start()
            for cp in w_copies(None, d2, cs.at[1], cr.at[1], core):
                cp.start()

        @pl.when(k >= 1)
        def _():
            multiply(k - 1)

        slope_step(k)
        norm_step(k)
        return carry

    lax.fori_loop(0, N_TOK, gather_step, 0)
    bias_step()
    multiply(jnp.int32(N_TOK - 1))

    def x_arrive(h):
        for i in range(3):
            other = ((x + i + 1) % 4 * 2 + yh) * 2 + c
            other = flipped(other) if h else other
            for cp in w_copies(None, other, xs.at[h, 2 - i], xr.at[h, 2 - i], xp[2 - i]):
                cp.wait_recv()
            for cp in w_copies(None, other, cs.at[2 + 3 * h + i], cr.at[2 + 3 * h + i], core):
                cp.start()

    pg[...] = (acc[...] * slope[...].reshape(512, slope.shape[2])).astype(BF16)
    combf = acc
    combf[...] = jnp.zeros_like(combf)

    token = dest[...]
    hot = (lax.broadcasted_iota(jnp.int32, (16, 64), 0) == token).astype(F32)
    before = (
        lax.broadcasted_iota(jnp.int32, (64, 64), 0) < lax.broadcasted_iota(jnp.int32, (64, 64), 1)
    ).astype(F32)
    rank = jnp.sum(jnp.dot(hot, before, preferred_element_type=F32) * hot, axis=0, keepdims=True)
    target = token * 16 + rank.astype(jnp.int32)
    row = lax.broadcasted_iota(jnp.int32, (256, 64), 0)
    placing = jnp.concatenate(
        [(row == target).astype(F32), (row == target + 8).astype(F32)], axis=1
    ).astype(BF16)

    def ry_copy(f, i):
        return remote(S.at[f, i], R.at[f, i], rys.at[f, i], ryr.at[f, i], (p1, p2)[i])

    def rz_copy(f, i):
        return remote(T.at[f, i], ZR.at[f, i], rzs.at[f, i], rzr.at[f, i], zp[i])

    def a_copy(j, s):
        dd = (d + s) % 16
        return remote(
            OUT.at[j, pl.ds(pl.multiple_of(dd * 16, 16), 16)],
            A.at[j, pl.ds(pl.multiple_of(d * 16, 16), 16)],
            as_.at[j],
            ar.at[j],
            dps[s - 1],
        )

    cidx = [d, d2]
    for h in range(2):
        for i in range(3):
            other = ((x + i + 1) % 4 * 2 + yh) * 2 + c
            cidx.append(flipped(other) if h else other)

    def weights_arrive():
        for n, index in enumerate(cidx):
            for cp in w_copies(None, index + 1 - 2 * c, cs.at[n], cr.at[n], core):
                cp.wait_recv()
        wo2[...] = wo[...].astype(F32).reshape(wo2.shape).astype(BF16)
        emit(1, wq, wq_o).start()
        emit(2, wo2, wo_o).start()

    def first_product(i):
        up_copy(i).wait()
        part = lax.dot_general(pg[...], down_v[i % 4, :, 0:V], NT, preferred_element_type=F32)

        @pl.when(i + 4 < N_FEAT)
        def _():
            up_copy(i + 4).start()

        part = part.reshape(4, 128, V)
        S[i, 0] = part[:, 64:96, :].astype(BF16)
        S[i, 1] = part[:, 96:128, :].astype(BF16)
        for h in range(2):
            ry_copy(i, h).start()
        own[i % 4] = part[:, 0:64, :]

    def over_y(f):
        for h in range(2):
            ry_copy(f, h).wait_recv()
        total = own[f % 4] + jnp.concatenate([R[f, 0].astype(F32), R[f, 1].astype(F32)], axis=1)
        T[f] = total[1:4].astype(BF16)
        T0[f % 2] = total[0]
        for h in (0, 2, 1):
            rz_copy(f, h).start()

    def over_z(f):
        for h in range(3):
            rz_copy(f, h).wait_recv()
        M[f] = (
            T0[f % 2] + ZR[f, 0].astype(F32) + ZR[f, 1].astype(F32) + ZR[f, 2].astype(F32)
        ).astype(BF16)

    def send_rows(j):
        both = jnp.concatenate([M[2 * j], M[2 * j + 1]], axis=0)
        OUT[j] = jnp.dot(placing, both, preferred_element_type=F32).astype(BF16)
        for s in range(1, 16):
            a_copy(j, s).start()
        here = pl.ds(pl.multiple_of(d * 16, 16), 16)
        A[j, here, :] = OUT[j, here, :]

    def open_step(i, carry):
        first_product(i)
        return carry

    lax.fori_loop(0, 3, open_step, 0)
    x_arrive(0)
    x_arrive(1)

    def sum_step(f, carry):
        over_y(f)

        @pl.when(f + 3 < N_FEAT)
        def _():
            first_product(f + 3)

        @pl.when(f >= 1)
        def _():
            over_z(f - 1)

        @pl.when((f >= 2) & (f % 2 == 0))
        def _():
            send_rows(f // 2 - 1)

        @pl.when(f == 0)
        def _():
            weights_arrive()
            lax.fori_loop(0, 3, qkv_step, 0)
            emit(4, proj, proj_o).start()

        @pl.when(f >= 1)
        def _():
            head_step(f - 1)

        return carry

    lax.fori_loop(0, N_FEAT, sum_step, 0)
    head_step(7)
    emit(5, prob, prob_o).start()
    over_z(N_FEAT - 1)
    send_rows(3)
    normt[...] = norm[...].astype(F32).T.astype(BF16)
    emit(3, normt, normt_o).start()
    output_step()

    fifteen = pl.ds(0, 240)
    for j in range(4):
        pltpu.make_async_copy(A.at[j, fifteen], A.at[j, fifteen], ar.at[j]).wait()
    out_row = lax.broadcasted_iota(jnp.int32, (128, 256), 0)
    in_row = lax.broadcasted_iota(jnp.int32, (128, 256), 1)
    wanted = (out_row % 4) * 64 + (out_row // 32) * 16 + (out_row // 4) % 8
    for h in range(2):
        order = (in_row == wanted + 8 * h).astype(F32).astype(BF16)
        for g in range(4):
            stacked = A[:, 64 * g : 64 * g + 64, :].reshape(256, V)
            cot[128 * g : 128 * g + 128, V * h : V * h + V] = jnp.dot(
                order, stacked, preferred_element_type=F32
            ).astype(BF16)
    emit(0, cot, cot_o).start()

    for n, index in enumerate(cidx):
        for cp in w_copies(None, index, cs.at[n], cr.at[n], core):
            cp.wait_send()
    for cp in w_copies((qw, ow), d, ws.at[0], wr.at[0], p2):
        cp.wait_send()
    for h in range(2):
        for i in range(3):
            for cp in w_copies(None, d2 if h else d, xs.at[h, i], xr.at[h, i], xp[i]):
                cp.wait_send()
    for zz in range(4):
        pre_copy(zz).wait_send()

    def drain(k, carry):
        for i in range(3):
            z_copy(k, i).wait_send()
        for i in range(2):
            y_copy(k, i).wait_send()
        return carry

    lax.fori_loop(0, N_TOK, drain, 0)

    def drain2(f, carry):
        for i in range(2):
            ry_copy(f, i).wait_send()
        for i in range(3):
            rz_copy(f, i).wait_send()
        return carry

    lax.fori_loop(0, N_FEAT, drain2, 0)
    for j in range(4):
        pltpu.make_async_copy(OUT.at[j, fifteen], OUT.at[j, fifteen], as_.at[j]).wait()
    pairs = [
        (cot, cot_o), (wq, wq_o), (wo2, wo_o), (normt, normt_o), (proj, proj_o),
        (prob, prob_o), (combt, combt_o), (n2, n2_o), (r2, r2_o),
    ]
    for n, (source, target) in enumerate(pairs):
        emit(n, source, target).wait()


def merger(tok, dest, down, up, pre, qw, ow, xin, win, ng, mg):
    vm = pl.BlockSpec(memory_space=pltpu.VMEM)
    hbm = pl.BlockSpec(memory_space=pl.ANY)
    dma = pltpu.SemaphoreType.DMA
    hid = pre.shape[1]
    feat = up.shape[0]
    V = feat // N_FEAT
    kept = [
        ((512, 1280), BF16),
        ((16,) + qw.shape, BF16),
        ((640, 1280), BF16),
        ((1280, 512), BF16),
        ((3, 512, 640), BF16),
        ((8, 4, 128, 256), BF16),
        ((640, 512), BF16),
        ((512, 1280), F32),
        ((512, 1), F32),
    ]
    return pl.pallas_call(
        merger_kernel,
        name="merger",
        out_shape=tuple(jax.ShapeDtypeStruct(*k) for k in kept),
        in_specs=[hbm, vm, hbm, hbm, vm, vm, vm, vm, vm, vm, vm],
        out_specs=(hbm,) * len(kept),
        scratch_shapes=[
            pltpu.VMEM((4, 128, tok.shape[1]), BF16),
            pltpu.VMEM((4, 640, 1024), BF16),
            pltpu.VMEM((4, 128, hid), F32),
            pltpu.VMEM((512, hid), F32),
            pltpu.VMEM((512, hid), BF16),
            pltpu.VMEM((128, hid), BF16),
            pltpu.VMEM((N_FEAT, 2, 4, 32, V), BF16),
            pltpu.VMEM((N_FEAT, 2, 4, 32, V), BF16),
            pltpu.VMEM((4, 4, 64, V), F32),
            pltpu.VMEM((N_FEAT, 3, 64, V), BF16),
            pltpu.VMEM((2, 64, V), F32),
            pltpu.VMEM((N_FEAT, 3, 64, V), BF16),
            pltpu.VMEM((N_FEAT, 64, V), BF16),
            pltpu.VMEM((4, 256, V), BF16),
            pltpu.VMEM((4, 256, V), BF16),
            pltpu.VMEM((512, 1280), BF16),
            pltpu.VMEM((16,) + qw.shape, BF16),
            pltpu.VMEM((16,) + ow.shape, BF16),
            pltpu.VMEM((640, 1280), BF16),
            pltpu.VMEM((512, 1280), BF16),
            pltpu.VMEM((1280, 512), BF16),
            pltpu.VMEM((3, 512, 640), BF16),
            pltpu.VMEM((8, 4, 128, 256), BF16),
            pltpu.VMEM((640, 512), BF16),
            pltpu.VMEM((512, 1280), F32),
            pltpu.VMEM((512, 1), F32),
            pltpu.VMEM((4, 128, 256), F32),
            dma((1,)),
            dma((4,)),
            dma((9,)),
            dma((N_TOK, 3)), dma((N_TOK, 3)), dma((N_TOK, 2)), dma((N_TOK, 2)),
            dma((4,)), dma((4,)),
            dma((1, 2)), dma((1, 2)),
            dma((2, 3, 2)), dma((2, 3, 2)),
            dma((8, 2)), dma((8, 2)),
            dma((N_FEAT, 2)), dma((N_FEAT, 2)),
            dma((N_FEAT, 3)), dma((N_FEAT, 3)),
            dma((4,)), dma((4,)),
        ],
        compiler_params=pltpu.CompilerParams(
            collective_id=1, has_side_effects=True, vmem_limit_bytes=62 << 20
        ),
        cost_estimate=pl.CostEstimate(flops=9 * 10**9, bytes_accessed=40 * 10**6, transcendentals=0),
    )(tok, dest, down, up, pre, qw, ow, xin, win, ng, mg)


def block_kernel(
    cot_i, wq_i, wo_i, normt_i, proj_i, prob_i, combt_i, n2_i, r2_i, xin, ng, mg,
    lg, pout, oout,
    cot, wq, wo, normt, proj, prob, combt, n2, r2,
    db, dc, wof, DP, dpb, g,
    C, S, Z, XR, ZR, E1, E2, XR2, ZR2, E, YR, F, FR,
    ins, cs, cr, xs, xr, zs, zr, x2s, x2r, z2s, z2r, ys, yr, fs, fr,
):
    x, yh, c, z, yl = place()
    pairs = [
        (cot_i, cot), (n2_i, n2), (r2_i, r2), (wo_i, wo), (combt_i, combt), (prob_i, prob), (proj_i, proj),
        (normt_i, normt), (wq_i, wq),
    ]
    loads = [pltpu.make_async_copy(a, b, ins.at[n]) for n, (a, b) in enumerate(pairs)]
    for cp in loads:
        cp.start()
    zp = [at(x, yh, c, (z + s) % 4, yl) for s in (1, 2, 3)]
    xp = [at((x + s) % 4, yh, c, z, yl) for s in (1, 2, 3)]
    core = at(x, yh, 1 - c, z, yl)
    p1 = at(x, yh, c, z, 1 - yl)
    p2 = at(x, 1 - yh, c, z, 1 - yl)
    yhp = at(x, 1 - yh, c, z, yl)
    greet(zp + xp + [core, p1, p2, yhp])

    def core_copy(p):
        return remote(g.at[p, :, 1 - c], C.at[p], cs.at[p], cr.at[p], core)

    def x_copy(p, i):
        return remote(
            S.at[p, pl.ds((x + i + 1) % 4 * 2, 2)], XR.at[i, p], xs.at[p, i], xr.at[p, i], xp[i]
        )

    def z_copy(i):
        t = (z + i + 1) % 4
        return remote(Z.at[t % 2, t // 2], ZR.at[i], zs.at[i], zr.at[i], zp[i])

    def summed(p):
        core_copy(p).wait_recv()
        total = (g[p, :, c].astype(F32) + C[p].astype(F32)).astype(BF16)
        if p < 2:
            S[p] = total
        else:
            total = total.reshape(4, 2, 80, 640)
            Z[p - 2, 0] = total[:, 0]
            Z[p - 2, 1] = total[:, 1]

    def z_start(part):
        for i in (0, 2, 1):

            @pl.when((z + i + 1) % 2 == part)
            def _():
                z_copy(i).start()

    loads[0].wait()
    loads[1].wait()
    loads[2].wait()
    loads[3].wait()

    def out_step(t, carry):
        rows = pl.ds(pl.multiple_of(t * 128, 128), 128)
        slope = cot[rows, :].astype(F32) * mg[...]
        unit = n2[rows, :]
        grad = r2[rows, :] * (slope - unit * jnp.mean(slope * unit, axis=-1, keepdims=True))
        n2[rows, :] = grad
        db[rows, :] = grad.astype(BF16)
        dc[rows, :] = lax.dot_general(
            grad.astype(BF16), wo[...], NT, preferred_element_type=F32
        ).astype(BF16)
        return carry

    lax.fori_loop(0, 4, out_step, 0)
    loads[4].wait()

    def wo_step(t, carry):
        cols = pl.ds(pl.multiple_of(t * 640, 128), 640)
        wof[t] = jnp.dot(combt[...], db[:, cols], preferred_element_type=F32)
        return carry

    lax.fori_loop(0, 2, wo_step, 0)
    g[3] = (
        jnp.concatenate([wof[0].reshape(16, 40, 640), wof[1].reshape(16, 40, 640)], axis=1)
        .astype(BF16)
        .reshape(8, 2, 80, 640)
    )
    core_copy(3).start()

    DP[...] = jnp.zeros_like(DP)
    loads[5].wait()
    loads[6].wait()

    def head_step(h, carry):
        lanes, mask = head_lanes(h)
        for b in range(4):
            rows, keys = pl.ds(128 * b, 128), pl.ds(KEYS[b], 256)
            query = proj[0, rows, lanes] * mask
            key = proj[1, keys, lanes] * mask
            grad = dc[rows, lanes] * mask
            share = prob[h, b]
            wide = share.astype(F32)
            slope = lax.dot_general(grad, proj[2, keys, lanes], NT, preferred_element_type=F32)
            slope = wide * (slope - jnp.sum(slope * wide, axis=-1, keepdims=True)) * HEAD_DIM ** (-0.5)
            slope = slope.astype(BF16)
            DP[0, rows, lanes] += jnp.dot(slope, key, preferred_element_type=F32)
            DP[1, keys, lanes] += lax.dot_general(slope, query, TN, preferred_element_type=F32)
            DP[2, keys, lanes] += lax.dot_general(share, grad, TN, preferred_element_type=F32)

        @pl.when(h == 3)
        def _():
            summed(3)
            z_start(1)

        return carry

    lax.fori_loop(0, 8, head_step, 0)
    loads[7].wait()
    loads[8].wait()

    def weight_grad(p):
        dpb[p] = DP[p].astype(BF16)
        g[p] = (
            jnp.dot(normt[...], dpb[p], preferred_element_type=F32).astype(BF16).reshape(8, 2, 80, 640)
        )
        core_copy(p).start()

    def input_step(t, carry):
        rows = pl.ds(pl.multiple_of(t * 128, 128), 128)
        slope = jnp.zeros((128, 1280), F32)
        for p in range(3):
            slope += lax.dot_general(
                dpb[p, rows, :],
                wq[:, :, 640 * p : 640 * p + 640].reshape(1280, 640),
                NT,
                preferred_element_type=F32,
            )
        slope = slope.astype(BF16).astype(F32) * ng[...]
        value = xin[rows, :].astype(F32)
        factor = lax.rsqrt(jnp.mean(value * value, axis=-1, keepdims=True) + EPSILON)
        unit = value * factor
        grad = factor * (slope - unit * jnp.mean(slope * unit, axis=-1, keepdims=True))
        lg[rows, :] = (grad + n2[rows, :]).astype(BF16)
        return carry

    weight_grad(0)
    weight_grad(1)
    summed(0)
    for i in (0, 2, 1):
        x_copy(0, i).start()
    weight_grad(2)
    summed(1)
    for i in (0, 2, 1):
        x_copy(1, i).start()
    lax.fori_loop(0, 1, input_step, 0)
    summed(2)
    z_start(0)
    lax.fori_loop(1, 4, input_step, 0)

    for i in range(3):
        z_copy(i).wait_recv()
    mine = Z[z % 2, z // 2].astype(F32)
    for i in range(3):
        mine = mine + ZR[i].astype(F32)
    E2[...] = mine.astype(BF16)

    def x2_copy(i):
        return remote(E2.at[(x + i + 1) % 4], XR2.at[i], x2s.at[i], x2r.at[i], xp[i])

    for i in (0, 2, 1):
        x2_copy(i).start()
    for p in range(2):
        for i in range(3):
            x_copy(p, i).wait_recv()
        mine = S[p, pl.ds(2 * x, 2)].astype(F32)
        for i in range(3):
            mine = mine + XR[i, p].astype(F32)
        E1[0, p] = mine[0].astype(BF16)
        E1[1, p] = mine[1].astype(BF16)

    def z2_copy(i):
        t = (z + i + 1) % 4
        return remote(E1.at[t // 2, t % 2], ZR2.at[i], z2s.at[i], z2r.at[i], zp[i])

    for i in (0, 2, 1):
        z2_copy(i).start()
    for i in range(3):
        x2_copy(i).wait_recv()
    mine = E2[x].astype(F32)
    for i in range(3):
        mine = mine + XR2[i].astype(F32)
    E[1] = mine.astype(BF16)
    for i in range(3):
        z2_copy(i).wait_recv()
    mine = E1[z // 2, z % 2].astype(F32)
    for i in range(3):
        mine = mine + ZR2[i].astype(F32)
    E[0] = mine.astype(BF16)

    def y_copy(i):
        return remote(E, YR.at[i], ys.at[i], yr.at[i], (p1, p2, yhp)[i])

    owner = yh == z // 2

    @pl.when(owner)
    def _():
        y_copy(0).start()
        for i in range(3):
            y_copy(i).wait_recv()
        F[...] = (
            (E[...].astype(F32) + YR[0].astype(F32) + YR[1].astype(F32) + YR[2].astype(F32)) * (1.0 / 128.0)
        ).astype(BF16)
        y_copy(0).wait_send()

    @pl.when(jnp.logical_not(owner))
    def _():
        for i in (1, 2):
            y_copy(i).start()
        for i in (1, 2):
            y_copy(i).wait_send()

    def f_copy(i):
        return remote(F, FR.at[z % 2], fs.at[i], fr.at[z % 2], zp[i])

    @pl.when(owner)
    def _():
        for i in range(3):
            f_copy(i).start()
        FR[z % 2] = F[...]

    def f_wait(slot):
        pltpu.make_async_copy(FR.at[slot], FR.at[slot], fr.at[slot]).wait()

    @pl.when(owner)
    def _():
        f_wait(1 - z % 2)
        for i in range(3):
            f_copy(i).wait_send()

    @pl.when(jnp.logical_not(owner))
    def _():
        f_wait(0)
        f_wait(1)

    for p in range(3):
        pout[:, 640 * p : 640 * p + 640] = FR[p % 2, p // 2].astype(F32)
    last = FR[1, 1].astype(F32)
    oout[:, 0:640] = last[0:40]
    oout[:, 640:1280] = last[40:80]

    for p in range(4):
        core_copy(p).wait_send()
    for i in range(3):
        for p in range(2):
            x_copy(p, i).wait_send()
        z_copy(i).wait_send()
        x2_copy(i).wait_send()
        z2_copy(i).wait_send()


def block_grads(cot, wq, wo, normt, proj, prob, combt, n2, r2, xin, ng, mg):
    vm = pl.BlockSpec(memory_space=pltpu.VMEM)
    hbm = pl.BlockSpec(memory_space=pl.ANY)
    dma = pltpu.SemaphoreType.DMA
    t = (80, 640)
    held = (cot, wq, wo, normt, proj, prob, combt, n2, r2)
    return pl.pallas_call(
        block_kernel,
        name="block",
        out_shape=(
            jax.ShapeDtypeStruct((512, 1280), BF16),
            jax.ShapeDtypeStruct((80, 1920), F32),
            jax.ShapeDtypeStruct((40, 1280), F32),
        ),
        in_specs=[hbm] * 9 + [vm] * 3,
        out_specs=(vm, vm, vm),
        scratch_shapes=[pltpu.VMEM(k.shape, k.dtype) for k in held]
        + [
            pltpu.VMEM((512, 1280), BF16),
            pltpu.VMEM((512, 640), BF16),
            pltpu.VMEM((2, 640, 640), F32),
            pltpu.VMEM((3, 512, 640), F32),
            pltpu.VMEM((3, 512, 640), BF16),
            pltpu.VMEM((4, 8, 2) + t, BF16),
            pltpu.VMEM((4, 8) + t, BF16),
            pltpu.VMEM((2, 8) + t, BF16),
            pltpu.VMEM((2, 2, 4) + t, BF16),
            pltpu.VMEM((3, 2, 2) + t, BF16),
            pltpu.VMEM((3, 4) + t, BF16),
            pltpu.VMEM((2, 2) + t, BF16),
            pltpu.VMEM((4,) + t, BF16),
            pltpu.VMEM((3,) + t, BF16),
            pltpu.VMEM((3,) + t, BF16),
            pltpu.VMEM((2,) + t, BF16),
            pltpu.VMEM((3, 2) + t, BF16),
            pltpu.VMEM((2,) + t, BF16),
            pltpu.VMEM((2, 2) + t, BF16),
            dma((9,)),
            dma((4,)), dma((4,)),
            dma((2, 3)), dma((2, 3)),
            dma((3,)), dma((3,)),
            dma((3,)), dma((3,)),
            dma((3,)), dma((3,)),
            dma((3,)), dma((3,)),
            dma((3,)), dma((2,)),
        ],
        compiler_params=pltpu.CompilerParams(
            collective_id=2, has_side_effects=True, vmem_limit_bytes=62 << 20
        ),
        cost_estimate=pl.CostEstimate(flops=8 * 10**9, bytes_accessed=40 * 10**6, transcendentals=0),
    )(cot, wq, wo, normt, proj, prob, combt, n2, r2, xin, ng, mg)


def local(
    token_grads,
    token_dest,
    merger_down,
    merger_up,
    merger_pre,
    layer_input,
    window_ids,
    norm_gain,
    merge_gain,
    qkv_weight,
    proj_weight,
):
    norm_row, merge_row = norm_gain.reshape(1, 1280), merge_gain.reshape(1, 1280)
    kept = merger(
        token_grads, token_dest.reshape(1, 64), merger_down, merger_up, merger_pre, qkv_weight, proj_weight,
        layer_input, window_ids, norm_row, merge_row,
    )
    return block_grads(*kept, layer_input, norm_row, merge_row)


def solution(mesh):
    return jax.shard_map(
        local,
        mesh=mesh,
        in_specs=(
            P(("dp", "llm"), None),
            P(("dp", "llm"), None),
            P("llm", None),
            P(None, "llm"),
            P("dp", "llm"),
            P(("dp", "llm"), None),
            P(("dp", "llm"), None),
            P(),
            P(),
            P("dp", None),
            P("dp", None),
        ),
        out_specs=(P(("dp", "llm"), None), P("dp", None), P("dp", None)),
        check_vma=False,
    )
```

```python
import jax
import jax.numpy as jnp
from jax import lax
from jax.experimental import pallas as pl
from jax.experimental.pallas import tpu as pltpu
from jax.sharding import PartitionSpec as P

MESH = pl.DeviceIdType.MESH
HEAD_DIM = 80
CAP = 8
EPSILON = 1e-06
BF16 = jnp.bfloat16
F32 = jnp.float32

NT = (((1,), (1,)), ((), ()))
TN = (((0,), (0,)), ((), ()))

N_TOK = 8
N_NARROW = 5
N_LEFT = 384
N_FEAT = 8


def gelu_slope(values):
    return (
        0.5 * (1.0 + lax.erf(values * 0.7071067811865476))
        + values * jnp.exp(-0.5 * values * values) * 0.3989422804014327
    )


def rms_scale(values, scaling):
    return values * lax.rsqrt(jnp.mean(values * values, axis=-1, keepdims=True) + EPSILON) * scaling


KEYS = (0, 64, 192, 256)


def head_lanes(h):
    start = 128 * jnp.minimum(5 * h // 8, 3)
    lane = lax.broadcasted_iota(jnp.int32, (1, 256), 1) + start
    mask = ((lane >= HEAD_DIM * h) & (lane < HEAD_DIM * h + HEAD_DIM)).astype(F32).astype(BF16)
    return pl.ds(pl.multiple_of(start, 128), 256), mask


def place():
    d, l = lax.axis_index("dp"), lax.axis_index("llm")
    return d // 4, (d // 2) % 2, d % 2, l // 2, l % 2


def at(x, yh, c, z, yl):
    return (x * 2 + yh) * 2 + c, z * 2 + yl


def remote(src, dst, send, recv, device):
    return pltpu.make_async_remote_copy(
        src_ref=src, dst_ref=dst, send_sem=send, recv_sem=recv, device_id=device, device_id_type=MESH
    )


def greet(devices):
    barrier = pltpu.get_barrier_semaphore()
    for device in devices:
        pl.semaphore_signal(barrier, inc=1, device_id=device, device_id_type=MESH)
    pl.semaphore_wait(barrier, len(devices))


def merger_kernel(
    tok, dest, down, up, pre, qw, ow, xin, win, ng, mg,
    cot_o, wq_o, wo_o, normt_o, proj_o, prob_o, combt_o, n2_o, r2_o,
    G, down_v, slope, acc, pg, pre2,
    S, R, own, T, T0, ZR, M, OUT, A,
    cot, wq, wo, wo2, norm, normt, proj, prob, combt, n2, r2, bias,
    loc, dsem, os_, or_, outs, zs, zr, ns, nr, ys, yr, ps, pr, ws, wr, xs, xr, cs, cr, rys, ryr, rzs, rzr, as_, ar,
):
    x, yh, c, z, yl = place()
    d = (x * 2 + yh) * 2 + c
    l = z * 2 + yl
    zp = [at(x, yh, c, (z + s) % 4, yl) for s in (1, 2, 3)]
    p1 = at(x, yh, c, z, 1 - yl)
    p2 = at(x, 1 - yh, c, z, 1 - yl)
    yhp = at(x, 1 - yh, c, z, yl)
    xp = [at((x + s) % 4, yh, c, z, yl) for s in (1, 2, 3)]
    core = at(x, yh, 1 - c, z, yl)
    dps = [((d + s) % 16, l) for s in range(1, 16)]

    cp_tok = pltpu.make_async_copy(tok, G.at[0, pl.ds(0, 64)], loc.at[0])
    cp_tok.start()
    for k in range(4):
        pltpu.make_async_copy(down.at[:, pl.ds(1024 * k, 1024)], down_v.at[k], dsem.at[k]).start()
    greet(zp + [p1, p2] + dps)
    cp_tok.wait()

    W = G.shape[2] // N_TOK

    def col(k):
        return pl.ds(pl.multiple_of(k * W, W), W)

    def down_copy(k):
        return pltpu.make_async_copy(down.at[:, col(k)], down_v.at[k % 4], dsem.at[k % 4])

    V = M.shape[2]

    def up_copy(f):
        rows = pl.ds(pl.multiple_of(f * V, V), V)
        return pltpu.make_async_copy(up.at[rows], down_v.at[f % 4, :, pl.ds(0, V)], dsem.at[f % 4])

    def z_copy(k, i, rows):
        return remote(
            G.at[0, pl.ds(0, rows), col(k)],
            G.at[(3, 1)[i], pl.ds(0, rows), col(k)],
            zs.at[k, i],
            zr.at[k, i],
            (zp[0], zp[2])[i],
        )

    def on_copy(k, i, rows):
        half = pl.ds(pl.multiple_of(k * W + i * (W // 2), W // 2), W // 2)
        return remote(
            G.at[(3, 1)[i], pl.ds(0, rows), half],
            G.at[2, pl.ds(0, rows), half],
            ns.at[k, i],
            nr.at[k, i],
            (zp[0], zp[2])[i],
        )

    def each(k, act):
        @pl.when(k < N_NARROW)
        def _():
            act(64)

        @pl.when(k >= N_NARROW)
        def _():
            act(128)

    def y_copy(k, i):
        return remote(
            G.at[:, pl.ds(32 * i, 32), col(k)],
            G.at[:, pl.ds(64 + 32 * i, 32), col(k)],
            ys.at[k, i],
            yr.at[k, i],
            (p1, p2)[i],
        )

    def o_copy(i):
        wide = pl.ds(N_NARROW * W, (N_TOK - N_NARROW) * W)
        return remote(
            G.at[0, pl.ds(32 * i, 32), wide],
            G.at[0, pl.ds(64 + 32 * i, 32), wide],
            os_.at[i],
            or_.at[i],
            (p1, p2)[i],
        )

    o_copy(0).start()
    for k in range(2):
        for i in range(2):
            z_copy(k, i, 64).start()

    def pre_copy(zz):
        rows = pl.ds(pl.multiple_of((2 * zz + 1 - yl) * 64 + 32, 32), 32)
        return remote(pre.at[rows], pre2.at[pl.ds(32 * zz, 32)], ps.at[zz], pr.at[zz], yhp)

    def w_copies(source, index, sends, recvs, device):
        first = wq.at[index] if source is None else source[0]
        second = wo.at[index] if source is None else source[1]
        return [
            remote(first, wq.at[index], sends.at[0], recvs.at[0], device),
            remote(second, wo.at[index], sends.at[1], recvs.at[1], device),
        ]

    def flipped(dd):
        return dd + 2 - 4 * ((dd // 2) % 2)

    wq[d] = qw[...]
    wo[d] = ow[...]
    d2 = flipped(d)
    for cp in w_copies((qw, ow), d, ws.at[0], wr.at[0], p2):
        cp.start()
    o_copy(1).start()
    for i in (0, 2, 1):
        for cp in w_copies((qw, ow), d, xs.at[0, i], xr.at[0, i], xp[i]):
            cp.start()
    for cp in w_copies((qw, ow), d, cs.at[0], cr.at[0], core):
        cp.start()
    for zz in range(4):
        pre_copy(zz).start()

    def emit(n, source, target):
        return pltpu.make_async_copy(source, target, outs.at[n])

    def slope_step(r):
        @pl.when(r == 0)
        def _():
            for zz in range(4):
                pre_copy(zz).wait_recv()

        zz = (z + r) % 4
        mine = pre[pl.ds(pl.multiple_of((2 * zz + yl) * 64, 64), 64), :]
        slope[r, 0:64, :] = gelu_slope(mine.astype(F32))
        first = pre[pl.ds(pl.multiple_of((2 * zz + 1 - yl) * 64, 64), 32), :]
        second = pre2[pl.ds(pl.multiple_of(zz * 32, 32), 32), :]
        slope[r, 64:96, :] = gelu_slope(first.astype(F32))
        slope[r, 96:128, :] = gelu_slope(second.astype(F32))

    def norm_step(k):
        rows = pl.ds(pl.multiple_of(k * 128, 128), 128)
        norm[rows, :] = rms_scale(xin[rows, :].astype(F32), ng[...].reshape(1, 1280)).astype(BF16)

    def bias_step():
        for b in range(4):
            queries = jnp.broadcast_to(win[:, 128 * b : 128 * b + 128].astype(F32), (128, 128)).T
            for h in range(2):
                keys = win[:, KEYS[b] + 128 * h : KEYS[b] + 128 * h + 128].astype(F32)
                bias[b, :, 128 * h : 128 * h + 128] = jnp.where(queries == keys, 0.0, -1e30)

    def qkv_step(p, carry):
        cols = pl.ds(pl.multiple_of(p * 640, 128), 640)
        weight = wq[:, :, cols].reshape(1280, 640)
        proj[p] = jnp.dot(norm[...], weight, preferred_element_type=F32).astype(BF16)
        return carry

    def head_step(h):
        lanes, mask = head_lanes(h)
        for b in range(4):
            rows, keys = pl.ds(128 * b, 128), pl.ds(KEYS[b], 256)
            scores = lax.dot_general(
                proj[0, rows, lanes] * mask, proj[1, keys, lanes], NT, preferred_element_type=F32
            )
            scores = scores * HEAD_DIM ** (-0.5) + bias[b]
            powers = jnp.exp(scores - jnp.max(scores, axis=-1, keepdims=True))
            share = (powers / jnp.sum(powers, axis=-1, keepdims=True)).astype(BF16)
            prob[h, b] = share
            combf[rows, lanes] += jnp.dot(share, proj[2, keys, lanes] * mask, preferred_element_type=F32)

    def output_step():
        comb = combf[...].astype(BF16)
        combt[...] = combf[...].T.astype(BF16)
        emit(6, combt, combt_o).start()
        for t in range(4):
            rows = pl.ds(128 * t, 128)
            value = xin[rows, :].astype(F32) + jnp.dot(
                comb[128 * t : 128 * t + 128], wo2[...], preferred_element_type=F32
            )
            factor = lax.rsqrt(jnp.mean(value * value, axis=-1, keepdims=True) + EPSILON)
            n2[rows, :] = value * factor
            r2[rows, :] = factor
        emit(7, n2, n2_o).start()
        emit(8, r2, r2_o).start()

    acc[...] = jnp.zeros_like(acc)

    def multiply(k):
        @pl.when(k < N_NARROW)
        def _():
            for i in range(2):
                y_copy(k, i).wait_recv()

        tile = G[:, :, col(k)].reshape(512, W)
        down_copy(k).wait()
        acc[...] += lax.dot_general(tile, down_v[k % 4], NT, preferred_element_type=F32)

        @pl.when(k + 4 < N_TOK)
        def _():
            down_copy(k + 4).start()

        @pl.when(k >= 4)
        def _():
            up_copy(k - 4).start()


    def x_arrive(h):
        for i in range(3):
            other = ((x + i + 1) % 4 * 2 + yh) * 2 + c
            other = flipped(other) if h else other
            for cp in w_copies(None, other, xs.at[h, 2 - i], xr.at[h, 2 - i], xp[2 - i]):
                cp.wait_recv()
            for cp in w_copies(None, other, cs.at[2 + 3 * h + i], cr.at[2 + 3 * h + i], core):
                cp.start()

    def z_send(k):
        def act(rows):
            for i in range(2):
                z_copy(k, i, rows).start()

        each(k, act)

    def z_forward(k):
        def act(rows):
            for i in range(2):
                z_copy(k, i, rows).wait_recv()
                on_copy(k, i, rows).start()

        each(k, act)

    def y_forward(k):
        def act(rows):
            for i in range(2):
                on_copy(k, i, rows).wait_recv()
            if rows == 64:
                for i in range(2):
                    y_copy(k, i).start()

        each(k, act)

    def gather_step(k, carry):
        @pl.when(k == 3)
        def _():
            o_copy(0).wait_recv()
            o_copy(1).wait_recv()

        @pl.when(k + 2 < N_TOK)
        def _():
            z_send(k + 2)

        @pl.when(k < N_TOK)
        def _():
            z_forward(k)

        @pl.when(k == N_TOK)
        def _():
            multiply(k - 2)

        @pl.when(k >= 1)
        def _():
            y_forward(k - 1)

        @pl.when(k == 2)
        def _():
            for cp in w_copies((qw, ow), d2, ws.at[0], wr.at[0], p2):
                cp.wait_recv()
            for i in (0, 2, 1):
                for cp in w_copies(None, d2, xs.at[1, i], xr.at[1, i], xp[i]):
                    cp.start()
            for cp in w_copies(None, d2, cs.at[1], cr.at[1], core):
                cp.start()

        @pl.when((k >= 3) & (k < N_TOK))
        def _():
            multiply(k - 3)

        @pl.when(k >= N_TOK - 1)
        def _():
            multiply(jnp.where(k == N_TOK, N_TOK - 1, N_TOK - 3))

        @pl.when(k < 4)
        def _():
            norm_step(k)

        @pl.when((k >= 4) & (k < 8))
        def _():
            slope_step(k - 4)

        @pl.when(k == 6)
        def _():
            x_arrive(0)

        return carry

    lax.fori_loop(0, N_TOK + 1, gather_step, 0)
    bias_step()

    pg[...] = (acc[...] * slope[...].reshape(512, slope.shape[2])).astype(BF16)
    combf = acc
    combf[...] = jnp.zeros_like(combf)

    token = dest[...]
    hot = (lax.broadcasted_iota(jnp.int32, (16, 64), 0) == token).astype(F32)
    before = (
        lax.broadcasted_iota(jnp.int32, (64, 64), 0) < lax.broadcasted_iota(jnp.int32, (64, 64), 1)
    ).astype(F32)
    rank = jnp.sum(jnp.dot(hot, before, preferred_element_type=F32) * hot, axis=0, keepdims=True)
    target = token * 16 + rank.astype(jnp.int32)
    row = lax.broadcasted_iota(jnp.int32, (256, 64), 0)
    placing = jnp.concatenate(
        [(row == target).astype(F32), (row == target + 8).astype(F32)], axis=1
    ).astype(BF16)

    def ry_copy(f, i):
        return remote(S.at[f, i], R.at[f, i], rys.at[f, i], ryr.at[f, i], (p1, p2)[i])

    def rz_copy(f, i):
        return remote(T.at[f, i], ZR.at[f, i], rzs.at[f, i], rzr.at[f, i], zp[i])

    def a_copy(j, s):
        dd = (d + s) % 16
        return remote(
            OUT.at[j, pl.ds(pl.multiple_of(dd * 16, 16), 16)],
            A.at[j, pl.ds(pl.multiple_of(d * 16, 16), 16)],
            as_.at[j],
            ar.at[j],
            dps[s - 1],
        )

    cidx = [d, d2]
    for h in range(2):
        for i in range(3):
            other = ((x + i + 1) % 4 * 2 + yh) * 2 + c
            cidx.append(flipped(other) if h else other)

    def weights_arrive():
        for n, index in enumerate(cidx):
            for cp in w_copies(None, index + 1 - 2 * c, cs.at[n], cr.at[n], core):
                cp.wait_recv()
        wo2[...] = wo[...].astype(F32).reshape(wo2.shape).astype(BF16)
        emit(1, wq, wq_o).start()
        emit(2, wo2, wo_o).start()

    def first_product(i):
        up_copy(i).wait()
        part = lax.dot_general(pg[...], down_v[i % 4, :, 0:V], NT, preferred_element_type=F32)

        @pl.when(i + 4 < N_FEAT)
        def _():
            up_copy(i + 4).start()

        part = part.reshape(4, 128, V)
        S[i, 0] = part[:, 64:96, :].astype(BF16)
        S[i, 1] = part[:, 96:128, :].astype(BF16)
        for h in range(2):
            ry_copy(i, h).start()
        own[i % 4] = part[:, 0:64, :]

    def over_y(f):
        for h in range(2):
            ry_copy(f, h).wait_recv()
        total = own[f % 4] + jnp.concatenate([R[f, 0].astype(F32), R[f, 1].astype(F32)], axis=1)
        T[f] = total[1:4].astype(BF16)
        T0[f % 4] = total[0]
        for h in (0, 2, 1):
            rz_copy(f, h).start()

    def over_z(f):
        for h in range(3):
            rz_copy(f, h).wait_recv()
        M[f] = (
            T0[f % 4] + ZR[f, 0].astype(F32) + ZR[f, 1].astype(F32) + ZR[f, 2].astype(F32)
        ).astype(BF16)

    def send_rows(j):
        both = jnp.concatenate([M[2 * j], M[2 * j + 1]], axis=0)
        OUT[j] = jnp.dot(placing, both, preferred_element_type=F32).astype(BF16)
        for s in range(1, 16):
            a_copy(j, s).start()
        here = pl.ds(pl.multiple_of(d * 16, 16), 16)
        A[j, here, :] = OUT[j, here, :]

    def open_step(i, carry):
        first_product(i)
        return carry

    lax.fori_loop(0, 3, open_step, 0)
    x_arrive(1)

    def sum_step(f, carry):
        over_y(f)

        @pl.when(f + 3 < N_FEAT)
        def _():
            first_product(f + 3)

        @pl.when(f >= 2)
        def _():
            over_z(f - 2)

        @pl.when((f >= 3) & (f % 2 == 1))
        def _():
            send_rows(f // 2 - 1)

        @pl.when(f == 0)
        def _():
            weights_arrive()
            lax.fori_loop(0, 3, qkv_step, 0)
            emit(4, proj, proj_o).start()

        @pl.when(f >= 1)
        def _():
            head_step(f - 1)

        return carry

    lax.fori_loop(0, N_FEAT, sum_step, 0)
    over_z(N_FEAT - 2)
    head_step(7)
    emit(5, prob, prob_o).start()
    over_z(N_FEAT - 1)
    send_rows(3)
    normt[...] = norm[...].astype(F32).T.astype(BF16)
    emit(3, normt, normt_o).start()
    output_step()

    fifteen = pl.ds(0, 240)
    for j in range(4):
        pltpu.make_async_copy(A.at[j, fifteen], A.at[j, fifteen], ar.at[j]).wait()
    out_row = lax.broadcasted_iota(jnp.int32, (128, 256), 0)
    in_row = lax.broadcasted_iota(jnp.int32, (128, 256), 1)
    wanted = (out_row % 4) * 64 + (out_row // 32) * 16 + (out_row // 4) % 8
    for h in range(2):
        order = (in_row == wanted + 8 * h).astype(F32).astype(BF16)
        for g in range(4):
            stacked = A[:, 64 * g : 64 * g + 64, :].reshape(256, V)
            cot[128 * g : 128 * g + 128, V * h : V * h + V] = jnp.dot(
                order, stacked, preferred_element_type=F32
            ).astype(BF16)
    emit(0, cot, cot_o).start()

    for n, index in enumerate(cidx):
        for cp in w_copies(None, index, cs.at[n], cr.at[n], core):
            cp.wait_send()
    for cp in w_copies((qw, ow), d, ws.at[0], wr.at[0], p2):
        cp.wait_send()
    for h in range(2):
        for i in range(3):
            for cp in w_copies(None, d2 if h else d, xs.at[h, i], xr.at[h, i], xp[i]):
                cp.wait_send()
    for zz in range(4):
        pre_copy(zz).wait_send()

    def drain(k, carry):
        def act(rows):
            for i in range(2):
                z_copy(k, i, rows).wait_send()
                on_copy(k, i, rows).wait_send()
                if rows == 64:
                    y_copy(k, i).wait_send()

        each(k, act)
        return carry

    lax.fori_loop(0, N_TOK, drain, 0)
    o_copy(0).wait_send()
    o_copy(1).wait_send()

    def drain2(f, carry):
        for i in range(2):
            ry_copy(f, i).wait_send()
        for i in range(3):
            rz_copy(f, i).wait_send()
        return carry

    lax.fori_loop(0, N_FEAT, drain2, 0)
    for j in range(4):
        pltpu.make_async_copy(OUT.at[j, fifteen], OUT.at[j, fifteen], as_.at[j]).wait()
    pairs = [
        (cot, cot_o), (wq, wq_o), (wo2, wo_o), (normt, normt_o), (proj, proj_o),
        (prob, prob_o), (combt, combt_o), (n2, n2_o), (r2, r2_o),
    ]
    for n, (source, target) in enumerate(pairs):
        emit(n, source, target).wait()


def merger(tok, dest, down, up, pre, qw, ow, xin, win, ng, mg):
    vm = pl.BlockSpec(memory_space=pltpu.VMEM)
    hbm = pl.BlockSpec(memory_space=pl.ANY)
    dma = pltpu.SemaphoreType.DMA
    hid = pre.shape[1]
    feat = up.shape[0]
    V = feat // N_FEAT
    kept = [
        ((512, 1280), BF16),
        ((16,) + qw.shape, BF16),
        ((640, 1280), BF16),
        ((1280, 512), BF16),
        ((3, 512, 640), BF16),
        ((8, 4, 128, 256), BF16),
        ((640, 512), BF16),
        ((512, 1280), F32),
        ((512, 1), F32),
    ]
    return pl.pallas_call(
        merger_kernel,
        name="merger",
        out_shape=tuple(jax.ShapeDtypeStruct(*k) for k in kept),
        in_specs=[hbm, vm, hbm, hbm, vm, vm, vm, vm, vm, vm, vm],
        out_specs=(hbm,) * len(kept),
        scratch_shapes=[
            pltpu.VMEM((4, 128, tok.shape[1]), BF16),
            pltpu.VMEM((4, 640, 1024), BF16),
            pltpu.VMEM((4, 128, hid), F32),
            pltpu.VMEM((512, hid), F32),
            pltpu.VMEM((512, hid), BF16),
            pltpu.VMEM((128, hid), BF16),
            pltpu.VMEM((N_FEAT, 2, 4, 32, V), BF16),
            pltpu.VMEM((N_FEAT, 2, 4, 32, V), BF16),
            pltpu.VMEM((4, 4, 64, V), F32),
            pltpu.VMEM((N_FEAT, 3, 64, V), BF16),
            pltpu.VMEM((4, 64, V), F32),
            pltpu.VMEM((N_FEAT, 3, 64, V), BF16),
            pltpu.VMEM((N_FEAT, 64, V), BF16),
            pltpu.VMEM((4, 256, V), BF16),
            pltpu.VMEM((4, 256, V), BF16),
            pltpu.VMEM((512, 1280), BF16),
            pltpu.VMEM((16,) + qw.shape, BF16),
            pltpu.VMEM((16,) + ow.shape, BF16),
            pltpu.VMEM((640, 1280), BF16),
            pltpu.VMEM((512, 1280), BF16),
            pltpu.VMEM((1280, 512), BF16),
            pltpu.VMEM((3, 512, 640), BF16),
            pltpu.VMEM((8, 4, 128, 256), BF16),
            pltpu.VMEM((640, 512), BF16),
            pltpu.VMEM((512, 1280), F32),
            pltpu.VMEM((512, 1), F32),
            pltpu.VMEM((4, 128, 256), F32),
            dma((1,)),
            dma((4,)),
            dma((2,)), dma((2,)),
            dma((9,)),
            dma((N_TOK, 2)), dma((N_TOK, 2)), dma((N_TOK, 2)), dma((N_TOK, 2)), dma((N_TOK, 2)), dma((N_TOK, 2)),
            dma((4,)), dma((4,)),
            dma((1, 2)), dma((1, 2)),
            dma((2, 3, 2)), dma((2, 3, 2)),
            dma((8, 2)), dma((8, 2)),
            dma((N_FEAT, 2)), dma((N_FEAT, 2)),
            dma((N_FEAT, 3)), dma((N_FEAT, 3)),
            dma((4,)), dma((4,)),
        ],
        compiler_params=pltpu.CompilerParams(
            collective_id=1, has_side_effects=True, vmem_limit_bytes=62 << 20
        ),
        cost_estimate=pl.CostEstimate(flops=9 * 10**9, bytes_accessed=40 * 10**6, transcendentals=0),
    )(tok, dest, down, up, pre, qw, ow, xin, win, ng, mg)


def block_kernel(
    cot_i, wq_i, wo_i, normt_i, proj_i, prob_i, combt_i, n2_i, r2_i, xin, ng, mg,
    lg, pout, oout,
    cot, wq, wo, normt, proj, prob, combt, n2, r2,
    db, dc, wof, DP, dpb,
    gl, ga, gb, Cl, Ca, Cb, Z, ZR, E2, XR2, El, YRl, Fl, FRl,
    Sa, XRa, E1, ZR2, Ea, YRa, Fa, FRa, Sb, YRb, Eb2, XRb, Zb, Fb,
    ins, cls, clr, cas, car, cbs, cbr, zs, zr, x2s, x2r, yls, ylr, fls, flr,
    xas, xar, z2s, z2r, yas, yar, fas, far, ybs, ybr, xbs, xbr, zbs, zbr, pbs, pbr,
):
    x, yh, c, z, yl = place()
    pairs = [
        (cot_i, cot), (n2_i, n2), (r2_i, r2), (wo_i, wo), (combt_i, combt), (prob_i, prob), (proj_i, proj),
        (normt_i, normt), (wq_i, wq),
    ]
    loads = [pltpu.make_async_copy(a, b, ins.at[n]) for n, (a, b) in enumerate(pairs)]
    for cp in loads:
        cp.start()
    zp = [at(x, yh, c, (z + s) % 4, yl) for s in (1, 2, 3)]
    xp = [at((x + s) % 4, yh, c, z, yl) for s in (1, 2, 3)]
    core = at(x, yh, 1 - c, z, yl)
    p1 = at(x, yh, c, z, 1 - yl)
    p2 = at(x, 1 - yh, c, z, 1 - yl)
    yhp = at(x, 1 - yh, c, z, yl)
    greet(zp + xp + [core, p1, p2, yhp])

    def cl_copy(p):
        return remote(gl.at[p, :, 1 - c], Cl.at[p], cls.at[p], clr.at[p], core)

    def ca_copy(p):
        return remote(ga.at[p, :, 1 - c], Ca.at[p], cas.at[p], car.at[p], core)

    def cb_copy(p):
        return remote(gb.at[p, :, 1 - c], Cb.at[p], cbs.at[p], cbr.at[p], core)

    def z_copy(i):
        t = (z + i + 1) % 4
        return remote(Z.at[t % 2, t // 2], ZR.at[i], zs.at[i], zr.at[i], zp[i])

    def summed_l(p):
        cl_copy(p).wait_recv()
        total = (gl[p, :, c].astype(F32) + Cl[p].astype(F32)).astype(BF16).reshape(4, 2, 80, 640)
        Z[p, 0] = total[:, 0]
        Z[p, 1] = total[:, 1]
        for i in (0, 2, 1):

            @pl.when((z + i + 1) % 2 == p)
            def _():
                z_copy(i).start()

    def x2_copy(i):
        return remote(E2.at[(x + i + 1) % 4], XR2.at[i], x2s.at[i], x2r.at[i], xp[i])

    def xa_copy(p, i):
        return remote(
            Sa.at[p, pl.ds((x + i + 1) % 4 * 2, 2)], XRa.at[i, p], xas.at[p, i], xar.at[p, i], xp[i]
        )

    def summed_a(p):
        ca_copy(p).wait_recv()
        Sa[p] = (ga[p, :, c].astype(F32) + Ca[p].astype(F32)).astype(BF16)
        for i in (0, 2, 1):
            xa_copy(p, i).start()

    def z2_copy(i):
        t = (z + i + 1) % 4
        return remote(E1.at[t // 2, t % 2], ZR2.at[i], z2s.at[i], z2r.at[i], zp[i])

    def yb_copy(i):
        return remote(
            Sb.at[(1 - yl, 1 - yl, yl)[i], (yh, 1 - yh, 1 - yh)[i]],
            YRb.at[i],
            ybs.at[i],
            ybr.at[i],
            (p1, p2, yhp)[i],
        )

    def summed_b(p):
        cb_copy(p).wait_recv()
        total = (gb[p, :, c].astype(F32) + Cb[p].astype(F32)).astype(BF16)
        total = total.reshape((4, 2) + total.shape[1:])
        Sb[p, 0] = total[:, 0]
        Sb[p, 1] = total[:, 1]

    def xb_copy(i):
        return remote(Eb2.at[(x + i + 1) % 4], XRb.at[i], xbs.at[i], xbr.at[i], xp[i])

    def zb_copy(i):
        return remote(Zb.at[z], Zb.at[z], zbs.at[i], zbr.at[i], zp[i])

    def pb_copy():
        return remote(Fb.at[yl], Fb.at[yl], pbs.at[0], pbr.at[0], p1)

    owner = yh == z // 2

    def y_copy(i, e, yr, s_sem, r_sem):
        return remote(e, yr.at[i], s_sem.at[i], r_sem.at[i], (p1, p2, yhp)[i])

    def f_copy(i, f, fr, s_sem, r_sem):
        return remote(f, fr.at[z % 2], s_sem.at[i], r_sem.at[z % 2], zp[i])

    def owners_send(e, yr, s_sem, r_sem):
        @pl.when(owner)
        def _():
            y_copy(0, e, yr, s_sem, r_sem).start()

        @pl.when(jnp.logical_not(owner))
        def _():
            for i in (1, 2):
                y_copy(i, e, yr, s_sem, r_sem).start()

    def owners_sum(e, yr, s_sem, r_sem, f, fr, fs_sem, fr_sem):
        @pl.when(owner)
        def _():
            for i in range(3):
                y_copy(i, e, yr, s_sem, r_sem).wait_recv()
            total = (e[...].astype(F32) + yr[0].astype(F32)) + (yr[1].astype(F32) + yr[2].astype(F32))
            f[...] = (total * (1.0 / 128.0)).astype(BF16)
            for i in (0, 2, 1):
                f_copy(i, f, fr, fs_sem, fr_sem).start()
            fr[z % 2] = f[...]

    def owners_end(e, yr, s_sem, r_sem, f, fr, fs_sem, fr_sem):
        @pl.when(owner)
        def _():
            y_copy(0, e, yr, s_sem, r_sem).wait_send()
            there = 1 - z % 2
            pltpu.make_async_copy(fr.at[there], fr.at[there], fr_sem.at[there]).wait()
            for i in range(3):
                f_copy(i, f, fr, fs_sem, fr_sem).wait_send()

        @pl.when(jnp.logical_not(owner))
        def _():
            for i in (1, 2):
                y_copy(i, e, yr, s_sem, r_sem).wait_send()
            for there in range(2):
                pltpu.make_async_copy(fr.at[there], fr.at[there], fr_sem.at[there]).wait()

    last_l = (El, YRl, yls, ylr)
    last_a = (Ea, YRa, yas, yar)
    more_l = (Fl, FRl, fls, flr)
    more_a = (Fa, FRa, fas, far)

    loads[0].wait()
    loads[1].wait()
    loads[2].wait()
    loads[3].wait()

    def out_step(t, carry):
        rows = pl.ds(pl.multiple_of(t * 128, 128), 128)
        slope = cot[rows, :].astype(F32) * mg[...].reshape(1, 1280)
        unit = n2[rows, :]
        grad = r2[rows, :] * (slope - unit * jnp.mean(slope * unit, axis=-1, keepdims=True))
        n2[rows, :] = grad
        db[rows, :] = grad.astype(BF16)
        return carry

    lax.fori_loop(0, 4, out_step, 0)
    dc[...] = lax.dot_general(db[...], wo[...], NT, preferred_element_type=F32).astype(BF16)
    loads[4].wait()

    def wo_step(t, carry):
        cols = pl.ds(pl.multiple_of(t * 640, 128), 640)
        wof[t] = jnp.dot(combt[...], db[:, cols], preferred_element_type=F32)
        return carry

    lax.fori_loop(0, 2, wo_step, 0)
    gl[1] = (
        jnp.concatenate([wof[0].reshape(16, 40, 640), wof[1].reshape(16, 40, 640)], axis=1)
        .astype(BF16)
        .reshape(8, 2, 80, 640)
    )
    cl_copy(1).start()

    DP[...] = jnp.zeros_like(DP)
    loads[5].wait()

    def value_step(h, carry):
        lanes, mask = head_lanes(h)
        for b in range(4):
            grad = dc[pl.ds(128 * b, 128), lanes] * mask
            DP[2, pl.ds(KEYS[b], 256), lanes] += lax.dot_general(
                prob[h, b], grad, TN, preferred_element_type=F32
            )
        return carry

    lax.fori_loop(0, 8, value_step, 0)
    summed_l(1)
    loads[7].wait()
    dpb[2] = DP[2].astype(BF16)
    gl[0] = jnp.dot(normt[...], dpb[2], preferred_element_type=F32).astype(BF16).reshape(8, 2, 80, 640)
    cl_copy(0).start()
    loads[6].wait()

    def part_grad(p, first, width):
        cols = slice(first, first + width)
        dpb[p, :, cols] = DP[p, :, cols].astype(BF16)
        grad = jnp.dot(normt[...], dpb[p, :, cols], preferred_element_type=F32)
        return grad.astype(BF16).reshape(8, 2, 80, width)

    def head_step(h, carry):
        lanes, mask = head_lanes(h)
        for b in range(4):
            rows, keys = pl.ds(128 * b, 128), pl.ds(KEYS[b], 256)
            query = proj[0, rows, lanes] * mask
            key = proj[1, keys, lanes] * mask
            grad = dc[rows, lanes] * mask
            wide = prob[h, b].astype(F32)
            slope = lax.dot_general(grad, proj[2, keys, lanes], NT, preferred_element_type=F32)
            slope = wide * (slope - jnp.sum(slope * wide, axis=-1, keepdims=True)) * HEAD_DIM ** (-0.5)
            slope = slope.astype(BF16)
            DP[0, rows, lanes] += jnp.dot(slope, key, preferred_element_type=F32)
            DP[1, keys, lanes] += lax.dot_general(slope, query, TN, preferred_element_type=F32)

        @pl.when(h == 1)
        def _():
            summed_l(0)

        @pl.when(h == 4)
        def _():
            for p in range(2):
                ga[p] = part_grad(p, 0, N_LEFT)
                ca_copy(p).start()

        @pl.when(h == 6)
        def _():
            summed_a(0)
            summed_a(1)

        return carry

    lax.fori_loop(0, 8, head_step, 0)
    for p in range(2):
        gb[p] = part_grad(p, N_LEFT, 640 - N_LEFT)
        cb_copy(p).start()

    for i in range(3):
        z_copy(i).wait_recv()
    mine = Z[z % 2, z // 2].astype(F32)
    for i in range(3):
        mine = mine + ZR[i].astype(F32)
    E2[...] = mine.astype(BF16)
    for i in (0, 2, 1):
        x2_copy(i).start()
    loads[8].wait()

    def input_dot(half):
        total = jnp.zeros((512, 640), F32)
        for p in range(3):
            total += lax.dot_general(
                dpb[p],
                wq[8 * half : 8 * half + 8, :, 640 * p : 640 * p + 640].reshape(640, 640),
                NT,
                preferred_element_type=F32,
            )
        wof[half, 0:512, :] = total

    input_dot(0)
    summed_b(0)
    summed_b(1)
    for i in range(3):
        yb_copy(i).start()
    for i in range(3):
        x2_copy(i).wait_recv()
    mine = E2[x].astype(F32)
    for i in range(3):
        mine = mine + XR2[i].astype(F32)
    El[...] = mine.astype(BF16)
    owners_send(*last_l)
    input_dot(1)

    for p in range(2):
        for i in range(3):
            xa_copy(p, i).wait_recv()
        mine = Sa[p, pl.ds(2 * x, 2)].astype(F32)
        for i in range(3):
            mine = mine + XRa[i, p].astype(F32)
        E1[0, p] = mine[0].astype(BF16)
        E1[1, p] = mine[1].astype(BF16)
    for i in (0, 2, 1):
        z2_copy(i).start()
    owners_sum(*last_l, *more_l)

    def input_step(t, carry):
        rows = pl.ds(pl.multiple_of(t * 128, 128), 128)
        slope = jnp.concatenate([wof[0, rows, :], wof[1, rows, :]], axis=1)
        slope = slope.astype(BF16).astype(F32) * ng[...].reshape(1, 1280)
        value = xin[rows, :].astype(F32)
        factor = lax.rsqrt(jnp.mean(value * value, axis=-1, keepdims=True) + EPSILON)
        unit = value * factor
        grad = factor * (slope - unit * jnp.mean(slope * unit, axis=-1, keepdims=True))
        lg[rows, :] = (grad + n2[rows, :]).astype(BF16)
        return carry

    lax.fori_loop(0, 4, input_step, 0)

    for i in range(3):
        yb_copy(i).wait_recv()
    mine = Sb[yl, yh].astype(F32)
    for i in range(3):
        mine = mine + YRb[i].astype(F32)
    Eb2[...] = mine.astype(BF16)
    for i in (0, 2, 1):
        xb_copy(i).start()

    for i in range(3):
        z2_copy(i).wait_recv()
    mine = E1[z // 2, z % 2].astype(F32)
    for i in range(3):
        mine = mine + ZR2[i].astype(F32)
    Ea[...] = mine.astype(BF16)
    owners_send(*last_a)

    for i in range(3):
        xb_copy(i).wait_recv()
    mine = Eb2[x].astype(F32)
    for i in range(3):
        mine = mine + XRb[i].astype(F32)
    Zb[z] = mine.astype(BF16)
    for i in (0, 2, 1):
        zb_copy(i).start()
    owners_sum(*last_a, *more_a)
    for i in range(3):
        there = (z + 3 - i) % 4
        pltpu.make_async_copy(Zb.at[there], Zb.at[there], zbr.at[i]).wait()
    total = (Zb[0].astype(F32) + Zb[1].astype(F32)) + (Zb[2].astype(F32) + Zb[3].astype(F32))
    Fb[yl] = (total * (1.0 / 128.0)).astype(BF16)
    pb_copy().start()

    owners_end(*last_l, *more_l)
    pout[:, 1280:1920] = FRl[0].astype(F32)
    last = FRl[1].astype(F32)
    oout[:, 0:640] = last[0:40]
    oout[:, 640:1280] = last[40:80]
    owners_end(*last_a, *more_a)
    other = 1 - yl
    pltpu.make_async_copy(Fb.at[other], Fb.at[other], pbr.at[0]).wait()
    for p in range(2):
        pout[:, 640 * p : 640 * p + N_LEFT] = FRa[p].astype(F32)
        pout[:, 640 * p + N_LEFT : 640 * p + 640] = Fb[p].astype(F32)

    pb_copy().wait_send()
    for p in range(2):
        cl_copy(p).wait_send()
        ca_copy(p).wait_send()
        cb_copy(p).wait_send()
    for i in range(3):
        for p in range(2):
            xa_copy(p, i).wait_send()
        z_copy(i).wait_send()
        x2_copy(i).wait_send()
        z2_copy(i).wait_send()
        yb_copy(i).wait_send()
        xb_copy(i).wait_send()
        zb_copy(i).wait_send()


def block_grads(cot, wq, wo, normt, proj, prob, combt, n2, r2, xin, ng, mg):
    vm = pl.BlockSpec(memory_space=pltpu.VMEM)
    hbm = pl.BlockSpec(memory_space=pl.ANY)
    dma = pltpu.SemaphoreType.DMA
    t, ta, tb = (80, 640), (80, N_LEFT), (80, 640 - N_LEFT)
    held = (cot, wq, wo, normt, proj, prob, combt, n2, r2)
    return pl.pallas_call(
        block_kernel,
        name="block",
        out_shape=(
            jax.ShapeDtypeStruct((512, 1280), BF16),
            jax.ShapeDtypeStruct((80, 1920), F32),
            jax.ShapeDtypeStruct((40, 1280), F32),
        ),
        in_specs=[hbm] * 9 + [vm] * 3,
        out_specs=(vm, vm, vm),
        scratch_shapes=[pltpu.VMEM(k.shape, k.dtype) for k in held]
        + [
            pltpu.VMEM((512, 1280), BF16),
            pltpu.VMEM((512, 640), BF16),
            pltpu.VMEM((2, 640, 640), F32),
            pltpu.VMEM((3, 512, 640), F32),
            pltpu.VMEM((3, 512, 640), BF16),
            pltpu.VMEM((2, 8, 2) + t, BF16),
            pltpu.VMEM((2, 8, 2) + ta, BF16),
            pltpu.VMEM((2, 8, 2) + tb, BF16),
            pltpu.VMEM((2, 8) + t, BF16),
            pltpu.VMEM((2, 8) + ta, BF16),
            pltpu.VMEM((2, 8) + tb, BF16),
            pltpu.VMEM((2, 2, 4) + t, BF16),
            pltpu.VMEM((3, 4) + t, BF16),
            pltpu.VMEM((4,) + t, BF16),
            pltpu.VMEM((3,) + t, BF16),
            pltpu.VMEM(t, BF16),
            pltpu.VMEM((3,) + t, BF16),
            pltpu.VMEM(t, BF16),
            pltpu.VMEM((2,) + t, BF16),
            pltpu.VMEM((2, 8) + ta, BF16),
            pltpu.VMEM((3, 2, 2) + ta, BF16),
            pltpu.VMEM((2, 2) + ta, BF16),
            pltpu.VMEM((3,) + ta, BF16),
            pltpu.VMEM(ta, BF16),
            pltpu.VMEM((3,) + ta, BF16),
            pltpu.VMEM(ta, BF16),
            pltpu.VMEM((2,) + ta, BF16),
            pltpu.VMEM((2, 2, 4) + tb, BF16),
            pltpu.VMEM((3, 4) + tb, BF16),
            pltpu.VMEM((4,) + tb, BF16),
            pltpu.VMEM((3,) + tb, BF16),
            pltpu.VMEM((4,) + tb, BF16),
            pltpu.VMEM((2,) + tb, BF16),
            dma((9,)),
            dma((2,)), dma((2,)), dma((2,)), dma((2,)), dma((2,)), dma((2,)),
            dma((3,)), dma((3,)), dma((3,)), dma((3,)), dma((3,)), dma((3,)), dma((3,)), dma((2,)),
            dma((2, 3)), dma((2, 3)), dma((3,)), dma((3,)), dma((3,)), dma((3,)), dma((3,)), dma((2,)),
            dma((3,)), dma((3,)), dma((3,)), dma((3,)), dma((3,)), dma((3,)), dma((1,)), dma((1,)),
        ],
        compiler_params=pltpu.CompilerParams(
            collective_id=2, has_side_effects=True, vmem_limit_bytes=62 << 20
        ),
        cost_estimate=pl.CostEstimate(flops=8 * 10**9, bytes_accessed=40 * 10**6, transcendentals=0),
    )(cot, wq, wo, normt, proj, prob, combt, n2, r2, xin, ng, mg)


def local(
    token_grads,
    token_dest,
    merger_down,
    merger_up,
    merger_pre,
    layer_input,
    window_ids,
    norm_gain,
    merge_gain,
    qkv_weight,
    proj_weight,
):
    kept = merger(
        token_grads, token_dest.reshape(1, 64), merger_down, merger_up, merger_pre, qkv_weight, proj_weight,
        layer_input, window_ids, norm_gain, merge_gain,
    )
    return block_grads(*kept, layer_input, norm_gain, merge_gain)


def solution(mesh):
    return jax.shard_map(
        local,
        mesh=mesh,
        in_specs=(
            P(("dp", "llm"), None),
            P(("dp", "llm"), None),
            P("llm", None),
            P(None, "llm"),
            P("dp", "llm"),
            P(("dp", "llm"), None),
            P(("dp", "llm"), None),
            P(),
            P(),
            P("dp", None),
            P("dp", None),
        ),
        out_specs=(P(("dp", "llm"), None), P("dp", None), P("dp", None)),
        check_vma=False,
    )
```

```python
import jax
import jax.numpy as jnp
from jax import lax
from jax.experimental import pallas as pl
from jax.experimental.pallas import tpu as pltpu
from jax.sharding import PartitionSpec as P

MESH = pl.DeviceIdType.MESH
HEAD_DIM = 80
CAP = 8
EPSILON = 1e-06
BF16 = jnp.bfloat16
F32 = jnp.float32

NT = (((1,), (1,)), ((), ()))
TN = (((0,), (0,)), ((), ()))

N_TOK = 8
N_NARROW = 5
N_LEFT = 384
N_FEAT = 8


def gelu_slope(values):
    return (
        0.5 * (1.0 + lax.erf(values * 0.7071067811865476))
        + values * jnp.exp(-0.5 * values * values) * 0.3989422804014327
    )


def rms_scale(values, scaling):
    return values * lax.rsqrt(jnp.mean(values * values, axis=-1, keepdims=True) + EPSILON) * scaling


KEYS = (0, 64, 192, 256)


def head_lanes(h):
    start = 128 * jnp.minimum(5 * h // 8, 3)
    lane = lax.broadcasted_iota(jnp.int32, (1, 256), 1) + start
    mask = ((lane >= HEAD_DIM * h) & (lane < HEAD_DIM * h + HEAD_DIM)).astype(F32).astype(BF16)
    return pl.ds(pl.multiple_of(start, 128), 256), mask


def overlap(parts):
    a, b, c, d = parts
    return jnp.concatenate(
        [
            a[0:64],
            a[64:192] + b[0:128],
            a[192:256] + b[128:192] + c[0:64],
            b[192:256] + c[64:128] + d[0:64],
            c[128:256] + d[64:192],
            d[192:256],
        ],
        axis=0,
    )


def place():
    d, l = lax.axis_index("dp"), lax.axis_index("llm")
    return d // 4, (d // 2) % 2, d % 2, l // 2, l % 2


def at(x, yh, c, z, yl):
    return (x * 2 + yh) * 2 + c, z * 2 + yl


def remote(src, dst, send, recv, device):
    return pltpu.make_async_remote_copy(
        src_ref=src, dst_ref=dst, send_sem=send, recv_sem=recv, device_id=device, device_id_type=MESH
    )


def greet(devices):
    barrier = pltpu.get_barrier_semaphore()
    for device in devices:
        pl.semaphore_signal(barrier, inc=1, device_id=device, device_id_type=MESH)


def met(devices):
    pl.semaphore_wait(pltpu.get_barrier_semaphore(), len(devices))


def merger_kernel(
    tok, dest, down, up, pre, qw, ow, xin, win, ng, mg,
    cot_o, wq_o, wo_o, normt_o, proj_o, prob_o, combt_o, n2_o, r2_o,
    G, down_v, slope, acc, pg, pre2,
    S, R, own, T, T0, ZR, QS, QR, Q0, M, OUT, A,
    cot, wq, wo, wo2, norm, normt, proj, prob, combt, n2, r2, bias,
    loc, dsem, os_, or_, outs, zs, zr, ns, nr, ys, yr, ps, pr, ws, wr, xs, xr, cs, cr, rys, ryr, rzs, rzr, qs, qr, as_, ar,
):
    x, yh, c, z, yl = place()
    d = (x * 2 + yh) * 2 + c
    l = z * 2 + yl
    zp = [at(x, yh, c, (z + s) % 4, yl) for s in (1, 2, 3)]
    p1 = at(x, yh, c, z, 1 - yl)
    p2 = at(x, 1 - yh, c, z, 1 - yl)
    yhp = at(x, 1 - yh, c, z, yl)
    xp = [at((x + s) % 4, yh, c, z, yl) for s in (1, 2, 3)]
    core = at(x, yh, 1 - c, z, yl)
    dps = [((d + s) % 16, l) for s in range(1, 16)]

    cp_tok = pltpu.make_async_copy(tok, G.at[0, pl.ds(0, 64)], loc.at[0])
    cp_tok.start()
    for k in range(4):
        pltpu.make_async_copy(down.at[:, pl.ds(1024 * k, 1024)], down_v.at[k], dsem.at[k]).start()
    greet(zp + [p1, p2] + dps)
    met(zp + [p1, p2] + dps)
    cp_tok.wait()

    W = G.shape[2] // N_TOK

    def col(k):
        return pl.ds(pl.multiple_of(k * W, W), W)

    def down_copy(k):
        return pltpu.make_async_copy(down.at[:, col(k)], down_v.at[k % 4], dsem.at[k % 4])

    V = M.shape[2]

    def up_copy(f):
        rows = pl.ds(pl.multiple_of(f * V, V), V)
        return pltpu.make_async_copy(up.at[rows], down_v.at[f % 4, :, pl.ds(0, V)], dsem.at[f % 4])

    def z_copy(k, i, rows):
        return remote(
            G.at[0, pl.ds(0, rows), col(k)],
            G.at[(3, 1)[i], pl.ds(0, rows), col(k)],
            zs.at[k, i],
            zr.at[k, i],
            (zp[0], zp[2])[i],
        )

    def on_copy(k, i, rows):
        half = pl.ds(pl.multiple_of(k * W + i * (W // 2), W // 2), W // 2)
        return remote(
            G.at[(3, 1)[i], pl.ds(0, rows), half],
            G.at[2, pl.ds(0, rows), half],
            ns.at[k, i],
            nr.at[k, i],
            (zp[0], zp[2])[i],
        )

    def each(k, act):
        @pl.when(k < N_NARROW)
        def _():
            act(64)

        @pl.when(k >= N_NARROW)
        def _():
            act(128)

    def y_copy(k, i):
        return remote(
            G.at[:, pl.ds(32 * i, 32), col(k)],
            G.at[:, pl.ds(64 + 32 * i, 32), col(k)],
            ys.at[k, i],
            yr.at[k, i],
            (p1, p2)[i],
        )

    def o_copy(i):
        wide = pl.ds(N_NARROW * W, (N_TOK - N_NARROW) * W)
        return remote(
            G.at[0, pl.ds(32 * i, 32), wide],
            G.at[0, pl.ds(64 + 32 * i, 32), wide],
            os_.at[i],
            or_.at[i],
            (p1, p2)[i],
        )

    o_copy(0).start()
    for k in range(2):
        for i in range(2):
            z_copy(k, i, 64).start()

    def pre_copy(zz):
        rows = pl.ds(pl.multiple_of((2 * zz + 1 - yl) * 64 + 32, 32), 32)
        return remote(pre.at[rows], pre2.at[pl.ds(32 * zz, 32)], ps.at[zz], pr.at[zz], yhp)

    def w_copies(source, index, sends, recvs, device):
        first = wq.at[index] if source is None else source[0]
        second = wo.at[index] if source is None else source[1]
        return [
            remote(first, wq.at[index], sends.at[0], recvs.at[0], device),
            remote(second, wo.at[index], sends.at[1], recvs.at[1], device),
        ]

    def flipped(dd):
        return dd + 2 - 4 * ((dd // 2) % 2)

    wq[d] = qw[...]
    wo[d] = ow[...]
    d2 = flipped(d)
    for cp in w_copies((qw, ow), d, ws.at[0], wr.at[0], p2):
        cp.start()
    o_copy(1).start()
    for i in (0, 2, 1):
        for cp in w_copies((qw, ow), d, xs.at[0, i], xr.at[0, i], xp[i]):
            cp.start()
    for cp in w_copies((qw, ow), d, cs.at[0], cr.at[0], core):
        cp.start()
    for zz in range(4):
        pre_copy(zz).start()

    def emit(n, source, target):
        return pltpu.make_async_copy(source, target, outs.at[n])

    def slope_step(r):
        @pl.when(r == 0)
        def _():
            for zz in range(4):
                pre_copy(zz).wait_recv()

        zz = (z + r) % 4
        mine = pre[pl.ds(pl.multiple_of((2 * zz + yl) * 64, 64), 64), :]
        slope[r, 0:64, :] = gelu_slope(mine.astype(F32))
        first = pre[pl.ds(pl.multiple_of((2 * zz + 1 - yl) * 64, 64), 32), :]
        second = pre2[pl.ds(pl.multiple_of(zz * 32, 32), 32), :]
        slope[r, 64:96, :] = gelu_slope(first.astype(F32))
        slope[r, 96:128, :] = gelu_slope(second.astype(F32))

    def norm_step(k):
        rows = pl.ds(pl.multiple_of(k * 128, 128), 128)
        norm[rows, :] = rms_scale(xin[rows, :].astype(F32), ng[...].reshape(1, 1280)).astype(BF16)

    def bias_step():
        for b in range(4):
            queries = jnp.broadcast_to(win[:, 128 * b : 128 * b + 128].astype(F32), (128, 128)).T
            for h in range(2):
                keys = win[:, KEYS[b] + 128 * h : KEYS[b] + 128 * h + 128].astype(F32)
                bias[b, :, 128 * h : 128 * h + 128] = jnp.where(queries == keys, 0.0, -1e30)

    def qkv_step(p, carry):
        cols = pl.ds(pl.multiple_of(p * 640, 128), 640)
        weight = wq[:, :, cols].reshape(1280, 640)
        proj[p] = jnp.dot(norm[...], weight, preferred_element_type=F32).astype(BF16)
        return carry

    def head_step(h):
        lanes, mask = head_lanes(h)
        shares = []
        for b in range(4):
            scores = lax.dot_general(
                proj[0, pl.ds(128 * b, 128), lanes] * mask,
                proj[1, pl.ds(KEYS[b], 256), lanes],
                NT,
                preferred_element_type=F32,
            )
            scores = scores * HEAD_DIM ** (-0.5) + bias[b]
            powers = jnp.exp(scores - jnp.max(scores, axis=-1, keepdims=True))
            shares.append((powers * (1.0 / jnp.sum(powers, axis=-1, keepdims=True))).astype(BF16))
        parts = [
            jnp.dot(shares[b], proj[2, pl.ds(KEYS[b], 256), lanes] * mask, preferred_element_type=F32)
            for b in range(4)
        ]
        for b in range(4):
            prob[h, b] = shares[b]
        combf[:, lanes] += jnp.concatenate(parts, axis=0)

    def output_step():
        comb = combf[...].astype(BF16)
        combt[...] = combf[...].T.astype(BF16)
        emit(6, combt, combt_o).start()
        for t in range(4):
            rows = pl.ds(128 * t, 128)
            value = xin[rows, :].astype(F32) + jnp.dot(
                comb[128 * t : 128 * t + 128], wo2[...], preferred_element_type=F32
            )
            factor = lax.rsqrt(jnp.mean(value * value, axis=-1, keepdims=True) + EPSILON)
            n2[rows, :] = value * factor
            r2[rows, :] = factor
        emit(7, n2, n2_o).start()
        emit(8, r2, r2_o).start()

    acc[...] = jnp.zeros_like(acc)

    def multiply(k):
        @pl.when(k < N_NARROW)
        def _():
            for i in range(2):
                y_copy(k, i).wait_recv()

        tile = G[:, :, col(k)].reshape(512, W)
        down_copy(k).wait()
        acc[...] += lax.dot_general(tile, down_v[k % 4], NT, preferred_element_type=F32)

        @pl.when(k + 4 < N_TOK)
        def _():
            down_copy(k + 4).start()

        @pl.when(k >= 4)
        def _():
            up_copy(k - 4).start()


    def x_arrive(h):
        for i in range(3):
            other = ((x + i + 1) % 4 * 2 + yh) * 2 + c
            other = flipped(other) if h else other
            for cp in w_copies(None, other, xs.at[h, 2 - i], xr.at[h, 2 - i], xp[2 - i]):
                cp.wait_recv()
            for cp in w_copies(None, other, cs.at[2 + 3 * h + i], cr.at[2 + 3 * h + i], core):
                cp.start()

    def z_send(k):
        def act(rows):
            for i in range(2):
                z_copy(k, i, rows).start()

        each(k, act)

    def z_forward(k):
        def act(rows):
            for i in range(2):
                z_copy(k, i, rows).wait_recv()
                on_copy(k, i, rows).start()

        each(k, act)

    def y_forward(k):
        def act(rows):
            for i in range(2):
                on_copy(k, i, rows).wait_recv()
            if rows == 64:
                for i in range(2):
                    y_copy(k, i).start()

        each(k, act)

    def gather_step(k, carry):
        @pl.when(k == 3)
        def _():
            o_copy(0).wait_recv()
            o_copy(1).wait_recv()

        @pl.when(k + 2 < N_TOK)
        def _():
            z_send(k + 2)

        @pl.when(k < N_TOK)
        def _():
            z_forward(k)

        @pl.when(k >= 3)
        def _():
            multiply(jnp.where(k == N_TOK, N_TOK - 2, k - 3))

        @pl.when(k >= 1)
        def _():
            y_forward(k - 1)

        @pl.when(k == 2)
        def _():
            for cp in w_copies((qw, ow), d2, ws.at[0], wr.at[0], p2):
                cp.wait_recv()
            for i in (0, 2, 1):
                for cp in w_copies(None, d2, xs.at[1, i], xr.at[1, i], xp[i]):
                    cp.start()
            for cp in w_copies(None, d2, cs.at[1], cr.at[1], core):
                cp.start()

        @pl.when(k >= N_TOK - 1)
        def _():
            multiply(jnp.where(k == N_TOK, N_TOK - 1, N_TOK - 3))

        @pl.when(k < 4)
        def _():
            norm_step(k)

        @pl.when((k >= 4) & (k < 8))
        def _():
            slope_step(k - 4)

        @pl.when(k == 6)
        def _():
            x_arrive(0)

        return carry

    lax.fori_loop(0, N_TOK + 1, gather_step, 0)
    bias_step()

    pg[...] = (acc[...] * slope[...].reshape(512, slope.shape[2])).astype(BF16)
    combf = acc
    combf[...] = jnp.zeros_like(combf)

    token = dest[...]
    hot = (lax.broadcasted_iota(jnp.int32, (16, 64), 0) == token).astype(F32)
    before = (
        lax.broadcasted_iota(jnp.int32, (64, 64), 0) < lax.broadcasted_iota(jnp.int32, (64, 64), 1)
    ).astype(F32)
    rank = jnp.sum(jnp.dot(hot, before, preferred_element_type=F32) * hot, axis=0, keepdims=True)
    target = token * 16 + rank.astype(jnp.int32)
    row = lax.broadcasted_iota(jnp.int32, (256, 64), 0)
    placing = jnp.concatenate(
        [(row == target).astype(F32), (row == target + 8).astype(F32)], axis=1
    ).astype(BF16)

    def ry_copy(f, i):
        return remote(S.at[f, i], R.at[f, i], rys.at[f, i], ryr.at[f, i], (p1, p2)[i])

    def rz_copy(f, i):
        return remote(T.at[f, i], ZR.at[f, i], rzs.at[f, i], rzr.at[f, i], zp[i])

    def a_copy(j, s):
        dd = (d + s) % 16
        return remote(
            OUT.at[j, pl.ds(pl.multiple_of(dd * 16, 16), 16)],
            A.at[j, pl.ds(pl.multiple_of(d * 16, 16), 16)],
            as_.at[j],
            ar.at[j],
            dps[s - 1],
        )

    cidx = [d, d2]
    for h in range(2):
        for i in range(3):
            other = ((x + i + 1) % 4 * 2 + yh) * 2 + c
            cidx.append(flipped(other) if h else other)

    def weights_arrive():
        for n, index in enumerate(cidx):
            for cp in w_copies(None, index + 1 - 2 * c, cs.at[n], cr.at[n], core):
                cp.wait_recv()
        wo2[...] = wo[...].astype(F32).reshape(wo2.shape).astype(BF16)
        emit(1, wq, wq_o).start()
        emit(2, wo2, wo_o).start()

    def product(i):
        up_copy(i).wait()
        part = lax.dot_general(pg[...], down_v[i % 4, :, 0:V], NT, preferred_element_type=F32)

        @pl.when(i + 4 < N_FEAT)
        def _():
            up_copy(i + 4).start()

        return part.reshape(4, 128, V)

    def q_copy(f, i):
        return remote(QS.at[f, i], QR.at[f, i], qs.at[f, i], qr.at[f, i], zp[i])

    def z_product(f, carry):
        part = product(f)
        QS[f] = part[1:4].astype(BF16)
        for i in (0, 2, 1):
            q_copy(f, i).start()
        Q0[f] = part[0]
        return carry

    def z_sum(f):
        for i in range(3):
            q_copy(f, i).wait_recv()
        total = Q0[f] + QR[f, 0].astype(F32) + QR[f, 1].astype(F32) + QR[f, 2].astype(F32)
        S[f, 0, 0] = total[64:96].astype(BF16)
        S[f, 1, 0] = total[96:128].astype(BF16)
        Q0[f, 0:64] = total[0:64]
        for i in range(2):
            qy_copy(f, i).start()

    def qy_copy(f, i):
        return remote(S.at[f, i, 0], R.at[f, i, 0], rys.at[f, i], ryr.at[f, i], (p1, p2)[i])

    def z_end(f):
        for i in range(2):
            qy_copy(f, i).wait_recv()
        M[f] = (
            Q0[f, 0:64] + jnp.concatenate([R[f, 0, 0].astype(F32), R[f, 1, 0].astype(F32)], axis=0)
        ).astype(BF16)

    def y_product(f, carry):
        part = product(f)
        S[f, 0] = part[:, 64:96, :].astype(BF16)
        S[f, 1] = part[:, 96:128, :].astype(BF16)
        for h in range(2):
            ry_copy(f, h).start()
        own[f % 4] = part[:, 0:64, :]
        return carry

    def over_y(f):
        for h in range(2):
            ry_copy(f, h).wait_recv()
        total = own[f % 4] + jnp.concatenate([R[f, 0].astype(F32), R[f, 1].astype(F32)], axis=1)
        T[f] = total[1:4].astype(BF16)
        T0[f % 4] = total[0]
        for h in (0, 2, 1):
            rz_copy(f, h).start()

    def over_z(f):
        for h in range(3):
            rz_copy(f, h).wait_recv()
        M[f] = (
            T0[f % 4] + ZR[f, 0].astype(F32) + ZR[f, 1].astype(F32) + ZR[f, 2].astype(F32)
        ).astype(BF16)

    def send_rows(j):
        both = jnp.concatenate([M[2 * j], M[2 * j + 1]], axis=0)
        OUT[j] = jnp.dot(placing, both, preferred_element_type=F32).astype(BF16)
        for s in range(1, 16):
            a_copy(j, s).start()
        here = pl.ds(pl.multiple_of(d * 16, 16), 16)
        A[j, here, :] = OUT[j, here, :]

    lax.fori_loop(0, 2, z_product, 0)
    lax.fori_loop(2, 5, y_product, 0)
    x_arrive(1)

    def late_head(h, carry):
        head_step(h)
        return carry

    def sum_step(f, carry):
        over_y(f)

        @pl.when(f + 3 < N_FEAT)
        def _():
            y_product(f + 3, 0)

        @pl.when(f == 2)
        def _():
            weights_arrive()

        @pl.when(f == 3)
        def _():
            lax.fori_loop(0, 3, qkv_step, 0)
            emit(4, proj, proj_o).start()

        @pl.when((f == 4) | (f == 5))
        def _():
            head_step(f - 4)

        @pl.when(f >= 6)
        def _():
            lax.fori_loop(2 * f - 10, 2 * f - 8, late_head, 0)

        @pl.when(f >= 4)
        def _():
            over_z(f - 2)

        @pl.when((f == 3) | (f == 4))
        def _():
            z_sum(f - 3)

        @pl.when(f == 5)
        def _():
            z_end(0)
            z_end(1)
            send_rows(jnp.int32(0))

        @pl.when((f == 5) | (f == 7))
        def _():
            send_rows((f - 3) // 2)

        return carry

    lax.fori_loop(2, N_FEAT, sum_step, 0)
    over_z(N_FEAT - 2)
    head_step(6)
    over_z(N_FEAT - 1)
    send_rows(3)

    head_step(7)
    emit(5, prob, prob_o).start()
    normt[...] = norm[...].astype(F32).T.astype(BF16)
    emit(3, normt, normt_o).start()
    output_step()

    fifteen = pl.ds(0, 240)
    for j in range(4):
        pltpu.make_async_copy(A.at[j, fifteen], A.at[j, fifteen], ar.at[j]).wait()
    out_row = lax.broadcasted_iota(jnp.int32, (128, 256), 0)
    in_row = lax.broadcasted_iota(jnp.int32, (128, 256), 1)
    wanted = (out_row % 4) * 64 + (out_row // 32) * 16 + (out_row // 4) % 8
    for h in range(2):
        order = (in_row == wanted + 8 * h).astype(F32).astype(BF16)
        for g in range(4):
            stacked = A[:, 64 * g : 64 * g + 64, :].reshape(256, V)
            cot[128 * g : 128 * g + 128, V * h : V * h + V] = jnp.dot(
                order, stacked, preferred_element_type=F32
            ).astype(BF16)
    emit(0, cot, cot_o).start()

    for n, index in enumerate(cidx):
        for cp in w_copies(None, index, cs.at[n], cr.at[n], core):
            cp.wait_send()
    for cp in w_copies((qw, ow), d, ws.at[0], wr.at[0], p2):
        cp.wait_send()
    for h in range(2):
        for i in range(3):
            for cp in w_copies(None, d2 if h else d, xs.at[h, i], xr.at[h, i], xp[i]):
                cp.wait_send()
    for zz in range(4):
        pre_copy(zz).wait_send()

    def drain(k, carry):
        def act(rows):
            for i in range(2):
                z_copy(k, i, rows).wait_send()
                on_copy(k, i, rows).wait_send()
                if rows == 64:
                    y_copy(k, i).wait_send()

        each(k, act)
        return carry

    lax.fori_loop(0, N_TOK, drain, 0)
    o_copy(0).wait_send()
    o_copy(1).wait_send()

    def drain2(f, carry):
        for i in range(2):
            ry_copy(f, i).wait_send()
        for i in range(3):
            rz_copy(f, i).wait_send()
        return carry

    lax.fori_loop(2, N_FEAT, drain2, 0)
    for f in range(2):
        for i in range(3):
            q_copy(f, i).wait_send()
        for i in range(2):
            qy_copy(f, i).wait_send()
    for j in range(4):
        pltpu.make_async_copy(OUT.at[j, fifteen], OUT.at[j, fifteen], as_.at[j]).wait()
    pairs = [
        (cot, cot_o), (wq, wq_o), (wo2, wo_o), (normt, normt_o), (proj, proj_o),
        (prob, prob_o), (combt, combt_o), (n2, n2_o), (r2, r2_o),
    ]
    for n, (source, target) in enumerate(pairs):
        emit(n, source, target).wait()


def merger(tok, dest, down, up, pre, qw, ow, xin, win, ng, mg):
    vm = pl.BlockSpec(memory_space=pltpu.VMEM)
    hbm = pl.BlockSpec(memory_space=pl.ANY)
    dma = pltpu.SemaphoreType.DMA
    hid = pre.shape[1]
    feat = up.shape[0]
    V = feat // N_FEAT
    kept = [
        ((512, 1280), BF16),
        ((16,) + qw.shape, BF16),
        ((640, 1280), BF16),
        ((1280, 512), BF16),
        ((3, 512, 640), BF16),
        ((8, 4, 128, 256), BF16),
        ((640, 512), BF16),
        ((512, 1280), F32),
        ((512, 1), F32),
    ]
    return pl.pallas_call(
        merger_kernel,
        name="merger",
        out_shape=tuple(jax.ShapeDtypeStruct(*k) for k in kept),
        in_specs=[hbm, vm, hbm, hbm, vm, vm, vm, vm, vm, vm, vm],
        out_specs=(hbm,) * len(kept),
        scratch_shapes=[
            pltpu.VMEM((4, 128, tok.shape[1]), BF16),
            pltpu.VMEM((4, 640, 1024), BF16),
            pltpu.VMEM((4, 128, hid), F32),
            pltpu.VMEM((512, hid), F32),
            pltpu.VMEM((512, hid), BF16),
            pltpu.VMEM((128, hid), BF16),
            pltpu.VMEM((N_FEAT, 2, 4, 32, V), BF16),
            pltpu.VMEM((N_FEAT, 2, 4, 32, V), BF16),
            pltpu.VMEM((4, 4, 64, V), F32),
            pltpu.VMEM((N_FEAT, 3, 64, V), BF16),
            pltpu.VMEM((4, 64, V), F32),
            pltpu.VMEM((N_FEAT, 3, 64, V), BF16),
            pltpu.VMEM((2, 3, 128, V), BF16),
            pltpu.VMEM((2, 3, 128, V), BF16),
            pltpu.VMEM((2, 128, V), F32),
            pltpu.VMEM((N_FEAT, 64, V), BF16),
            pltpu.VMEM((4, 256, V), BF16),
            pltpu.VMEM((4, 256, V), BF16),
            pltpu.VMEM((512, 1280), BF16),
            pltpu.VMEM((16,) + qw.shape, BF16),
            pltpu.VMEM((16,) + ow.shape, BF16),
            pltpu.VMEM((640, 1280), BF16),
            pltpu.VMEM((512, 1280), BF16),
            pltpu.VMEM((1280, 512), BF16),
            pltpu.VMEM((3, 512, 640), BF16),
            pltpu.VMEM((8, 4, 128, 256), BF16),
            pltpu.VMEM((640, 512), BF16),
            pltpu.VMEM((512, 1280), F32),
            pltpu.VMEM((512, 1), F32),
            pltpu.VMEM((4, 128, 256), F32),
            dma((1,)),
            dma((4,)),
            dma((2,)), dma((2,)),
            dma((9,)),
            dma((N_TOK, 2)), dma((N_TOK, 2)), dma((N_TOK, 2)), dma((N_TOK, 2)), dma((N_TOK, 2)), dma((N_TOK, 2)),
            dma((4,)), dma((4,)),
            dma((1, 2)), dma((1, 2)),
            dma((2, 3, 2)), dma((2, 3, 2)),
            dma((8, 2)), dma((8, 2)),
            dma((N_FEAT, 2)), dma((N_FEAT, 2)),
            dma((N_FEAT, 3)), dma((N_FEAT, 3)),
            dma((2, 3)), dma((2, 3)),
            dma((4,)), dma((4,)),
        ],
        compiler_params=pltpu.CompilerParams(
            collective_id=1, has_side_effects=True, vmem_limit_bytes=62 << 20
        ),
        cost_estimate=pl.CostEstimate(flops=9 * 10**9, bytes_accessed=40 * 10**6, transcendentals=0),
    )(tok, dest, down, up, pre, qw, ow, xin, win, ng, mg)


def block_kernel(
    cot_i, wq_i, wo_i, normt_i, proj_i, prob_i, combt_i, n2_i, r2_i, xin, ng, mg,
    lg, pout, oout,
    cot, wq, wo, normt, proj, prob, combt, n2, r2,
    db, dc, wof, DP, dpb,
    gl, ga, Cl, Ca, Z, ZR, E2, XR2, El, YRl, Fl, FRl,
    Sa, XRa, E1, ZR2, Ea, YRa, Fa, FRa,
    gm, Cm, Sm, YRm, Em, XRm, Zm, Fm,
    gb, Cb, Sb, YRb, Eb, XRb, Zb, Fb,
    ins, cls, clr, cas, car, zs, zr, x2s, x2r, yls, ylr, fls, flr,
    xas, xar, z2s, z2r, yas, yar, fas, far,
    cms, cmr, yms, ymr, xms, xmr, zms, zmr, pms, pmr,
    cbs, cbr, ybs, ybr, xbs, xbr, zbs, zbr, pbs, pbr,
):
    x, yh, c, z, yl = place()
    pairs = [
        (cot_i, cot), (n2_i, n2), (r2_i, r2), (wo_i, wo), (combt_i, combt), (prob_i, prob), (proj_i, proj),
        (normt_i, normt), (wq_i, wq),
    ]
    loads = [pltpu.make_async_copy(a, b, ins.at[n]) for n, (a, b) in enumerate(pairs)]
    zp = [at(x, yh, c, (z + s) % 4, yl) for s in (1, 2, 3)]
    xp = [at((x + s) % 4, yh, c, z, yl) for s in (1, 2, 3)]
    core = at(x, yh, 1 - c, z, yl)
    p1 = at(x, yh, c, z, 1 - yl)
    p2 = at(x, 1 - yh, c, z, 1 - yl)
    yhp = at(x, 1 - yh, c, z, yl)

    greet(zp + xp + [core, p1, p2, yhp])
    for cp in loads[:3]:
        cp.start()

    def cl_copy(p):
        return remote(gl.at[p, :, 1 - c], Cl.at[p], cls.at[p], clr.at[p], core)

    def ca_copy(p):
        return remote(ga.at[p, :, 1 - c], Ca.at[p], cas.at[p], car.at[p], core)

    def z_copy(i):
        t = (z + i + 1) % 4
        return remote(Z.at[t % 2, t // 2], ZR.at[i], zs.at[i], zr.at[i], zp[i])

    def summed_l(p):
        cl_copy(p).wait_recv()
        total = (gl[p, :, c].astype(F32) + Cl[p].astype(F32)).astype(BF16).reshape(4, 2, 80, N_LEFT)
        Z[p, 0] = total[:, 0]
        Z[p, 1] = total[:, 1]
        for i in (0, 2, 1):

            @pl.when((z + i + 1) % 2 == p)
            def _():
                z_copy(i).start()

    def x2_copy(i):
        return remote(E2.at[(x + i + 1) % 4], XR2.at[i], x2s.at[i], x2r.at[i], xp[i])

    def xa_copy(p, i):
        return remote(
            Sa.at[p, pl.ds((x + i + 1) % 4 * 2, 2)], XRa.at[i, p], xas.at[p, i], xar.at[p, i], xp[i]
        )

    def summed_a(p):
        ca_copy(p).wait_recv()
        Sa[p] = (ga[p, :, c].astype(F32) + Ca[p].astype(F32)).astype(BF16)
        for i in (0, 2, 1):
            xa_copy(p, i).start()

    def z2_copy(i):
        t = (z + i + 1) % 4
        return remote(E1.at[t // 2, t % 2], ZR2.at[i], z2s.at[i], z2r.at[i], zp[i])

    def y_first(g, C, S, YR, E, XR, ZZ, F, cs, cr, ys, yr, xs, xr, zs, zr, ps, pr):
        def c_copy(p):
            return remote(g.at[p, :, 1 - c], C.at[p], cs.at[p], cr.at[p], core)

        def y_copy(i):
            return remote(
                S.at[(1 - yl, 1 - yl, yl)[i], (yh, 1 - yh, 1 - yh)[i]],
                YR.at[i],
                ys.at[i],
                yr.at[i],
                (p1, p2, yhp)[i],
            )

        def x_copy(i):
            return remote(E.at[(x + i + 1) % 4], XR.at[i], xs.at[i], xr.at[i], xp[i])

        def z_copy(i):
            return remote(ZZ.at[z], ZZ.at[z], zs.at[i], zr.at[i], zp[i])

        def p_copy():
            return remote(F.at[yl], F.at[yl], ps.at[0], pr.at[0], p1)

        def add_cores(p):
            c_copy(p).wait_recv()
            total = (g[p, :, c].astype(F32) + C[p].astype(F32)).astype(BF16)
            total = total.reshape((4, 2) + total.shape[1:])
            S[p, 0] = total[:, 0]
            S[p, 1] = total[:, 1]

        def start_y():
            for i in range(3):
                y_copy(i).start()

        def add_y():
            for i in range(3):
                y_copy(i).wait_recv()
            mine = S[yl, yh].astype(F32)
            for i in range(3):
                mine = mine + YR[i].astype(F32)
            E[...] = mine.astype(BF16)
            for i in (0, 2, 1):
                x_copy(i).start()

        def add_x():
            for i in range(3):
                x_copy(i).wait_recv()
            mine = E[x].astype(F32)
            for i in range(3):
                mine = mine + XR[i].astype(F32)
            ZZ[z] = mine.astype(BF16)
            for i in (0, 2, 1):
                z_copy(i).start()

        def add_z():
            for i in range(3):
                there = (z + 3 - i) % 4
                pltpu.make_async_copy(ZZ.at[there], ZZ.at[there], zr.at[i]).wait()
            total = (ZZ[0].astype(F32) + ZZ[1].astype(F32)) + (ZZ[2].astype(F32) + ZZ[3].astype(F32))
            F[yl] = (total * (1.0 / 128.0)).astype(BF16)
            p_copy().start()

        def finish():
            other = 1 - yl
            pltpu.make_async_copy(F.at[other], F.at[other], pr.at[0]).wait()

        def drain():
            p_copy().wait_send()
            for p in range(2):
                c_copy(p).wait_send()
            for i in range(3):
                y_copy(i).wait_send()
                x_copy(i).wait_send()
                z_copy(i).wait_send()

        return c_copy, add_cores, start_y, add_y, add_x, add_z, finish, drain

    m_core, m_cores, m_start, m_y, m_x, m_z, m_finish, m_drain = y_first(
        gm, Cm, Sm, YRm, Em, XRm, Zm, Fm, cms, cmr, yms, ymr, xms, xmr, zms, zmr, pms, pmr
    )
    b_core, b_cores, b_start, b_y, b_x, b_z, b_finish, b_drain = y_first(
        gb, Cb, Sb, YRb, Eb, XRb, Zb, Fb, cbs, cbr, ybs, ybr, xbs, xbr, zbs, zbr, pbs, pbr
    )

    owner = yh == z // 2

    def y_copy(i, e, yr, s_sem, r_sem):
        return remote(e, yr.at[i], s_sem.at[i], r_sem.at[i], (p1, p2, yhp)[i])

    def f_copy(i, f, fr, s_sem, r_sem):
        return remote(f, fr.at[z % 2], s_sem.at[i], r_sem.at[z % 2], zp[i])

    def owners_send(e, yr, s_sem, r_sem):
        @pl.when(owner)
        def _():
            y_copy(0, e, yr, s_sem, r_sem).start()

        @pl.when(jnp.logical_not(owner))
        def _():
            for i in (1, 2):
                y_copy(i, e, yr, s_sem, r_sem).start()

    def owners_sum(e, yr, s_sem, r_sem, f, fr, fs_sem, fr_sem):
        @pl.when(owner)
        def _():
            for i in range(3):
                y_copy(i, e, yr, s_sem, r_sem).wait_recv()
            total = (e[...].astype(F32) + yr[0].astype(F32)) + (yr[1].astype(F32) + yr[2].astype(F32))
            f[...] = (total * (1.0 / 128.0)).astype(BF16)
            for i in (0, 2, 1):
                f_copy(i, f, fr, fs_sem, fr_sem).start()
            fr[z % 2] = f[...]

    def owners_end(e, yr, s_sem, r_sem, f, fr, fs_sem, fr_sem):
        @pl.when(owner)
        def _():
            y_copy(0, e, yr, s_sem, r_sem).wait_send()
            there = 1 - z % 2
            pltpu.make_async_copy(fr.at[there], fr.at[there], fr_sem.at[there]).wait()
            for i in range(3):
                f_copy(i, f, fr, fs_sem, fr_sem).wait_send()

        @pl.when(jnp.logical_not(owner))
        def _():
            for i in (1, 2):
                y_copy(i, e, yr, s_sem, r_sem).wait_send()
            for there in range(2):
                pltpu.make_async_copy(fr.at[there], fr.at[there], fr_sem.at[there]).wait()

    last_l = (El, YRl, yls, ylr)
    last_a = (Ea, YRa, yas, yar)
    more_l = (Fl, FRl, fls, flr)
    more_a = (Fa, FRa, fas, far)

    loads[0].wait()
    loads[1].wait()
    loads[2].wait()
    for cp in loads[3:]:
        cp.start()

    def out_step(t, carry):
        rows = pl.ds(pl.multiple_of(t * 128, 128), 128)
        slope = cot[rows, :].astype(F32) * mg[...].reshape(1, 1280)
        unit = n2[rows, :]
        grad = r2[rows, :] * (slope - unit * jnp.mean(slope * unit, axis=-1, keepdims=True))
        n2[rows, :] = grad
        db[rows, :] = grad.astype(BF16)
        return carry

    lax.fori_loop(0, 4, out_step, 0)
    loads[3].wait()
    dc[...] = lax.dot_general(db[...], wo[...], NT, preferred_element_type=F32).astype(BF16)
    loads[4].wait()

    def wo_step(t, carry):
        cols = pl.ds(pl.multiple_of(t * 640, 128), 640)
        wof[t] = jnp.dot(combt[...], db[:, cols], preferred_element_type=F32)
        return carry

    lax.fori_loop(0, 2, wo_step, 0)
    grad_o = (
        jnp.concatenate([wof[0].reshape(16, 40, 640), wof[1].reshape(16, 40, 640)], axis=1)
        .astype(BF16)
        .reshape(8, 2, 80, 640)
    )
    gl[1] = grad_o[..., :N_LEFT]
    gm[1] = grad_o[..., N_LEFT:]
    met(zp + xp + [core, p1, p2, yhp])
    cl_copy(1).start()
    m_core(1).start()

    DP[...] = jnp.zeros_like(DP)
    loads[5].wait()

    def value_step(h, carry):
        lanes, mask = head_lanes(h)
        parts = [
            lax.dot_general(
                prob[h, b], dc[pl.ds(128 * b, 128), lanes] * mask, TN, preferred_element_type=F32
            )
            for b in range(4)
        ]
        DP[2, :, lanes] += overlap(parts)
        return carry

    lax.fori_loop(0, 8, value_step, 0)
    loads[7].wait()
    def part_grad(p, first, width):
        cols = slice(first, first + width)
        dpb[p, :, cols] = DP[p, :, cols].astype(BF16)
        grad = jnp.dot(normt[...], dpb[p, :, cols], preferred_element_type=F32)
        return grad.astype(BF16).reshape(8, 2, 80, width)

    gl[0] = part_grad(2, 0, N_LEFT)
    cl_copy(0).start()
    gm[0] = part_grad(2, N_LEFT, 640 - N_LEFT)
    m_core(0).start()
    summed_l(1)
    m_cores(1)
    loads[6].wait()

    def head_step(h, carry):
        lanes, mask = head_lanes(h)
        slopes = []
        for b in range(4):
            grad = dc[pl.ds(128 * b, 128), lanes] * mask
            wide = prob[h, b].astype(F32)
            slope = lax.dot_general(
                grad, proj[2, pl.ds(KEYS[b], 256), lanes], NT, preferred_element_type=F32
            )
            slope = wide * (slope - jnp.sum(slope * wide, axis=-1, keepdims=True)) * HEAD_DIM ** (-0.5)
            slopes.append(slope.astype(BF16))
        parts = [
            jnp.dot(slopes[b], proj[1, pl.ds(KEYS[b], 256), lanes] * mask, preferred_element_type=F32)
            for b in range(4)
        ]
        DP[0, :, lanes] += jnp.concatenate(parts, axis=0)
        parts = [
            lax.dot_general(
                slopes[b], proj[0, pl.ds(128 * b, 128), lanes] * mask, TN, preferred_element_type=F32
            )
            for b in range(4)
        ]
        DP[1, :, lanes] += overlap(parts)

        @pl.when(h == 0)
        def _():
            summed_l(0)
            m_cores(0)
            m_start()

        @pl.when(h == 4)
        def _():
            for p in range(2):
                ga[p] = part_grad(p, 0, N_LEFT)
                ca_copy(p).start()

        @pl.when(h == 6)
        def _():
            summed_a(0)
            summed_a(1)
            m_y()

        return carry

    lax.fori_loop(0, 8, head_step, 0)
    for p in range(2):
        gb[p] = part_grad(p, N_LEFT, 640 - N_LEFT)
        b_core(p).start()

    def input_dot(half):
        total = jnp.zeros((512, 640), F32)
        for p in range(3):
            total += lax.dot_general(
                dpb[p],
                wq[8 * half : 8 * half + 8, :, 640 * p : 640 * p + 640].reshape(640, 640),
                NT,
                preferred_element_type=F32,
            )
        wof[half, 0:512, :] = total

    loads[8].wait()
    input_dot(0)
    b_cores(0)
    b_cores(1)
    b_start()

    for i in range(3):
        z_copy(i).wait_recv()
    mine = Z[z % 2, z // 2].astype(F32)
    for i in range(3):
        mine = mine + ZR[i].astype(F32)
    E2[...] = mine.astype(BF16)
    for i in (0, 2, 1):
        x2_copy(i).start()
    input_dot(1)

    def input_step(t, carry):
        rows = pl.ds(pl.multiple_of(t * 128, 128), 128)
        slope = jnp.concatenate([wof[0, rows, :], wof[1, rows, :]], axis=1)
        slope = slope.astype(BF16).astype(F32) * ng[...].reshape(1, 1280)
        value = xin[rows, :].astype(F32)
        factor = lax.rsqrt(jnp.mean(value * value, axis=-1, keepdims=True) + EPSILON)
        unit = value * factor
        grad = factor * (slope - unit * jnp.mean(slope * unit, axis=-1, keepdims=True))
        lg[rows, :] = (grad + n2[rows, :]).astype(BF16)
        return carry

    lax.fori_loop(0, 4, input_step, 0)

    for p in range(2):
        for i in range(3):
            xa_copy(p, i).wait_recv()
        mine = Sa[p, pl.ds(2 * x, 2)].astype(F32)
        for i in range(3):
            mine = mine + XRa[i, p].astype(F32)
        E1[0, p] = mine[0].astype(BF16)
        E1[1, p] = mine[1].astype(BF16)
    for i in (0, 2, 1):
        z2_copy(i).start()
    m_x()
    b_y()
    for i in range(3):
        x2_copy(i).wait_recv()
    mine = E2[x].astype(F32)
    for i in range(3):
        mine = mine + XR2[i].astype(F32)
    El[...] = mine.astype(BF16)
    owners_send(*last_l)
    for i in range(3):
        z2_copy(i).wait_recv()
    mine = E1[z // 2, z % 2].astype(F32)
    for i in range(3):
        mine = mine + ZR2[i].astype(F32)
    Ea[...] = mine.astype(BF16)
    owners_send(*last_a)
    m_z()
    b_x()
    owners_sum(*last_l, *more_l)
    owners_sum(*last_a, *more_a)
    b_z()

    m_finish()
    owners_end(*last_l, *more_l)
    pout[:, 1280 : 1280 + N_LEFT] = FRl[0].astype(F32)
    pout[:, 1280 + N_LEFT : 1920] = Fm[0].astype(F32)
    left, right = FRl[1].astype(F32), Fm[1].astype(F32)
    oout[:, 0:N_LEFT] = left[0:40]
    oout[:, N_LEFT:640] = right[0:40]
    oout[:, 640 : 640 + N_LEFT] = left[40:80]
    oout[:, 640 + N_LEFT : 1280] = right[40:80]
    owners_end(*last_a, *more_a)
    b_finish()
    for p in range(2):
        pout[:, 640 * p : 640 * p + N_LEFT] = FRa[p].astype(F32)
        pout[:, 640 * p + N_LEFT : 640 * p + 640] = Fb[p].astype(F32)

    m_drain()
    b_drain()
    for p in range(2):
        cl_copy(p).wait_send()
        ca_copy(p).wait_send()
    for i in range(3):
        for p in range(2):
            xa_copy(p, i).wait_send()
        z_copy(i).wait_send()
        x2_copy(i).wait_send()
        z2_copy(i).wait_send()


def block_grads(cot, wq, wo, normt, proj, prob, combt, n2, r2, xin, ng, mg):
    vm = pl.BlockSpec(memory_space=pltpu.VMEM)
    hbm = pl.BlockSpec(memory_space=pl.ANY)
    dma = pltpu.SemaphoreType.DMA
    ta, tb = (80, N_LEFT), (80, 640 - N_LEFT)
    held = (cot, wq, wo, normt, proj, prob, combt, n2, r2)
    return pl.pallas_call(
        block_kernel,
        name="block",
        out_shape=(
            jax.ShapeDtypeStruct((512, 1280), BF16),
            jax.ShapeDtypeStruct((80, 1920), F32),
            jax.ShapeDtypeStruct((40, 1280), F32),
        ),
        in_specs=[hbm] * 9 + [vm] * 3,
        out_specs=(vm, vm, vm),
        scratch_shapes=[pltpu.VMEM(k.shape, k.dtype) for k in held]
        + [
            pltpu.VMEM((512, 1280), BF16),
            pltpu.VMEM((512, 640), BF16),
            pltpu.VMEM((2, 640, 640), F32),
            pltpu.VMEM((3, 512, 640), F32),
            pltpu.VMEM((3, 512, 640), BF16),
            pltpu.VMEM((2, 8, 2) + ta, BF16),
            pltpu.VMEM((2, 8, 2) + ta, BF16),
            pltpu.VMEM((2, 8) + ta, BF16),
            pltpu.VMEM((2, 8) + ta, BF16),
            pltpu.VMEM((2, 2, 4) + ta, BF16),
            pltpu.VMEM((3, 4) + ta, BF16),
            pltpu.VMEM((4,) + ta, BF16),
            pltpu.VMEM((3,) + ta, BF16),
            pltpu.VMEM(ta, BF16),
            pltpu.VMEM((3,) + ta, BF16),
            pltpu.VMEM(ta, BF16),
            pltpu.VMEM((2,) + ta, BF16),
            pltpu.VMEM((2, 8) + ta, BF16),
            pltpu.VMEM((3, 2, 2) + ta, BF16),
            pltpu.VMEM((2, 2) + ta, BF16),
            pltpu.VMEM((3,) + ta, BF16),
            pltpu.VMEM(ta, BF16),
            pltpu.VMEM((3,) + ta, BF16),
            pltpu.VMEM(ta, BF16),
            pltpu.VMEM((2,) + ta, BF16),
        ]
        + [
            pltpu.VMEM((2, 8, 2) + tb, BF16),
            pltpu.VMEM((2, 8) + tb, BF16),
            pltpu.VMEM((2, 2, 4) + tb, BF16),
            pltpu.VMEM((3, 4) + tb, BF16),
            pltpu.VMEM((4,) + tb, BF16),
            pltpu.VMEM((3,) + tb, BF16),
            pltpu.VMEM((4,) + tb, BF16),
            pltpu.VMEM((2,) + tb, BF16),
        ]
        * 2
        + [
            dma((9,)),
            dma((2,)), dma((2,)), dma((2,)), dma((2,)),
            dma((3,)), dma((3,)), dma((3,)), dma((3,)), dma((3,)), dma((3,)), dma((3,)), dma((2,)),
            dma((2, 3)), dma((2, 3)), dma((3,)), dma((3,)), dma((3,)), dma((3,)), dma((3,)), dma((2,)),
        ]
        + [
            dma((2,)), dma((2,)), dma((3,)), dma((3,)), dma((3,)), dma((3,)), dma((3,)), dma((3,)),
            dma((1,)), dma((1,)),
        ]
        * 2,
        compiler_params=pltpu.CompilerParams(
            collective_id=2, has_side_effects=True, vmem_limit_bytes=62 << 20
        ),
        cost_estimate=pl.CostEstimate(flops=8 * 10**9, bytes_accessed=40 * 10**6, transcendentals=0),
    )(cot, wq, wo, normt, proj, prob, combt, n2, r2, xin, ng, mg)


def local(
    token_grads,
    token_dest,
    merger_down,
    merger_up,
    merger_pre,
    layer_input,
    window_ids,
    norm_gain,
    merge_gain,
    qkv_weight,
    proj_weight,
):
    kept = merger(
        token_grads, token_dest.reshape(1, 64), merger_down, merger_up, merger_pre, qkv_weight, proj_weight,
        layer_input, window_ids, norm_gain, merge_gain,
    )
    return block_grads(*kept, layer_input, norm_gain, merge_gain)


def solution(mesh):
    return jax.shard_map(
        local,
        mesh=mesh,
        in_specs=(
            P(("dp", "llm"), None),
            P(("dp", "llm"), None),
            P("llm", None),
            P(None, "llm"),
            P("dp", "llm"),
            P(("dp", "llm"), None),
            P(("dp", "llm"), None),
            P(),
            P(),
            P("dp", None),
            P("dp", None),
        ),
        out_specs=(P(("dp", "llm"), None), P("dp", None), P("dp", None)),
        check_vma=False,
    )
```

```python
import jax
import jax.numpy as jnp
from jax import lax
from jax.experimental import pallas as pl
from jax.experimental.pallas import tpu as pltpu
from jax.sharding import PartitionSpec as P

MESH = pl.DeviceIdType.MESH
HEAD_DIM = 80
CAP = 8
EPSILON = 1e-06
BF16 = jnp.bfloat16
F32 = jnp.float32

NT = (((1,), (1,)), ((), ()))
TN = (((0,), (0,)), ((), ()))

N_TOK = 16
N_NARROW = 10
N_LEFT = 384
N_X, N_Z = 256, 256
AHEAD = 3
LAG = 7
N_FEAT = 8


def gelu_slope(values):
    return (
        0.5 * (1.0 + lax.erf(values * 0.7071067811865476))
        + values * jnp.exp(-0.5 * values * values) * 0.3989422804014327
    )


def rms_scale(values, scaling):
    return values * lax.rsqrt(jnp.mean(values * values, axis=-1, keepdims=True) + EPSILON) * scaling


KEYS = (0, 64, 192, 256)


def head_lanes(h):
    start = 128 * jnp.minimum(5 * h // 8, 3)
    lane = lax.broadcasted_iota(jnp.int32, (1, 256), 1) + start
    mask = ((lane >= HEAD_DIM * h) & (lane < HEAD_DIM * h + HEAD_DIM)).astype(F32).astype(BF16)
    return pl.ds(pl.multiple_of(start, 128), 256), mask


def overlap(parts):
    a, b, c, d = parts
    return jnp.concatenate(
        [
            a[0:64],
            a[64:192] + b[0:128],
            a[192:256] + b[128:192] + c[0:64],
            b[192:256] + c[64:128] + d[0:64],
            c[128:256] + d[64:192],
            d[192:256],
        ],
        axis=0,
    )


def place():
    d, l = lax.axis_index("dp"), lax.axis_index("llm")
    return d // 4, (d // 2) % 2, d % 2, l // 2, l % 2


def at(x, yh, c, z, yl):
    return (x * 2 + yh) * 2 + c, z * 2 + yl


def remote(src, dst, send, recv, device):
    return pltpu.make_async_remote_copy(
        src_ref=src, dst_ref=dst, send_sem=send, recv_sem=recv, device_id=device, device_id_type=MESH
    )


def greet(devices):
    barrier = pltpu.get_barrier_semaphore()
    for device in devices:
        pl.semaphore_signal(barrier, inc=1, device_id=device, device_id_type=MESH)


def met(devices):
    pl.semaphore_wait(pltpu.get_barrier_semaphore(), len(devices))


def merger_kernel(
    tok, dest, down, up, pre, qw, ow, xin, win, ng, mg,
    cot_o, wq_o, wo_o, normt_o, proj_o, prob_o, combt_o, n2_o, r2_o,
    G, down_v, slope, acc, pg, pre2,
    S, R, own, T, T0, ZA, ZR, QS, QA, QR, Q0, M, OUT, A,
    cot, wq, wo, wo2, norm, normt, proj, prob, combt, n2, r2, bias,
    loc, dsem, os_, or_, outs, zs, zr, ns, nr, ys, yr, ps, pr, ws, wr, xs, xr, cs, cr, rys, ryr, rzs, rzr, qs, qr, as_, ar,
):
    x, yh, c, z, yl = place()
    d = (x * 2 + yh) * 2 + c
    l = z * 2 + yl
    zp = [at(x, yh, c, (z + s) % 4, yl) for s in (1, 2, 3)]
    p1 = at(x, yh, c, z, 1 - yl)
    p2 = at(x, 1 - yh, c, z, 1 - yl)
    yhp = at(x, 1 - yh, c, z, yl)
    xp = [at((x + s) % 4, yh, c, z, yl) for s in (1, 2, 3)]
    core = at(x, yh, 1 - c, z, yl)
    dps = [((d + s) % 16, l) for s in range(1, 16)]

    cp_tok = pltpu.make_async_copy(tok, G.at[0, pl.ds(0, 64)], loc.at[0])
    cp_tok.start()
    greet(zp + [p1, p2] + dps)
    met(zp + [p1, p2] + dps)
    cp_tok.wait()

    W = G.shape[2] // N_TOK

    def col(k):
        return pl.ds(pl.multiple_of(k * W, W), W)

    def chunk(p):
        turn = N_NARROW - LAG + 2
        return jnp.where(
            p < turn, p, jnp.where((p - turn) % 2 == 0, N_NARROW + (p - turn) // 2, turn + (p - turn) // 2)
        )

    def down_copy(p):
        return pltpu.make_async_copy(
            down.at[:, col(chunk(p))], down_v.at[p % 4, :, pl.ds(0, W)], dsem.at[p % 4]
        )

    for k in range(4):
        down_copy(jnp.int32(k)).start()
    V = M.shape[2]

    def up_copy(f):
        rows = pl.ds(pl.multiple_of(f * V, V), V)
        return pltpu.make_async_copy(up.at[rows], down_v.at[f % 4, :, pl.ds(0, V)], dsem.at[f % 4])

    def z_copy(k, i, rows):
        return remote(
            G.at[0, pl.ds(0, rows), col(k)],
            G.at[(3, 1)[i], pl.ds(0, rows), col(k)],
            zs.at[k, i],
            zr.at[k, i],
            (zp[0], zp[2])[i],
        )

    def on_copy(k, i, rows):
        half = pl.ds(pl.multiple_of(k * W + i * (W // 2), W // 2), W // 2)
        return remote(
            G.at[(3, 1)[i], pl.ds(0, rows), half],
            G.at[2, pl.ds(0, rows), half],
            ns.at[k, i],
            nr.at[k, i],
            (zp[0], zp[2])[i],
        )

    def each(k, act):
        @pl.when(k < N_NARROW)
        def _():
            act(64)

        @pl.when(k >= N_NARROW)
        def _():
            act(128)

    def y_copy(k, i):
        return remote(
            G.at[:, pl.ds(32 * i, 32), col(k)],
            G.at[:, pl.ds(64 + 32 * i, 32), col(k)],
            ys.at[k, i],
            yr.at[k, i],
            (p1, p2)[i],
        )

    def o_copy(i):
        wide = pl.ds(N_NARROW * W, (N_TOK - N_NARROW) * W)
        return remote(
            G.at[0, pl.ds(32 * i, 32), wide],
            G.at[0, pl.ds(64 + 32 * i, 32), wide],
            os_.at[i],
            or_.at[i],
            (p1, p2)[i],
        )

    o_copy(0).start()
    for k in range(AHEAD):
        for i in range(2):
            z_copy(k, i, 64).start()

    def pre_copy(zz):
        rows = pl.ds(pl.multiple_of((2 * zz + 1 - yl) * 64 + 32, 32), 32)
        return remote(pre.at[rows], pre2.at[pl.ds(32 * zz, 32)], ps.at[zz], pr.at[zz], yhp)

    def w_copies(source, index, sends, recvs, device):
        first = wq.at[index] if source is None else source[0]
        second = wo.at[index] if source is None else source[1]
        return [
            remote(first, wq.at[index], sends.at[0], recvs.at[0], device),
            remote(second, wo.at[index], sends.at[1], recvs.at[1], device),
        ]

    def flipped(dd):
        return dd + 2 - 4 * ((dd // 2) % 2)

    wq[d] = qw[...]
    wo[d] = ow[...]
    d2 = flipped(d)
    for cp in w_copies((qw, ow), d, ws.at[0], wr.at[0], p2):
        cp.start()
    o_copy(1).start()
    for i in (0, 2, 1):
        for cp in w_copies((qw, ow), d, xs.at[0, i], xr.at[0, i], xp[i]):
            cp.start()
    for cp in w_copies((qw, ow), d, cs.at[0], cr.at[0], core):
        cp.start()
    def emit(n, source, target):
        return pltpu.make_async_copy(source, target, outs.at[n])

    def slope_step(r):
        @pl.when(r == 0)
        def _():
            for zz in range(4):
                pre_copy(zz).wait_recv()

        zz = (z + r) % 4
        mine = pre[pl.ds(pl.multiple_of((2 * zz + yl) * 64, 64), 64), :]
        slope[r, 0:64, :] = gelu_slope(mine.astype(F32))
        first = pre[pl.ds(pl.multiple_of((2 * zz + 1 - yl) * 64, 64), 32), :]
        second = pre2[pl.ds(pl.multiple_of(zz * 32, 32), 32), :]
        slope[r, 64:96, :] = gelu_slope(first.astype(F32))
        slope[r, 96:128, :] = gelu_slope(second.astype(F32))

    def norm_step(k):
        rows = pl.ds(pl.multiple_of(k * 128, 128), 128)
        norm[rows, :] = rms_scale(xin[rows, :].astype(F32), ng[...].reshape(1, 1280)).astype(BF16)

    def bias_step():
        for b in range(4):
            queries = jnp.broadcast_to(win[:, 128 * b : 128 * b + 128].astype(F32), (128, 128)).T
            for h in range(2):
                keys = win[:, KEYS[b] + 128 * h : KEYS[b] + 128 * h + 128].astype(F32)
                bias[b, :, 128 * h : 128 * h + 128] = jnp.where(queries == keys, 0.0, -1e30)

    def qkv_step(p, carry):
        cols = pl.ds(pl.multiple_of(p * 640, 128), 640)
        weight = wq[:, :, cols].reshape(1280, 640)
        proj[p] = jnp.dot(norm[...], weight, preferred_element_type=F32).astype(BF16)
        return carry

    def head_step(h):
        lanes, mask = head_lanes(h)
        shares = []
        for b in range(4):
            scores = lax.dot_general(
                proj[0, pl.ds(128 * b, 128), lanes] * mask,
                proj[1, pl.ds(KEYS[b], 256), lanes],
                NT,
                preferred_element_type=F32,
            )
            scores = scores * HEAD_DIM ** (-0.5) + bias[b]
            powers = jnp.exp(scores - jnp.max(scores, axis=-1, keepdims=True))
            shares.append((powers * (1.0 / jnp.sum(powers, axis=-1, keepdims=True))).astype(BF16))
        parts = [
            jnp.dot(shares[b], proj[2, pl.ds(KEYS[b], 256), lanes] * mask, preferred_element_type=F32)
            for b in range(4)
        ]
        for b in range(4):
            prob[h, b] = shares[b]
        combf[:, lanes] += jnp.concatenate(parts, axis=0)

    def output_step():
        comb = combf[...].astype(BF16)
        combt[...] = combf[...].T.astype(BF16)
        emit(6, combt, combt_o).start()
        for t in range(4):
            rows = pl.ds(128 * t, 128)
            value = xin[rows, :].astype(F32) + jnp.dot(
                comb[128 * t : 128 * t + 128], wo2[...], preferred_element_type=F32
            )
            factor = lax.rsqrt(jnp.mean(value * value, axis=-1, keepdims=True) + EPSILON)
            n2[rows, :] = value * factor
            r2[rows, :] = factor
        emit(7, n2, n2_o).start()
        emit(8, r2, r2_o).start()

    acc[...] = jnp.zeros_like(acc)

    def multiply(p):
        k = chunk(p)

        @pl.when(k < N_NARROW)
        def _():
            for i in range(2):
                y_copy(k, i).wait_recv()

        tile = G[:, :, col(k)].reshape(512, W)
        down_copy(p).wait()
        acc[...] += lax.dot_general(tile, down_v[p % 4, :, 0:W], NT, preferred_element_type=F32)

        @pl.when(p + 4 < N_TOK)
        def _():
            down_copy(p + 4).start()

        @pl.when(p >= N_TOK - 4)
        def _():
            up_copy(p - (N_TOK - 4)).start()


    def x_arrive(h):
        for i in range(3):
            other = ((x + i + 1) % 4 * 2 + yh) * 2 + c
            other = flipped(other) if h else other
            for cp in w_copies(None, other, xs.at[h, 2 - i], xr.at[h, 2 - i], xp[2 - i]):
                cp.wait_recv()
            for cp in w_copies(None, other, cs.at[2 + 3 * h + i], cr.at[2 + 3 * h + i], core):
                cp.start()

    def z_send(k):
        def act(rows):
            for i in range(2):
                z_copy(k, i, rows).start()

        each(k, act)

    def z_forward(k):
        def act(rows):
            for i in range(2):
                z_copy(k, i, rows).wait_recv()
                on_copy(k, i, rows).start()

        each(k, act)

    def y_forward(k):
        def act(rows):
            for i in range(2):
                on_copy(k, i, rows).wait_recv()
            if rows == 64:
                for i in range(2):
                    y_copy(k, i).start()

        each(k, act)

    def gather_step(k, carry):
        @pl.when(k == N_NARROW - AHEAD)
        def _():
            o_copy(0).wait_recv()
            o_copy(1).wait_recv()

        @pl.when(k + AHEAD < N_TOK)
        def _():
            z_send(k + AHEAD)

        @pl.when(k < N_TOK)
        def _():
            z_forward(k)

        @pl.when(k == 2)
        def _():
            for zz in range(4):
                pre_copy(zz).start()

        @pl.when((k >= 2) & (k < N_TOK + 2))
        def _():
            y_forward(k - 2)

        @pl.when(k == 4)
        def _():
            for cp in w_copies((qw, ow), d2, ws.at[0], wr.at[0], p2):
                cp.wait_recv()
            for i in (0, 2, 1):
                for cp in w_copies(None, d2, xs.at[1, i], xr.at[1, i], xp[i]):
                    cp.start()
            for cp in w_copies(None, d2, cs.at[1], cr.at[1], core):
                cp.start()

        both = N_NARROW + 2

        @pl.when((k >= LAG) & (k <= N_TOK))
        def _():
            multiply(jnp.where(k < both, k - LAG, 2 * (k - both) + both - LAG))

        @pl.when(k >= both)
        def _():
            multiply(jnp.where(k > N_TOK, N_TOK - 1, 2 * (k - both) + both - LAG + 1))

        @pl.when(k < 4)
        def _():
            norm_step(k)

        @pl.when((k >= 10) & (k < 14))
        def _():
            slope_step(k - 10)

        @pl.when(k == 14)
        def _():
            x_arrive(0)

        return carry

    lax.fori_loop(0, N_TOK + 2, gather_step, 0)
    bias_step()

    pg[...] = (acc[...] * slope[...].reshape(512, slope.shape[2])).astype(BF16)
    combf = acc
    combf[...] = jnp.zeros_like(combf)

    token = dest[...]
    hot = (lax.broadcasted_iota(jnp.int32, (16, 64), 0) == token).astype(F32)
    before = (
        lax.broadcasted_iota(jnp.int32, (64, 64), 0) < lax.broadcasted_iota(jnp.int32, (64, 64), 1)
    ).astype(F32)
    rank = jnp.sum(jnp.dot(hot, before, preferred_element_type=F32) * hot, axis=0, keepdims=True)
    target = token * 16 + rank.astype(jnp.int32)
    row = lax.broadcasted_iota(jnp.int32, (256, 64), 0)
    placing = jnp.concatenate(
        [(row == target).astype(F32), (row == target + 8).astype(F32)], axis=1
    ).astype(BF16)

    def ry_copy(f, i):
        return remote(S.at[f, i], R.at[f, i], rys.at[f, i], ryr.at[f, i], (p1, p2)[i])

    def rz_copy(f, n):
        return z_parts(T, ZA, ZR, f, n, 64, rzs, rzr)

    def a_copy(j, s):
        dd = (d + s) % 16
        return remote(
            OUT.at[j, pl.ds(pl.multiple_of(dd * 16, 16), 16)],
            A.at[j, pl.ds(pl.multiple_of(d * 16, 16), 16)],
            as_.at[j],
            ar.at[j],
            dps[s - 1],
        )

    cidx = [d, d2]
    for h in range(2):
        for i in range(3):
            other = ((x + i + 1) % 4 * 2 + yh) * 2 + c
            cidx.append(flipped(other) if h else other)

    def weights_arrive():
        for n, index in enumerate(cidx):
            for cp in w_copies(None, index + 1 - 2 * c, cs.at[n], cr.at[n], core):
                cp.wait_recv()
        wo2[...] = wo[...].astype(F32).reshape(wo2.shape).astype(BF16)
        emit(1, wq, wq_o).start()
        emit(2, wo2, wo_o).start()

    def product(i):
        up_copy(i).wait()
        part = lax.dot_general(pg[...], down_v[i % 4, :, 0:V], NT, preferred_element_type=F32)

        @pl.when(i + 4 < N_FEAT)
        def _():
            up_copy(i + 4).start()

        return part.reshape(4, 128, V)

    def z_parts(T, ZA, ZR, f, n, rows, sends, recvs):
        low, high = pl.ds(0, rows // 2), pl.ds(rows // 2, rows // 2)
        source, target = (
            (T.at[f, 1, low], ZA.at[f, 0]),
            (T.at[f, 0, high], ZR.at[f, 0, high]),
            (T.at[f, 1, high], ZA.at[f, 1]),
            (T.at[f, 2, low], ZR.at[f, 1, low]),
            (T.at[f, 0, low], ZR.at[f, 0, low]),
            (T.at[f, 2, high], ZR.at[f, 1, high]),
        )[n]
        up = n in (0, 1, 4)
        return remote(source, target, sends.at[f, n], recvs.at[f, n], zp[0] if up else zp[2])

    def z_pass(copy, T, ZA, f, rows):
        half = rows // 2
        copy(f, 0).wait_recv()
        copy(f, 2).wait_recv()
        T[f, 0, 0:half] = (T[f, 0, 0:half].astype(F32) + ZA[f, 0].astype(F32)).astype(BF16)
        T[f, 2, half:rows] = (T[f, 2, half:rows].astype(F32) + ZA[f, 1].astype(F32)).astype(BF16)
        copy(f, 4).start()
        copy(f, 5).start()

    def q_copy(f, n):
        return z_parts(QS, QA, QR, f, n, 128, qs, qr)

    def z_product(f, carry):
        part = product(f)
        QS[f] = part[1:4].astype(BF16)
        for n in range(4):
            q_copy(f, n).start()
        Q0[f] = part[0]
        return carry

    def z_sum(f):
        for n in (1, 3, 4, 5):
            q_copy(f, n).wait_recv()
        total = Q0[f] + QR[f, 0].astype(F32) + QR[f, 1].astype(F32)
        S[f, 0, 0] = total[64:96].astype(BF16)
        S[f, 1, 0] = total[96:128].astype(BF16)
        Q0[f, 0:64] = total[0:64]
        for i in range(2):
            qy_copy(f, i).start()

    def qy_copy(f, i):
        return remote(S.at[f, i, 0], R.at[f, i, 0], rys.at[f, i], ryr.at[f, i], (p1, p2)[i])

    def z_end(f):
        for i in range(2):
            qy_copy(f, i).wait_recv()
        M[f] = (
            Q0[f, 0:64] + jnp.concatenate([R[f, 0, 0].astype(F32), R[f, 1, 0].astype(F32)], axis=0)
        ).astype(BF16)

    def y_product(f, carry):
        part = product(f)
        S[f, 0] = part[:, 64:96, :].astype(BF16)
        S[f, 1] = part[:, 96:128, :].astype(BF16)
        for h in range(2):
            ry_copy(f, h).start()
        own[f % 4] = part[:, 0:64, :]
        return carry

    def over_y(f):
        for h in range(2):
            ry_copy(f, h).wait_recv()
        total = own[f % 4] + jnp.concatenate([R[f, 0].astype(F32), R[f, 1].astype(F32)], axis=1)
        T[f] = total[1:4].astype(BF16)
        T0[f % 4] = total[0]
        for n in range(4):
            rz_copy(f, n).start()

    def over_z(f):
        for n in (1, 3, 4, 5):
            rz_copy(f, n).wait_recv()
        M[f] = (T0[f % 4] + ZR[f, 0].astype(F32) + ZR[f, 1].astype(F32)).astype(BF16)

    def send_rows(j):
        both = jnp.concatenate([M[2 * j], M[2 * j + 1]], axis=0)
        OUT[j] = jnp.dot(placing, both, preferred_element_type=F32).astype(BF16)
        for s in range(1, 16):
            a_copy(j, s).start()
        here = pl.ds(pl.multiple_of(d * 16, 16), 16)
        A[j, here, :] = OUT[j, here, :]

    lax.fori_loop(0, 2, z_product, 0)
    lax.fori_loop(2, 5, y_product, 0)
    x_arrive(1)

    def late_head(h, carry):
        head_step(h)
        return carry

    def sum_step(f, carry):
        over_y(f)

        @pl.when(f + 3 < N_FEAT)
        def _():
            y_product(f + 3, 0)

        @pl.when(f < 4)
        def _():
            z_pass(q_copy, QS, QA, f - 2, 128)

        @pl.when(f == 2)
        def _():
            weights_arrive()

        @pl.when((f == 3) | (f == 4))
        def _():
            z_sum(f - 3)

        @pl.when(f >= 3)
        def _():
            z_pass(rz_copy, T, ZA, f - 1, 64)

        @pl.when(f == 3)
        def _():
            lax.fori_loop(0, 3, qkv_step, 0)
            emit(4, proj, proj_o).start()

        @pl.when((f == 4) | (f == 5))
        def _():
            z_end(f - 4)
            head_step(f - 4)

        @pl.when(f == 5)
        def _():
            send_rows(jnp.int32(0))

        @pl.when(f >= 6)
        def _():
            lax.fori_loop(2 * f - 10, 2 * f - 8, late_head, 0)

        @pl.when(f >= 4)
        def _():
            over_z(f - 2)

        @pl.when((f == 5) | (f == 7))
        def _():
            send_rows((f - 3) // 2)

        return carry

    lax.fori_loop(2, N_FEAT, sum_step, 0)
    z_pass(rz_copy, T, ZA, N_FEAT - 1, 64)
    over_z(N_FEAT - 2)
    head_step(6)
    over_z(N_FEAT - 1)
    send_rows(3)
    head_step(7)
    emit(5, prob, prob_o).start()
    normt[...] = norm[...].astype(F32).T.astype(BF16)
    emit(3, normt, normt_o).start()
    output_step()

    fifteen = pl.ds(0, 240)
    for j in range(4):
        pltpu.make_async_copy(A.at[j, fifteen], A.at[j, fifteen], ar.at[j]).wait()
    out_row = lax.broadcasted_iota(jnp.int32, (128, 256), 0)
    in_row = lax.broadcasted_iota(jnp.int32, (128, 256), 1)
    wanted = (out_row % 4) * 64 + (out_row // 32) * 16 + (out_row // 4) % 8
    for h in range(2):
        order = (in_row == wanted + 8 * h).astype(F32).astype(BF16)
        for g in range(4):
            stacked = A[:, 64 * g : 64 * g + 64, :].reshape(256, V)
            cot[128 * g : 128 * g + 128, V * h : V * h + V] = jnp.dot(
                order, stacked, preferred_element_type=F32
            ).astype(BF16)
    emit(0, cot, cot_o).start()

    for n, index in enumerate(cidx):
        for cp in w_copies(None, index, cs.at[n], cr.at[n], core):
            cp.wait_send()
    for cp in w_copies((qw, ow), d, ws.at[0], wr.at[0], p2):
        cp.wait_send()
    for h in range(2):
        for i in range(3):
            for cp in w_copies(None, d2 if h else d, xs.at[h, i], xr.at[h, i], xp[i]):
                cp.wait_send()
    for zz in range(4):
        pre_copy(zz).wait_send()

    def drain(k, carry):
        def act(rows):
            for i in range(2):
                z_copy(k, i, rows).wait_send()
                on_copy(k, i, rows).wait_send()
                if rows == 64:
                    y_copy(k, i).wait_send()

        each(k, act)
        return carry

    lax.fori_loop(0, N_TOK, drain, 0)
    o_copy(0).wait_send()
    o_copy(1).wait_send()

    def drain2(f, carry):
        for i in range(2):
            ry_copy(f, i).wait_send()
        for n in range(6):
            rz_copy(f, n).wait_send()
        return carry

    lax.fori_loop(2, N_FEAT, drain2, 0)
    for f in range(2):
        for n in range(6):
            q_copy(f, n).wait_send()
        for i in range(2):
            qy_copy(f, i).wait_send()
    for j in range(4):
        pltpu.make_async_copy(OUT.at[j, fifteen], OUT.at[j, fifteen], as_.at[j]).wait()
    pairs = [
        (cot, cot_o), (wq, wq_o), (wo2, wo_o), (normt, normt_o), (proj, proj_o),
        (prob, prob_o), (combt, combt_o), (n2, n2_o), (r2, r2_o),
    ]
    for n, (source, target) in enumerate(pairs):
        emit(n, source, target).wait()


def merger(tok, dest, down, up, pre, qw, ow, xin, win, ng, mg):
    vm = pl.BlockSpec(memory_space=pltpu.VMEM)
    hbm = pl.BlockSpec(memory_space=pl.ANY)
    dma = pltpu.SemaphoreType.DMA
    hid = pre.shape[1]
    feat = up.shape[0]
    V = feat // N_FEAT
    kept = [
        ((512, 1280), BF16),
        ((16,) + qw.shape, BF16),
        ((640, 1280), BF16),
        ((1280, 512), BF16),
        ((3, 512, 640), BF16),
        ((8, 4, 128, 256), BF16),
        ((640, 512), BF16),
        ((512, 1280), F32),
        ((512, 1), F32),
    ]
    return pl.pallas_call(
        merger_kernel,
        name="merger",
        out_shape=tuple(jax.ShapeDtypeStruct(*k) for k in kept),
        in_specs=[hbm, vm, hbm, hbm, vm, vm, vm, vm, vm, vm, vm],
        out_specs=(hbm,) * len(kept),
        scratch_shapes=[
            pltpu.VMEM((4, 128, tok.shape[1]), BF16),
            pltpu.VMEM((4, 640, 640), BF16),
            pltpu.VMEM((4, 128, hid), F32),
            pltpu.VMEM((512, hid), F32),
            pltpu.VMEM((512, hid), BF16),
            pltpu.VMEM((128, hid), BF16),
            pltpu.VMEM((N_FEAT, 2, 4, 32, V), BF16),
            pltpu.VMEM((N_FEAT, 2, 4, 32, V), BF16),
            pltpu.VMEM((4, 4, 64, V), F32),
            pltpu.VMEM((N_FEAT, 3, 64, V), BF16),
            pltpu.VMEM((4, 64, V), F32),
            pltpu.VMEM((N_FEAT, 2, 32, V), BF16),
            pltpu.VMEM((N_FEAT, 2, 64, V), BF16),
            pltpu.VMEM((2, 3, 128, V), BF16),
            pltpu.VMEM((2, 2, 64, V), BF16),
            pltpu.VMEM((2, 2, 128, V), BF16),
            pltpu.VMEM((2, 128, V), F32),
            pltpu.VMEM((N_FEAT, 64, V), BF16),
            pltpu.VMEM((4, 256, V), BF16),
            pltpu.VMEM((4, 256, V), BF16),
            pltpu.VMEM((512, 1280), BF16),
            pltpu.VMEM((16,) + qw.shape, BF16),
            pltpu.VMEM((16,) + ow.shape, BF16),
            pltpu.VMEM((640, 1280), BF16),
            pltpu.VMEM((512, 1280), BF16),
            pltpu.VMEM((1280, 512), BF16),
            pltpu.VMEM((3, 512, 640), BF16),
            pltpu.VMEM((8, 4, 128, 256), BF16),
            pltpu.VMEM((640, 512), BF16),
            pltpu.VMEM((512, 1280), F32),
            pltpu.VMEM((512, 1), F32),
            pltpu.VMEM((4, 128, 256), F32),
            dma((1,)),
            dma((4,)),
            dma((2,)), dma((2,)),
            dma((9,)),
            dma((N_TOK, 2)), dma((N_TOK, 2)), dma((N_TOK, 2)), dma((N_TOK, 2)), dma((N_TOK, 2)), dma((N_TOK, 2)),
            dma((4,)), dma((4,)),
            dma((1, 2)), dma((1, 2)),
            dma((2, 3, 2)), dma((2, 3, 2)),
            dma((8, 2)), dma((8, 2)),
            dma((N_FEAT, 2)), dma((N_FEAT, 2)),
            dma((N_FEAT, 6)), dma((N_FEAT, 6)),
            dma((2, 6)), dma((2, 6)),
            dma((4,)), dma((4,)),
        ],
        compiler_params=pltpu.CompilerParams(
            collective_id=1, has_side_effects=True, vmem_limit_bytes=62 << 20
        ),
        cost_estimate=pl.CostEstimate(flops=9 * 10**9, bytes_accessed=40 * 10**6, transcendentals=0),
    )(tok, dest, down, up, pre, qw, ow, xin, win, ng, mg)


def block_kernel(
    cot_i, wq_i, wo_i, normt_i, proj_i, prob_i, combt_i, n2_i, r2_i, xin, ng, mg,
    lg, pout, oout,
    cot, wq, wo, normt, proj, prob, combt, n2, r2,
    db, dc, wof, DP, dpb,
    ga, Ca, Sa, XRa, E1, ZR2, Ea, YRa, Fa, FRa,
    gl, Cl, Zl, ZRl, El2, XRl, El, YRl, Fl, FRl,
    gc, Cc, Zc, ZRc, Ec2, XRc, Ec, YRc, Fc, FRc,
    gm, Cm, Sm, YRm, Em, XRm, Zm, Fm,
    gb, Cb, Sb, YRb, Eb, XRb, Zb, Fb,
    ins, cas, car, xas, xar, z2s, z2r, yas, yar, fas, far,
    cls, clr, zls, zlr, xls, xlr, yls, ylr, fls, flr,
    ccs, ccr, zcs, zcr, xcs, xcr, ycs, ycr, fcs, fcr,
    cms, cmr, yms, ymr, xms, xmr, zms, zmr, pms, pmr,
    cbs, cbr, ybs, ybr, xbs, xbr, zbs, zbr, pbs, pbr,
):
    x, yh, c, z, yl = place()
    pairs = [
        (cot_i, cot), (n2_i, n2), (r2_i, r2), (wo_i, wo), (combt_i, combt), (prob_i, prob), (proj_i, proj),
        (normt_i, normt), (wq_i, wq),
    ]
    loads = [pltpu.make_async_copy(a, b, ins.at[n]) for n, (a, b) in enumerate(pairs)]
    zp = [at(x, yh, c, (z + s) % 4, yl) for s in (1, 2, 3)]
    xp = [at((x + s) % 4, yh, c, z, yl) for s in (1, 2, 3)]
    core = at(x, yh, 1 - c, z, yl)
    p1 = at(x, yh, c, z, 1 - yl)
    p2 = at(x, 1 - yh, c, z, 1 - yl)
    yhp = at(x, 1 - yh, c, z, yl)

    greet(zp + xp + [core, p1, p2, yhp])
    for cp in loads[:3]:
        cp.start()

    def ca_copy(p):
        return remote(ga.at[p, :, 1 - c], Ca.at[p], cas.at[p], car.at[p], core)

    def xa_copy(p, i):
        return remote(
            Sa.at[p, pl.ds((x + i + 1) % 4 * 2, 2)], XRa.at[i, p], xas.at[p, i], xar.at[p, i], xp[i]
        )

    def summed_a(p):
        ca_copy(p).wait_recv()
        Sa[p] = (ga[p, :, c].astype(F32) + Ca[p].astype(F32)).astype(BF16)
        for i in (0, 2, 1):
            xa_copy(p, i).start()

    def z2_copy(i):
        t = (z + i + 1) % 4
        return remote(E1.at[t // 2, t % 2], ZR2.at[i], z2s.at[i], z2r.at[i], zp[i])

    def y_first(g, C, S, YR, E, XR, ZZ, F, cs, cr, ys, yr, xs, xr, zs, zr, ps, pr):
        def c_copy(p):
            return remote(g.at[p, :, 1 - c], C.at[p], cs.at[p], cr.at[p], core)

        def y_copy(i):
            return remote(
                S.at[(1 - yl, 1 - yl, yl)[i], (yh, 1 - yh, 1 - yh)[i]],
                YR.at[i],
                ys.at[i],
                yr.at[i],
                (p1, p2, yhp)[i],
            )

        def x_copy(i):
            return remote(E.at[(x + i + 1) % 4], XR.at[i], xs.at[i], xr.at[i], xp[i])

        def z_copy(i):
            return remote(ZZ.at[z], ZZ.at[z], zs.at[i], zr.at[i], zp[i])

        def p_copy():
            return remote(F.at[yl], F.at[yl], ps.at[0], pr.at[0], p1)

        def add_cores(p):
            c_copy(p).wait_recv()
            total = (g[p, :, c].astype(F32) + C[p].astype(F32)).astype(BF16)
            total = total.reshape((4, 2) + total.shape[1:])
            S[p, 0] = total[:, 0]
            S[p, 1] = total[:, 1]

        def start_y():
            for i in range(3):
                y_copy(i).start()

        def add_y():
            for i in range(3):
                y_copy(i).wait_recv()
            mine = S[yl, yh].astype(F32)
            for i in range(3):
                mine = mine + YR[i].astype(F32)
            E[...] = mine.astype(BF16)
            for i in (0, 2, 1):
                x_copy(i).start()

        def add_x():
            for i in range(3):
                x_copy(i).wait_recv()
            mine = E[x].astype(F32)
            for i in range(3):
                mine = mine + XR[i].astype(F32)
            ZZ[z] = mine.astype(BF16)
            for i in (0, 2, 1):
                z_copy(i).start()

        def add_z():
            for i in range(3):
                there = (z + 3 - i) % 4
                pltpu.make_async_copy(ZZ.at[there], ZZ.at[there], zr.at[i]).wait()
            total = (ZZ[0].astype(F32) + ZZ[1].astype(F32)) + (ZZ[2].astype(F32) + ZZ[3].astype(F32))
            F[yl] = (total * (1.0 / 128.0)).astype(BF16)
            p_copy().start()

        def finish():
            other = 1 - yl
            pltpu.make_async_copy(F.at[other], F.at[other], pr.at[0]).wait()

        def drain():
            p_copy().wait_send()
            for p in range(2):
                c_copy(p).wait_send()
            for i in range(3):
                y_copy(i).wait_send()
                x_copy(i).wait_send()
                z_copy(i).wait_send()

        return c_copy, add_cores, start_y, add_y, add_x, add_z, finish, drain

    m_core, m_cores, m_start, m_y, m_x, m_z, m_finish, m_drain = y_first(
        gm, Cm, Sm, YRm, Em, XRm, Zm, Fm, cms, cmr, yms, ymr, xms, xmr, zms, zmr, pms, pmr
    )
    b_core, b_cores, b_start, b_y, b_x, b_z, b_finish, b_drain = y_first(
        gb, Cb, Sb, YRb, Eb, XRb, Zb, Fb, cbs, cbr, ybs, ybr, xbs, xbr, zbs, zbr, pbs, pbr
    )

    owner = yh == z // 2

    def y_copy(i, e, yr, s_sem, r_sem):
        return remote(e, yr.at[i], s_sem.at[i], r_sem.at[i], (p1, p2, yhp)[i])

    def f_copy(i, f, fr, s_sem, r_sem):
        return remote(f, fr.at[z % 2], s_sem.at[i], r_sem.at[z % 2], zp[i])

    def owners_send(e, yr, s_sem, r_sem):
        @pl.when(owner)
        def _():
            y_copy(0, e, yr, s_sem, r_sem).start()

        @pl.when(jnp.logical_not(owner))
        def _():
            for i in (1, 2):
                y_copy(i, e, yr, s_sem, r_sem).start()

    def owners_sum(e, yr, s_sem, r_sem, f, fr, fs_sem, fr_sem):
        @pl.when(owner)
        def _():
            for i in range(3):
                y_copy(i, e, yr, s_sem, r_sem).wait_recv()
            total = (e[...].astype(F32) + yr[0].astype(F32)) + (yr[1].astype(F32) + yr[2].astype(F32))
            f[...] = (total * (1.0 / 128.0)).astype(BF16)
            for i in (0, 2, 1):
                f_copy(i, f, fr, fs_sem, fr_sem).start()
            fr[z % 2] = f[...]

    def owners_end(e, yr, s_sem, r_sem, f, fr, fs_sem, fr_sem):
        @pl.when(owner)
        def _():
            y_copy(0, e, yr, s_sem, r_sem).wait_send()
            there = 1 - z % 2
            pltpu.make_async_copy(fr.at[there], fr.at[there], fr_sem.at[there]).wait()
            for i in range(3):
                f_copy(i, f, fr, fs_sem, fr_sem).wait_send()

        @pl.when(jnp.logical_not(owner))
        def _():
            for i in (1, 2):
                y_copy(i, e, yr, s_sem, r_sem).wait_send()
            for there in range(2):
                pltpu.make_async_copy(fr.at[there], fr.at[there], fr_sem.at[there]).wait()

    def z_first(g, C, Z, ZR, E2, XR, E, YR, F, FR, cs, cr, zs, zr, xs, xr, ys, yr, fs, fr):
        def c_copy(p):
            return remote(g.at[p, :, 1 - c], C.at[p], cs.at[p], cr.at[p], core)

        def z_copy(i):
            t = (z + i + 1) % 4
            return remote(Z.at[t % 2, t // 2], ZR.at[i], zs.at[i], zr.at[i], zp[i])

        def x_copy(i):
            return remote(E2.at[(x + i + 1) % 4], XR.at[i], xs.at[i], xr.at[i], xp[i])

        def add_cores(p):
            c_copy(p).wait_recv()
            total = (g[p, :, c].astype(F32) + C[p].astype(F32)).astype(BF16)
            total = total.reshape((4, 2) + total.shape[1:])
            Z[p, 0] = total[:, 0]
            Z[p, 1] = total[:, 1]
            for i in (0, 2, 1):

                @pl.when((z + i + 1) % 2 == p)
                def _():
                    z_copy(i).start()

        def add_z():
            for i in range(3):
                z_copy(i).wait_recv()
            mine = Z[z % 2, z // 2].astype(F32)
            for i in range(3):
                mine = mine + ZR[i].astype(F32)
            E2[...] = mine.astype(BF16)
            for i in (0, 2, 1):
                x_copy(i).start()

        def add_x():
            for i in range(3):
                x_copy(i).wait_recv()
            mine = E2[x].astype(F32)
            for i in range(3):
                mine = mine + XR[i].astype(F32)
            E[...] = mine.astype(BF16)
            owners_send(E, YR, ys, yr)

        def add_y():
            owners_sum(E, YR, ys, yr, F, FR, fs, fr)

        def finish():
            owners_end(E, YR, ys, yr, F, FR, fs, fr)

        def drain():
            for p in range(2):
                c_copy(p).wait_send()
            for i in range(3):
                z_copy(i).wait_send()
                x_copy(i).wait_send()

        return c_copy, add_cores, add_z, add_x, add_y, finish, drain

    l_core, l_cores, l_z, l_x, l_y, l_finish, l_drain = z_first(
        gl, Cl, Zl, ZRl, El2, XRl, El, YRl, Fl, FRl, cls, clr, zls, zlr, xls, xlr, yls, ylr, fls, flr
    )
    c_core, c_cores, c_z, c_x, c_y, c_finish, c_drain = z_first(
        gc, Cc, Zc, ZRc, Ec2, XRc, Ec, YRc, Fc, FRc, ccs, ccr, zcs, zcr, xcs, xcr, ycs, ycr, fcs, fcr
    )
    last_a = (Ea, YRa, yas, yar)
    more_a = (Fa, FRa, fas, far)

    loads[0].wait()
    loads[1].wait()
    loads[2].wait()
    for cp in loads[3:]:
        cp.start()

    def out_step(t, carry):
        rows = pl.ds(pl.multiple_of(t * 128, 128), 128)
        slope = cot[rows, :].astype(F32) * mg[...].reshape(1, 1280)
        unit = n2[rows, :]
        grad = r2[rows, :] * (slope - unit * jnp.mean(slope * unit, axis=-1, keepdims=True))
        n2[rows, :] = grad
        db[rows, :] = grad.astype(BF16)
        return carry

    lax.fori_loop(0, 4, out_step, 0)
    loads[3].wait()
    dc[...] = lax.dot_general(db[...], wo[...], NT, preferred_element_type=F32).astype(BF16)
    loads[4].wait()

    def wo_step(t, carry):
        cols = pl.ds(pl.multiple_of(t * 640, 128), 640)
        wof[t] = jnp.dot(combt[...], db[:, cols], preferred_element_type=F32)
        return carry

    lax.fori_loop(0, 2, wo_step, 0)
    grad_o = (
        jnp.concatenate([wof[0].reshape(16, 40, 640), wof[1].reshape(16, 40, 640)], axis=1)
        .astype(BF16)
        .reshape(8, 2, 80, 640)
    )
    gl[1] = grad_o[..., :N_LEFT]
    gm[1] = grad_o[..., N_LEFT:]
    met(zp + xp + [core, p1, p2, yhp])
    l_core(1).start()
    m_core(1).start()

    DP[...] = jnp.zeros_like(DP)
    loads[5].wait()

    def value_step(h, carry):
        lanes, mask = head_lanes(h)
        parts = [
            lax.dot_general(
                prob[h, b], dc[pl.ds(128 * b, 128), lanes] * mask, TN, preferred_element_type=F32
            )
            for b in range(4)
        ]
        DP[2, :, lanes] += overlap(parts)
        return carry

    lax.fori_loop(0, 8, value_step, 0)
    loads[7].wait()
    def part_grad(p, first, width):
        cols = slice(first, first + width)
        dpb[p, :, cols] = DP[p, :, cols].astype(BF16)
        grad = jnp.dot(normt[...], dpb[p, :, cols], preferred_element_type=F32)
        return grad.astype(BF16).reshape(8, 2, 80, width)

    gl[0] = part_grad(2, 0, N_LEFT)
    l_core(0).start()
    gm[0] = part_grad(2, N_LEFT, 640 - N_LEFT)
    m_core(0).start()
    l_cores(1)
    m_cores(1)
    loads[6].wait()

    def head_step(h, carry):
        lanes, mask = head_lanes(h)
        slopes = []
        for b in range(4):
            grad = dc[pl.ds(128 * b, 128), lanes] * mask
            wide = prob[h, b].astype(F32)
            slope = lax.dot_general(
                grad, proj[2, pl.ds(KEYS[b], 256), lanes], NT, preferred_element_type=F32
            )
            slope = wide * (slope - jnp.sum(slope * wide, axis=-1, keepdims=True)) * HEAD_DIM ** (-0.5)
            slopes.append(slope.astype(BF16))
        parts = [
            jnp.dot(slopes[b], proj[1, pl.ds(KEYS[b], 256), lanes] * mask, preferred_element_type=F32)
            for b in range(4)
        ]
        DP[0, :, lanes] += jnp.concatenate(parts, axis=0)
        parts = [
            lax.dot_general(
                slopes[b], proj[0, pl.ds(128 * b, 128), lanes] * mask, TN, preferred_element_type=F32
            )
            for b in range(4)
        ]
        DP[1, :, lanes] += overlap(parts)

        @pl.when(h == 0)
        def _():
            l_cores(0)
            m_cores(0)
            m_start()

        @pl.when(h == 3)
        def _():
            for p in range(2):
                ga[p] = part_grad(p, 0, N_X)
                ca_copy(p).start()

        @pl.when(h == 5)
        def _():
            summed_a(0)
            summed_a(1)

        @pl.when(h == 6)
        def _():
            for p in range(2):
                gc[p] = part_grad(p, N_X, N_Z)
                c_core(p).start()

        return carry

    lax.fori_loop(0, 8, head_step, 0)
    for p in range(2):
        gb[p] = part_grad(p, N_X + N_Z, 640 - N_X - N_Z)
        b_core(p).start()
    m_y()
    c_cores(0)
    c_cores(1)

    def input_dot(half):
        total = jnp.zeros((512, 640), F32)
        for p in range(3):
            total += lax.dot_general(
                dpb[p],
                wq[8 * half : 8 * half + 8, :, 640 * p : 640 * p + 640].reshape(640, 640),
                NT,
                preferred_element_type=F32,
            )
        wof[half, 0:512, :] = total

    loads[8].wait()
    input_dot(0)
    b_cores(0)
    b_cores(1)
    b_start()
    l_z()

    for p in range(2):
        for i in range(3):
            xa_copy(p, i).wait_recv()
        mine = Sa[p, pl.ds(2 * x, 2)].astype(F32)
        for i in range(3):
            mine = mine + XRa[i, p].astype(F32)
        E1[0, p] = mine[0].astype(BF16)
        E1[1, p] = mine[1].astype(BF16)
    for i in (0, 2, 1):
        z2_copy(i).start()
    input_dot(1)
    m_x()
    l_x()

    def input_step(t, carry):
        rows = pl.ds(pl.multiple_of(t * 128, 128), 128)
        slope = jnp.concatenate([wof[0, rows, :], wof[1, rows, :]], axis=1)
        slope = slope.astype(BF16).astype(F32) * ng[...].reshape(1, 1280)
        value = xin[rows, :].astype(F32)
        factor = lax.rsqrt(jnp.mean(value * value, axis=-1, keepdims=True) + EPSILON)
        unit = value * factor
        grad = factor * (slope - unit * jnp.mean(slope * unit, axis=-1, keepdims=True))
        lg[rows, :] = (grad + n2[rows, :]).astype(BF16)
        return carry

    lax.fori_loop(0, 4, input_step, 0)

    c_z()
    b_y()
    for i in range(3):
        z2_copy(i).wait_recv()
    mine = E1[z // 2, z % 2].astype(F32)
    for i in range(3):
        mine = mine + ZR2[i].astype(F32)
    Ea[...] = mine.astype(BF16)
    owners_send(*last_a)
    m_z()
    l_y()
    b_x()
    c_x()
    owners_sum(*last_a, *more_a)
    b_z()
    c_y()

    m_finish()
    l_finish()
    pout[:, 1280 : 1280 + N_LEFT] = FRl[0].astype(F32)
    pout[:, 1280 + N_LEFT : 1920] = Fm[0].astype(F32)
    left, right = FRl[1].astype(F32), Fm[1].astype(F32)
    oout[:, 0:N_LEFT] = left[0:40]
    oout[:, N_LEFT:640] = right[0:40]
    oout[:, 640 : 640 + N_LEFT] = left[40:80]
    oout[:, 640 + N_LEFT : 1280] = right[40:80]
    owners_end(*last_a, *more_a)
    c_finish()
    b_finish()
    for p in range(2):
        first = 640 * p
        pout[:, first : first + N_X] = FRa[p].astype(F32)
        pout[:, first + N_X : first + N_X + N_Z] = FRc[p].astype(F32)
        pout[:, first + N_X + N_Z : first + 640] = Fb[p].astype(F32)

    for drain in (m_drain, b_drain, l_drain, c_drain):
        drain()
    for p in range(2):
        ca_copy(p).wait_send()
        for i in range(3):
            xa_copy(p, i).wait_send()
    for i in range(3):
        z2_copy(i).wait_send()


def block_grads(cot, wq, wo, normt, proj, prob, combt, n2, r2, xin, ng, mg):
    vm = pl.BlockSpec(memory_space=pltpu.VMEM)
    hbm = pl.BlockSpec(memory_space=pl.ANY)
    dma = pltpu.SemaphoreType.DMA
    tl, tm = (80, N_LEFT), (80, 640 - N_LEFT)
    ta, tc, tb = (80, N_X), (80, N_Z), (80, 640 - N_X - N_Z)
    held = (cot, wq, wo, normt, proj, prob, combt, n2, r2)
    return pl.pallas_call(
        block_kernel,
        name="block",
        out_shape=(
            jax.ShapeDtypeStruct((512, 1280), BF16),
            jax.ShapeDtypeStruct((80, 1920), F32),
            jax.ShapeDtypeStruct((40, 1280), F32),
        ),
        in_specs=[hbm] * 9 + [vm] * 3,
        out_specs=(vm, vm, vm),
        scratch_shapes=[pltpu.VMEM(k.shape, k.dtype) for k in held]
        + [
            pltpu.VMEM((512, 1280), BF16),
            pltpu.VMEM((512, 640), BF16),
            pltpu.VMEM((2, 640, 640), F32),
            pltpu.VMEM((3, 512, 640), F32),
            pltpu.VMEM((3, 512, 640), BF16),
            pltpu.VMEM((2, 8, 2) + ta, BF16),
            pltpu.VMEM((2, 8) + ta, BF16),
            pltpu.VMEM((2, 8) + ta, BF16),
            pltpu.VMEM((3, 2, 2) + ta, BF16),
            pltpu.VMEM((2, 2) + ta, BF16),
            pltpu.VMEM((3,) + ta, BF16),
            pltpu.VMEM(ta, BF16),
            pltpu.VMEM((3,) + ta, BF16),
            pltpu.VMEM(ta, BF16),
            pltpu.VMEM((2,) + ta, BF16),
        ]
        + [
            pltpu.VMEM(lead + t, BF16)
            for t in (tl, tc)
            for lead in ((2, 8, 2), (2, 8), (2, 2, 4), (3, 4), (4,), (3,), (), (3,), (), (2,))
        ]
        + [
            pltpu.VMEM(lead + t, BF16)
            for t in (tm, tb)
            for lead in ((2, 8, 2), (2, 8), (2, 2, 4), (3, 4), (4,), (3,), (4,), (2,))
        ]
        + [dma((9,))]
        + [
            dma(n)
            for n in ((2,), (2,), (2, 3), (2, 3), (3,), (3,), (3,), (3,), (3,), (2,))
        ]
        + [dma((n,)) for n in (2, 2, 3, 3, 3, 3, 3, 3, 3, 2) * 2]
        + [dma((n,)) for n in (2, 2, 3, 3, 3, 3, 3, 3, 1, 1) * 2],
        compiler_params=pltpu.CompilerParams(
            collective_id=2, has_side_effects=True, vmem_limit_bytes=62 << 20
        ),
        cost_estimate=pl.CostEstimate(flops=8 * 10**9, bytes_accessed=40 * 10**6, transcendentals=0),
    )(cot, wq, wo, normt, proj, prob, combt, n2, r2, xin, ng, mg)


def finish_kernel(a, b, c, out_a, out_b, out_c):
    out_a[...] = a[...]
    out_b[...] = b[...]
    out_c[...] = c[...]


def finish(*arrays):
    vm = pl.BlockSpec(memory_space=pltpu.VMEM)
    return pl.pallas_call(
        finish_kernel,
        name="finish",
        out_shape=tuple(jax.ShapeDtypeStruct(k.shape, k.dtype) for k in arrays),
        in_specs=[vm] * 3,
        out_specs=(vm,) * 3,
    )(*arrays)


def local(
    token_grads,
    token_dest,
    merger_down,
    merger_up,
    merger_pre,
    layer_input,
    window_ids,
    norm_gain,
    merge_gain,
    qkv_weight,
    proj_weight,
):
    kept = merger(
        token_grads, token_dest.reshape(1, 64), merger_down, merger_up, merger_pre, qkv_weight, proj_weight,
        layer_input, window_ids, norm_gain, merge_gain,
    )
    return finish(*block_grads(*kept, layer_input, norm_gain, merge_gain))


def solution(mesh):
    return jax.shard_map(
        local,
        mesh=mesh,
        in_specs=(
            P(("dp", "llm"), None),
            P(("dp", "llm"), None),
            P("llm", None),
            P(None, "llm"),
            P("dp", "llm"),
            P(("dp", "llm"), None),
            P(("dp", "llm"), None),
            P(),
            P(),
            P("dp", None),
            P("dp", None),
        ),
        out_specs=(P(("dp", "llm"), None), P("dp", None), P("dp", None)),
        check_vma=False,
    )
```

```python
import jax
import jax.numpy as jnp
from jax import lax
from jax.experimental import pallas as pl
from jax.experimental.pallas import tpu as pltpu
from jax.sharding import PartitionSpec as P

MESH = pl.DeviceIdType.MESH
HEAD_DIM = 80
CAP = 8
EPSILON = 1e-06
BF16 = jnp.bfloat16
F32 = jnp.float32

NT = (((1,), (1,)), ((), ()))
TN = (((0,), (0,)), ((), ()))

N_TOK = 16
N_NARROW = 10
N_LEFT = 384
N_X, N_Z = 256, 256
AHEAD = 3
LAG = 7
N_FEAT = 8


def gelu_slope(values):
    return (
        0.5 * (1.0 + lax.erf(values * 0.7071067811865476))
        + values * jnp.exp(-0.5 * values * values) * 0.3989422804014327
    )


def rms_scale(values, scaling):
    return values * lax.rsqrt(jnp.mean(values * values, axis=-1, keepdims=True) + EPSILON) * scaling


KEYS = (0, 64, 192, 256)


def head_lanes(h):
    start = 128 * jnp.minimum(5 * h // 8, 3)
    lane = lax.broadcasted_iota(jnp.int32, (1, 256), 1) + start
    mask = ((lane >= HEAD_DIM * h) & (lane < HEAD_DIM * h + HEAD_DIM)).astype(F32).astype(BF16)
    return pl.ds(pl.multiple_of(start, 128), 256), mask


def overlap(parts):
    a, b, c, d = parts
    return jnp.concatenate(
        [
            a[0:64],
            a[64:192] + b[0:128],
            a[192:256] + b[128:192] + c[0:64],
            b[192:256] + c[64:128] + d[0:64],
            c[128:256] + d[64:192],
            d[192:256],
        ],
        axis=0,
    )


def place():
    d, l = lax.axis_index("dp"), lax.axis_index("llm")
    return d // 4, (d // 2) % 2, d % 2, l // 2, l % 2


def at(x, yh, c, z, yl):
    return (x * 2 + yh) * 2 + c, z * 2 + yl


def remote(src, dst, send, recv, device):
    return pltpu.make_async_remote_copy(
        src_ref=src, dst_ref=dst, send_sem=send, recv_sem=recv, device_id=device, device_id_type=MESH
    )


def settle(ref, sem):
    pltpu.make_async_copy(ref, ref, sem).wait()


def greet(devices):
    barrier = pltpu.get_barrier_semaphore()
    for device in devices:
        pl.semaphore_signal(barrier, inc=1, device_id=device, device_id_type=MESH)


def met(devices):
    pl.semaphore_wait(pltpu.get_barrier_semaphore(), len(devices))


def merger_kernel(
    tok, dest, down, up, pre, qw, ow, xin, win, ng, mg,
    cot_o, wq_o, wo_o, normt_o, proj_o, prob_o, combt_o, n2_o, r2_o,
    G, down_v, slope, acc, pg, pre2,
    S, R, own, T, T0, ZA, ZR, QS, QA, QR, Q0, M, OUT, A,
    cot, wq, wo, wo2, norm, normt, proj, prob, combt, n2, r2, bias,
    loc, dsem, os_, or_, outs, zs, zr, ns, nr, ys, yr, ps, pr, ws, wr, xs, xr, cs, cr, rys, qys, ryr, rzs, rzr, qs, qr, as_, ar,
):
    x, yh, c, z, yl = place()
    d = (x * 2 + yh) * 2 + c
    l = z * 2 + yl
    zp = [at(x, yh, c, (z + s) % 4, yl) for s in (1, 2, 3)]
    p1 = at(x, yh, c, z, 1 - yl)
    p2 = at(x, 1 - yh, c, z, 1 - yl)
    yhp = at(x, 1 - yh, c, z, yl)
    xp = [at((x + s) % 4, yh, c, z, yl) for s in (1, 2, 3)]
    core = at(x, yh, 1 - c, z, yl)
    dps = [((d + s) % 16, l) for s in range(1, 16)]

    cp_tok = pltpu.make_async_copy(tok, G.at[0, pl.ds(0, 64)], loc.at[0])
    cp_tok.start()
    greet(zp + [p1, p2] + dps)
    met(zp + [p1, p2] + dps)
    cp_tok.wait()

    W = G.shape[2] // N_TOK

    def col(k):
        return pl.ds(pl.multiple_of(k * W, W), W)

    def chunk(p):
        turn = N_NARROW - LAG + 2
        return jnp.where(
            p < turn, p, jnp.where((p - turn) % 2 == 0, N_NARROW + (p - turn) // 2, turn + (p - turn) // 2)
        )

    def down_copy(p):
        return pltpu.make_async_copy(
            down.at[:, col(chunk(p))], down_v.at[p % 4, :, pl.ds(0, W)], dsem.at[p % 4]
        )

    for k in range(4):
        down_copy(jnp.int32(k)).start()
    V = M.shape[2]

    def up_copy(f):
        rows = pl.ds(pl.multiple_of(f * V, V), V)
        return pltpu.make_async_copy(up.at[rows], down_v.at[f % 4, :, pl.ds(0, V)], dsem.at[f % 4])

    def z_copy(k, i, rows):
        return remote(
            G.at[0, pl.ds(0, rows), col(k)],
            G.at[(3, 1)[i], pl.ds(0, rows), col(k)],
            zs.at[rows // 128, i],
            zr.at[k],
            (zp[0], zp[2])[i],
        )

    def on_copy(k, i, rows):
        half = pl.ds(pl.multiple_of(k * W + i * (W // 2), W // 2), W // 2)
        return remote(
            G.at[(3, 1)[i], pl.ds(0, rows), half],
            G.at[2, pl.ds(0, rows), half],
            ns.at[rows // 128, i],
            nr.at[k],
            (zp[0], zp[2])[i],
        )

    def each(k, act):
        @pl.when(k < N_NARROW)
        def _():
            act(64)

        @pl.when(k >= N_NARROW)
        def _():
            act(128)

    def y_copy(k, i):
        return remote(
            G.at[:, pl.ds(32 * i, 32), col(k)],
            G.at[:, pl.ds(64 + 32 * i, 32), col(k)],
            ys.at[i],
            yr.at[k],
            (p1, p2)[i],
        )

    def o_copy(i):
        wide = pl.ds(N_NARROW * W, (N_TOK - N_NARROW) * W)
        return remote(
            G.at[0, pl.ds(32 * i, 32), wide],
            G.at[0, pl.ds(64 + 32 * i, 32), wide],
            os_.at[i],
            or_.at[i],
            (p1, p2)[i],
        )

    o_copy(0).start()
    for k in range(AHEAD):
        for i in range(2):
            z_copy(k, i, 64).start()

    def pre_copy(zz):
        rows = pl.ds(pl.multiple_of((2 * zz + 1 - yl) * 64 + 32, 32), 32)
        return remote(pre.at[rows], pre2.at[pl.ds(32 * zz, 32)], ps.at[0], pr.at[0], yhp)

    def w_copies(source, index, sends, recvs, device):
        first = wq.at[index] if source is None else source[0]
        second = wo.at[index] if source is None else source[1]
        return [
            remote(first, wq.at[index], sends.at[0], recvs.at[0], device),
            remote(second, wo.at[index], sends.at[1], recvs.at[1], device),
        ]

    def flipped(dd):
        return dd + 2 - 4 * ((dd // 2) % 2)

    wq[d] = qw[...]
    wo[d] = ow[...]
    d2 = flipped(d)
    for cp in w_copies((qw, ow), d, ws.at[0], wr.at[0], p2):
        cp.start()
    o_copy(1).start()
    for i in (0, 2, 1):
        for cp in w_copies((qw, ow), d, xs, xr.at[0], xp[i]):
            cp.start()
    for cp in w_copies((qw, ow), d, cs, cr, core):
        cp.start()
    def emit(n, source, target):
        return pltpu.make_async_copy(source, target, outs.at[n])

    def slope_step(r):
        @pl.when(r == 0)
        def _():
            settle(pre2, pr.at[0])

        zz = (z + r) % 4
        mine = pre[pl.ds(pl.multiple_of((2 * zz + yl) * 64, 64), 64), :]
        slope[r, 0:64, :] = gelu_slope(mine.astype(F32))
        first = pre[pl.ds(pl.multiple_of((2 * zz + 1 - yl) * 64, 64), 32), :]
        second = pre2[pl.ds(pl.multiple_of(zz * 32, 32), 32), :]
        slope[r, 64:96, :] = gelu_slope(first.astype(F32))
        slope[r, 96:128, :] = gelu_slope(second.astype(F32))

    def norm_step(k):
        rows = pl.ds(pl.multiple_of(k * 128, 128), 128)
        norm[rows, :] = rms_scale(xin[rows, :].astype(F32), ng[...].reshape(1, 1280)).astype(BF16)

    def bias_step():
        for b in range(4):
            queries = jnp.broadcast_to(win[:, 128 * b : 128 * b + 128].astype(F32), (128, 128)).T
            for h in range(2):
                keys = win[:, KEYS[b] + 128 * h : KEYS[b] + 128 * h + 128].astype(F32)
                bias[b, :, 128 * h : 128 * h + 128] = jnp.where(queries == keys, 0.0, -1e30)

    def qkv_step(p, carry):
        cols = pl.ds(pl.multiple_of(p * 640, 128), 640)
        weight = wq[:, :, cols].reshape(1280, 640)
        proj[p] = jnp.dot(norm[...], weight, preferred_element_type=F32).astype(BF16)
        return carry

    def head_step(h):
        lanes, mask = head_lanes(h)
        shares = []
        for b in range(4):
            scores = lax.dot_general(
                proj[0, pl.ds(128 * b, 128), lanes] * mask,
                proj[1, pl.ds(KEYS[b], 256), lanes],
                NT,
                preferred_element_type=F32,
            )
            scores = scores * HEAD_DIM ** (-0.5) + bias[b]
            powers = jnp.exp(scores - jnp.max(scores, axis=-1, keepdims=True))
            shares.append((powers * (1.0 / jnp.sum(powers, axis=-1, keepdims=True))).astype(BF16))
        parts = [
            jnp.dot(shares[b], proj[2, pl.ds(KEYS[b], 256), lanes] * mask, preferred_element_type=F32)
            for b in range(4)
        ]
        for b in range(4):
            prob[h, b] = shares[b]
        combf[:, lanes] += jnp.concatenate(parts, axis=0)

    def output_step():
        comb = combf[...].astype(BF16)
        combt[...] = combf[...].T.astype(BF16)
        emit(6, combt, combt_o).start()
        for t in range(4):
            rows = pl.ds(128 * t, 128)
            value = xin[rows, :].astype(F32) + jnp.dot(
                comb[128 * t : 128 * t + 128], wo2[...], preferred_element_type=F32
            )
            factor = lax.rsqrt(jnp.mean(value * value, axis=-1, keepdims=True) + EPSILON)
            n2[rows, :] = value * factor
            r2[rows, :] = factor
        emit(7, n2, n2_o).start()
        emit(8, r2, r2_o).start()

    acc[...] = jnp.zeros_like(acc)

    def multiply(p):
        k = chunk(p)

        @pl.when(k < N_NARROW)
        def _():
            settle(G.at[:, pl.ds(64, 64), col(k)], yr.at[k])

        tile = G[:, :, col(k)].reshape(512, W)
        down_copy(p).wait()
        acc[...] += lax.dot_general(tile, down_v[p % 4, :, 0:W], NT, preferred_element_type=F32)

        @pl.when(p + 4 < N_TOK)
        def _():
            down_copy(p + 4).start()

        @pl.when(p >= N_TOK - 4)
        def _():
            up_copy(p - (N_TOK - 4)).start()


    def x_arrive(h):
        settle(wq.at[pl.ds(0, 3)], xr.at[h, 0])
        settle(wo.at[pl.ds(0, 3)], xr.at[h, 1])
        for i in range(3):
            other = ((x + i + 1) % 4 * 2 + yh) * 2 + c
            other = flipped(other) if h else other
            for cp in w_copies(None, other, cs, cr, core):
                cp.start()

    def z_send(k):
        def act(rows):
            for i in range(2):
                z_copy(k, i, rows).start()

        each(k, act)

    def z_forward(k):
        def act(rows):
            settle(G.at[pl.ds(0, 2), pl.ds(0, rows), col(k)], zr.at[k])
            for i in range(2):
                on_copy(k, i, rows).start()

        each(k, act)

    def y_forward(k):
        def act(rows):
            settle(G.at[2, pl.ds(0, rows), col(k)], nr.at[k])
            if rows == 64:
                for i in range(2):
                    y_copy(k, i).start()

        each(k, act)

    def gather_step(k, carry):
        @pl.when(k == N_NARROW - AHEAD)
        def _():
            o_copy(0).wait_recv()
            o_copy(1).wait_recv()

        @pl.when(k + AHEAD < N_TOK)
        def _():
            z_send(k + AHEAD)

        @pl.when(k < N_TOK)
        def _():
            z_forward(k)

        @pl.when(k == 2)
        def _():
            for zz in range(4):
                pre_copy(zz).start()

        @pl.when((k >= 2) & (k < N_TOK + 2))
        def _():
            y_forward(k - 2)

        @pl.when(k == 4)
        def _():
            for cp in w_copies((qw, ow), d2, ws.at[0], wr.at[0], p2):
                cp.wait_recv()
            for i in (0, 2, 1):
                for cp in w_copies(None, d2, xs, xr.at[1], xp[i]):
                    cp.start()
            for cp in w_copies(None, d2, cs, cr, core):
                cp.start()

        both = N_NARROW + 2

        @pl.when((k >= LAG) & (k <= N_TOK))
        def _():
            multiply(jnp.where(k < both, k - LAG, 2 * (k - both) + both - LAG))

        @pl.when(k >= both)
        def _():
            multiply(jnp.where(k > N_TOK, N_TOK - 1, 2 * (k - both) + both - LAG + 1))

        @pl.when(k < 4)
        def _():
            norm_step(k)

        @pl.when((k >= 10) & (k < 14))
        def _():
            slope_step(k - 10)

        @pl.when(k == 14)
        def _():
            x_arrive(0)

        return carry

    lax.fori_loop(0, N_TOK + 2, gather_step, 0)
    bias_step()

    pg[...] = (acc[...] * slope[...].reshape(512, slope.shape[2])).astype(BF16)
    combf = acc
    combf[...] = jnp.zeros_like(combf)

    token = dest[...]
    hot = (lax.broadcasted_iota(jnp.int32, (16, 64), 0) == token).astype(F32)
    before = (
        lax.broadcasted_iota(jnp.int32, (64, 64), 0) < lax.broadcasted_iota(jnp.int32, (64, 64), 1)
    ).astype(F32)
    rank = jnp.sum(jnp.dot(hot, before, preferred_element_type=F32) * hot, axis=0, keepdims=True)
    target = token * 16 + rank.astype(jnp.int32)
    row = lax.broadcasted_iota(jnp.int32, (256, 64), 0)
    placing = jnp.concatenate(
        [(row == target).astype(F32), (row == target + 8).astype(F32)], axis=1
    ).astype(BF16)

    def ry_copy(f, i):
        return remote(S.at[f, i], R.at[f, i], rys.at[i], ryr.at[f], (p1, p2)[i])

    def rz_copy(f, n):
        return z_parts(T, ZA, ZR, f, n, 64, rzs, rzr)

    def a_copy(j, s):
        dd = (d + s) % 16
        return remote(
            OUT.at[j, pl.ds(pl.multiple_of(dd * 16, 16), 16)],
            A.at[j, pl.ds(pl.multiple_of(d * 16, 16), 16)],
            as_.at[j],
            ar.at[j],
            dps[s - 1],
        )

    def weights_arrive():
        settle(wq.at[pl.ds(0, 8)], cr.at[0])
        settle(wo.at[pl.ds(0, 8)], cr.at[1])
        wo2[...] = wo[...].astype(F32).reshape(wo2.shape).astype(BF16)
        emit(1, wq, wq_o).start()
        emit(2, wo2, wo_o).start()

    def product(i):
        up_copy(i).wait()
        part = lax.dot_general(pg[...], down_v[i % 4, :, 0:V], NT, preferred_element_type=F32)

        @pl.when(i + 4 < N_FEAT)
        def _():
            up_copy(i + 4).start()

        return part.reshape(4, 128, V)

    def z_parts(T, ZA, ZR, f, n, rows, sends, recvs):
        low, high = pl.ds(0, rows // 2), pl.ds(rows // 2, rows // 2)
        source, target = (
            (T.at[f, 1, low], ZA.at[f, 0]),
            (T.at[f, 0, high], ZR.at[f, 0, high]),
            (T.at[f, 1, high], ZA.at[f, 1]),
            (T.at[f, 2, low], ZR.at[f, 1, low]),
            (T.at[f, 0, low], ZR.at[f, 0, low]),
            (T.at[f, 2, high], ZR.at[f, 1, high]),
        )[n]
        up = n in (0, 1, 4)
        return remote(
            source, target, sends.at[n], recvs.at[f, 0 if n in (0, 2) else 1], zp[0] if up else zp[2]
        )

    def z_pass(copy, T, ZA, recvs, f, rows):
        half = rows // 2
        settle(ZA.at[f], recvs.at[f, 0])
        T[f, 0, 0:half] = (T[f, 0, 0:half].astype(F32) + ZA[f, 0].astype(F32)).astype(BF16)
        T[f, 2, half:rows] = (T[f, 2, half:rows].astype(F32) + ZA[f, 1].astype(F32)).astype(BF16)
        copy(f, 4).start()
        copy(f, 5).start()

    def q_copy(f, n):
        return z_parts(QS, QA, QR, f, n, 128, qs, qr)

    def z_product(f, carry):
        part = product(f)
        QS[f] = part[1:4].astype(BF16)
        for n in range(4):
            q_copy(f, n).start()
        Q0[f] = part[0]
        return carry

    def z_sum(f):
        settle(QR.at[f], qr.at[f, 1])
        total = Q0[f] + QR[f, 0].astype(F32) + QR[f, 1].astype(F32)
        S[f, 0, 0] = total[64:96].astype(BF16)
        S[f, 1, 0] = total[96:128].astype(BF16)
        Q0[f, 0:64] = total[0:64]
        for i in range(2):
            qy_copy(f, i).start()

    def qy_copy(f, i):
        return remote(S.at[f, i, 0], R.at[f, i, 0], qys.at[i], ryr.at[f], (p1, p2)[i])

    def z_end(f):
        settle(R.at[f, :, 0], ryr.at[f])
        M[f] = (
            Q0[f, 0:64] + jnp.concatenate([R[f, 0, 0].astype(F32), R[f, 1, 0].astype(F32)], axis=0)
        ).astype(BF16)

    def y_product(f, carry):
        part = product(f)
        S[f, 0] = part[:, 64:96, :].astype(BF16)
        S[f, 1] = part[:, 96:128, :].astype(BF16)
        for h in range(2):
            ry_copy(f, h).start()
        own[f % 4] = part[:, 0:64, :]
        return carry

    def over_y(f):
        settle(R.at[f], ryr.at[f])
        total = own[f % 4] + jnp.concatenate([R[f, 0].astype(F32), R[f, 1].astype(F32)], axis=1)
        T[f] = total[1:4].astype(BF16)
        T0[f % 4] = total[0]
        for n in range(4):
            rz_copy(f, n).start()

    def over_z(f):
        settle(ZR.at[f], rzr.at[f, 1])
        M[f] = (T0[f % 4] + ZR[f, 0].astype(F32) + ZR[f, 1].astype(F32)).astype(BF16)

    def send_rows(j):
        both = jnp.concatenate([M[2 * j], M[2 * j + 1]], axis=0)
        OUT[j] = jnp.dot(placing, both, preferred_element_type=F32).astype(BF16)
        for s in range(1, 16):
            a_copy(j, s).start()
        here = pl.ds(pl.multiple_of(d * 16, 16), 16)
        A[j, here, :] = OUT[j, here, :]

    lax.fori_loop(0, 2, z_product, 0)
    lax.fori_loop(2, 5, y_product, 0)
    x_arrive(1)

    def late_head(h, carry):
        head_step(h)
        return carry

    def sum_step(f, carry):
        over_y(f)

        @pl.when(f + 3 < N_FEAT)
        def _():
            y_product(f + 3, 0)

        @pl.when(f < 4)
        def _():
            z_pass(q_copy, QS, QA, qr, f - 2, 128)

        @pl.when(f == 2)
        def _():
            weights_arrive()

        @pl.when((f == 3) | (f == 4))
        def _():
            z_sum(f - 3)

        @pl.when(f >= 3)
        def _():
            z_pass(rz_copy, T, ZA, rzr, f - 1, 64)

        @pl.when(f == 3)
        def _():
            lax.fori_loop(0, 3, qkv_step, 0)
            emit(4, proj, proj_o).start()

        @pl.when((f == 4) | (f == 5))
        def _():
            z_end(f - 4)
            head_step(f - 4)

        @pl.when(f == 5)
        def _():
            send_rows(jnp.int32(0))

        @pl.when(f >= 6)
        def _():
            lax.fori_loop(2 * f - 10, 2 * f - 8, late_head, 0)

        @pl.when(f >= 4)
        def _():
            over_z(f - 2)

        @pl.when((f == 5) | (f == 7))
        def _():
            send_rows((f - 3) // 2)

        return carry

    lax.fori_loop(2, N_FEAT, sum_step, 0)
    z_pass(rz_copy, T, ZA, rzr, N_FEAT - 1, 64)
    over_z(N_FEAT - 2)
    head_step(6)
    over_z(N_FEAT - 1)
    send_rows(3)
    head_step(7)
    emit(5, prob, prob_o).start()
    normt[...] = norm[...].astype(F32).T.astype(BF16)
    emit(3, normt, normt_o).start()
    output_step()

    fifteen = pl.ds(0, 240)
    for j in range(4):
        pltpu.make_async_copy(A.at[j, fifteen], A.at[j, fifteen], ar.at[j]).wait()
    out_row = lax.broadcasted_iota(jnp.int32, (128, 256), 0)
    in_row = lax.broadcasted_iota(jnp.int32, (128, 256), 1)
    wanted = (out_row % 4) * 64 + (out_row // 32) * 16 + (out_row // 4) % 8
    for h in range(2):
        order = (in_row == wanted + 8 * h).astype(F32).astype(BF16)
        for g in range(4):
            stacked = A[:, 64 * g : 64 * g + 64, :].reshape(256, V)
            cot[128 * g : 128 * g + 128, V * h : V * h + V] = jnp.dot(
                order, stacked, preferred_element_type=F32
            ).astype(BF16)
    emit(0, cot, cot_o).start()

    settle(wq.at[pl.ds(0, 8)], cs.at[0])
    settle(wo.at[pl.ds(0, 8)], cs.at[1])
    settle(wq.at[pl.ds(0, 6)], xs.at[0])
    settle(wo.at[pl.ds(0, 6)], xs.at[1])
    for cp in w_copies((qw, ow), d, ws.at[0], wr.at[0], p2):
        cp.wait_send()
    settle(pre2, ps.at[0])

    edge = N_NARROW * W
    for i in range(2):
        settle(G.at[0, pl.ds(0, 64), pl.ds(0, edge)], zs.at[0, i])
        settle(G.at[0, pl.ds(0, 128), pl.ds(edge, N_TOK * W - edge)], zs.at[1, i])
        settle(G.at[0, pl.ds(0, 64), pl.ds(0, edge // 2)], ns.at[0, i])
        settle(G.at[0, pl.ds(0, 128), pl.ds(0, (N_TOK * W - edge) // 2)], ns.at[1, i])
        settle(G.at[:, pl.ds(0, 32), pl.ds(0, edge)], ys.at[i])
    o_copy(0).wait_send()
    o_copy(1).wait_send()

    for n in range(6):
        settle(T.at[pl.ds(2, N_FEAT - 2), 0, pl.ds(0, 32)], rzs.at[n])
        settle(QS.at[:, 0, pl.ds(0, 64)], qs.at[n])
    for i in range(2):
        settle(S.at[pl.ds(2, N_FEAT - 2), i], rys.at[i])
        settle(S.at[pl.ds(0, 2), i, 0], qys.at[i])
    for j in range(4):
        pltpu.make_async_copy(OUT.at[j, fifteen], OUT.at[j, fifteen], as_.at[j]).wait()
    pairs = [
        (cot, cot_o), (wq, wq_o), (wo2, wo_o), (normt, normt_o), (proj, proj_o),
        (prob, prob_o), (combt, combt_o), (n2, n2_o), (r2, r2_o),
    ]
    for n, (source, target) in enumerate(pairs):
        emit(n, source, target).wait()


def merger(tok, dest, down, up, pre, qw, ow, xin, win, ng, mg):
    vm = pl.BlockSpec(memory_space=pltpu.VMEM)
    hbm = pl.BlockSpec(memory_space=pl.ANY)
    dma = pltpu.SemaphoreType.DMA
    hid = pre.shape[1]
    feat = up.shape[0]
    V = feat // N_FEAT
    kept = [
        ((512, 1280), BF16),
        ((16,) + qw.shape, BF16),
        ((640, 1280), BF16),
        ((1280, 512), BF16),
        ((3, 512, 640), BF16),
        ((8, 4, 128, 256), BF16),
        ((640, 512), BF16),
        ((512, 1280), F32),
        ((512, 1), F32),
    ]
    return pl.pallas_call(
        merger_kernel,
        name="merger",
        out_shape=tuple(jax.ShapeDtypeStruct(*k) for k in kept),
        in_specs=[hbm, vm, hbm, hbm, vm, vm, vm, vm, vm, vm, vm],
        out_specs=(hbm,) * len(kept),
        scratch_shapes=[
            pltpu.VMEM((4, 128, tok.shape[1]), BF16),
            pltpu.VMEM((4, 640, 640), BF16),
            pltpu.VMEM((4, 128, hid), F32),
            pltpu.VMEM((512, hid), F32),
            pltpu.VMEM((512, hid), BF16),
            pltpu.VMEM((128, hid), BF16),
            pltpu.VMEM((N_FEAT, 2, 4, 32, V), BF16),
            pltpu.VMEM((N_FEAT, 2, 4, 32, V), BF16),
            pltpu.VMEM((4, 4, 64, V), F32),
            pltpu.VMEM((N_FEAT, 3, 64, V), BF16),
            pltpu.VMEM((4, 64, V), F32),
            pltpu.VMEM((N_FEAT, 2, 32, V), BF16),
            pltpu.VMEM((N_FEAT, 2, 64, V), BF16),
            pltpu.VMEM((2, 3, 128, V), BF16),
            pltpu.VMEM((2, 2, 64, V), BF16),
            pltpu.VMEM((2, 2, 128, V), BF16),
            pltpu.VMEM((2, 128, V), F32),
            pltpu.VMEM((N_FEAT, 64, V), BF16),
            pltpu.VMEM((4, 256, V), BF16),
            pltpu.VMEM((4, 256, V), BF16),
            pltpu.VMEM((512, 1280), BF16),
            pltpu.VMEM((16,) + qw.shape, BF16),
            pltpu.VMEM((16,) + ow.shape, BF16),
            pltpu.VMEM((640, 1280), BF16),
            pltpu.VMEM((512, 1280), BF16),
            pltpu.VMEM((1280, 512), BF16),
            pltpu.VMEM((3, 512, 640), BF16),
            pltpu.VMEM((8, 4, 128, 256), BF16),
            pltpu.VMEM((640, 512), BF16),
            pltpu.VMEM((512, 1280), F32),
            pltpu.VMEM((512, 1), F32),
            pltpu.VMEM((4, 128, 256), F32),
            dma((1,)),
            dma((4,)),
            dma((2,)), dma((2,)),
            dma((9,)),
            dma((2, 2)), dma((N_TOK,)), dma((2, 2)), dma((N_TOK,)), dma((2,)), dma((N_NARROW,)),
            dma((1,)), dma((1,)),
            dma((1, 2)), dma((1, 2)),
            dma((2,)), dma((2, 2)),
            dma((2,)), dma((2,)),
            dma((2,)), dma((2,)), dma((N_FEAT,)),
            dma((6,)), dma((N_FEAT, 2)),
            dma((6,)), dma((2, 2)),
            dma((4,)), dma((4,)),
        ],
        compiler_params=pltpu.CompilerParams(
            collective_id=1, has_side_effects=True, vmem_limit_bytes=62 << 20
        ),
        cost_estimate=pl.CostEstimate(flops=9 * 10**9, bytes_accessed=40 * 10**6, transcendentals=0),
    )(tok, dest, down, up, pre, qw, ow, xin, win, ng, mg)


def block_kernel(
    cot_i, wq_i, wo_i, normt_i, proj_i, prob_i, combt_i, n2_i, r2_i, xin, ng, mg,
    lg, pout, oout,
    cot, wq, wo, normt, proj, prob, combt, n2, r2,
    db, dc, wof, DP, dpb,
    ga, Ca, Sa, XRa, E1, ZR2, Ea, YRa, Fa, FRa,
    gl, Cl, Zl, ZRl, El2, XRl, El, YRl, Fl, FRl,
    gc, Cc, Zc, ZRc, Ec2, XRc, Ec, YRc, Fc, FRc,
    gm, Cm, Sm, YRm, Em, XRm, Zm, Fm,
    gb, Cb, Sb, YRb, Eb, XRb, Zb, Fb,
    ins, cas, car, xas, xar, z2s, z2r, yas, yar, fas, far,
    cls, clr, zls, zlr, xls, xlr, yls, ylr, fls, flr,
    ccs, ccr, zcs, zcr, xcs, xcr, ycs, ycr, fcs, fcr,
    cms, cmr, yms, ymr, xms, xmr, zms, zmr, pms, pmr,
    cbs, cbr, ybs, ybr, xbs, xbr, zbs, zbr, pbs, pbr,
):
    x, yh, c, z, yl = place()
    pairs = [
        (cot_i, cot), (n2_i, n2), (r2_i, r2), (wo_i, wo), (combt_i, combt), (prob_i, prob), (proj_i, proj),
        (normt_i, normt), (wq_i, wq),
    ]
    loads = [pltpu.make_async_copy(a, b, ins.at[n]) for n, (a, b) in enumerate(pairs)]
    zp = [at(x, yh, c, (z + s) % 4, yl) for s in (1, 2, 3)]
    xp = [at((x + s) % 4, yh, c, z, yl) for s in (1, 2, 3)]
    core = at(x, yh, 1 - c, z, yl)
    p1 = at(x, yh, c, z, 1 - yl)
    p2 = at(x, 1 - yh, c, z, 1 - yl)
    yhp = at(x, 1 - yh, c, z, yl)

    greet(zp + xp + [core, p1, p2, yhp])
    for cp in loads[:3]:
        cp.start()

    def ca_copy(p):
        return remote(ga.at[p, :, 1 - c], Ca.at[p], cas.at[p], car.at[p], core)

    def xa_copy(p, i):
        return remote(
            Sa.at[p, pl.ds((x + i + 1) % 4 * 2, 2)], XRa.at[i, p], xas.at[0], xar.at[p], xp[i]
        )

    def summed_a(p):
        ca_copy(p).wait_recv()
        Sa[p] = (ga[p, :, c].astype(F32) + Ca[p].astype(F32)).astype(BF16)
        for i in (0, 2, 1):
            xa_copy(p, i).start()

    def z2_copy(i):
        t = (z + i + 1) % 4
        return remote(E1.at[t // 2, t % 2], ZR2.at[i], z2s.at[0], z2r.at[0], zp[i])

    def y_first(g, C, S, YR, E, XR, ZZ, F, cs, cr, ys, yr, xs, xr, zs, zr, ps, pr):
        def c_copy(p):
            return remote(g.at[p, :, 1 - c], C.at[p], cs.at[p], cr.at[p], core)

        def y_copy(i):
            return remote(
                S.at[(1 - yl, 1 - yl, yl)[i], (yh, 1 - yh, 1 - yh)[i]],
                YR.at[i],
                ys.at[0],
                yr.at[0],
                (p1, p2, yhp)[i],
            )

        def x_copy(i):
            return remote(E.at[(x + i + 1) % 4], XR.at[i], xs.at[0], xr.at[0], xp[i])

        def z_copy(i):
            return remote(ZZ.at[z], ZZ.at[z], zs.at[0], zr.at[0], zp[i])

        def p_copy():
            return remote(F.at[yl], F.at[yl], ps.at[0], pr.at[0], p1)

        def add_cores(p):
            c_copy(p).wait_recv()
            total = (g[p, :, c].astype(F32) + C[p].astype(F32)).astype(BF16)
            total = total.reshape((4, 2) + total.shape[1:])
            S[p, 0] = total[:, 0]
            S[p, 1] = total[:, 1]

        def start_y():
            for i in range(3):
                y_copy(i).start()

        def add_y():
            settle(YR, yr.at[0])
            mine = S[yl, yh].astype(F32)
            for i in range(3):
                mine = mine + YR[i].astype(F32)
            E[...] = mine.astype(BF16)
            for i in (0, 2, 1):
                x_copy(i).start()

        def add_x():
            settle(XR, xr.at[0])
            mine = E[x].astype(F32)
            for i in range(3):
                mine = mine + XR[i].astype(F32)
            ZZ[z] = mine.astype(BF16)
            for i in (0, 2, 1):
                z_copy(i).start()

        def add_z():
            settle(ZZ.at[pl.ds(0, 3)], zr.at[0])
            total = (ZZ[0].astype(F32) + ZZ[1].astype(F32)) + (ZZ[2].astype(F32) + ZZ[3].astype(F32))
            F[yl] = (total * (1.0 / 128.0)).astype(BF16)
            p_copy().start()

        def finish():
            other = 1 - yl
            pltpu.make_async_copy(F.at[other], F.at[other], pr.at[0]).wait()

        def drain():
            p_copy().wait_send()
            for p in range(2):
                c_copy(p).wait_send()
            settle(YR, ys.at[0])
            settle(XR, xs.at[0])
            settle(ZZ.at[pl.ds(0, 3)], zs.at[0])

        return c_copy, add_cores, start_y, add_y, add_x, add_z, finish, drain

    m_core, m_cores, m_start, m_y, m_x, m_z, m_finish, m_drain = y_first(
        gm, Cm, Sm, YRm, Em, XRm, Zm, Fm, cms, cmr, yms, ymr, xms, xmr, zms, zmr, pms, pmr
    )
    b_core, b_cores, b_start, b_y, b_x, b_z, b_finish, b_drain = y_first(
        gb, Cb, Sb, YRb, Eb, XRb, Zb, Fb, cbs, cbr, ybs, ybr, xbs, xbr, zbs, zbr, pbs, pbr
    )

    owner = yh == z // 2

    def y_copy(i, e, yr, s_sem, r_sem):
        return remote(e, yr.at[i], s_sem.at[0], r_sem.at[0], (p1, p2, yhp)[i])

    def f_copy(i, f, fr, s_sem, r_sem):
        return remote(f, fr.at[z % 2], s_sem.at[0], r_sem.at[z % 2], zp[i])

    def owners_send(e, yr, s_sem, r_sem):
        @pl.when(owner)
        def _():
            y_copy(0, e, yr, s_sem, r_sem).start()

        @pl.when(jnp.logical_not(owner))
        def _():
            for i in (1, 2):
                y_copy(i, e, yr, s_sem, r_sem).start()

    def owners_sum(e, yr, s_sem, r_sem, f, fr, fs_sem, fr_sem):
        @pl.when(owner)
        def _():
            settle(yr, r_sem.at[0])
            total = (e[...].astype(F32) + yr[0].astype(F32)) + (yr[1].astype(F32) + yr[2].astype(F32))
            f[...] = (total * (1.0 / 128.0)).astype(BF16)
            for i in (0, 2, 1):
                f_copy(i, f, fr, fs_sem, fr_sem).start()
            fr[z % 2] = f[...]

    def owners_end(e, yr, s_sem, r_sem, f, fr, fs_sem, fr_sem):
        @pl.when(owner)
        def _():
            settle(e, s_sem.at[0])
            there = 1 - z % 2
            pltpu.make_async_copy(fr.at[there], fr.at[there], fr_sem.at[there]).wait()
            settle(yr, fs_sem.at[0])

        @pl.when(jnp.logical_not(owner))
        def _():
            settle(yr.at[pl.ds(0, 2)], s_sem.at[0])
            for there in range(2):
                pltpu.make_async_copy(fr.at[there], fr.at[there], fr_sem.at[there]).wait()

    def z_first(g, C, Z, ZR, E2, XR, E, YR, F, FR, cs, cr, zs, zr, xs, xr, ys, yr, fs, fr):
        def c_copy(p):
            return remote(g.at[p, :, 1 - c], C.at[p], cs.at[p], cr.at[p], core)

        def z_copy(i):
            t = (z + i + 1) % 4
            return remote(Z.at[t % 2, t // 2], ZR.at[i], zs.at[0], zr.at[0], zp[i])

        def x_copy(i):
            return remote(E2.at[(x + i + 1) % 4], XR.at[i], xs.at[0], xr.at[0], xp[i])

        def add_cores(p):
            c_copy(p).wait_recv()
            total = (g[p, :, c].astype(F32) + C[p].astype(F32)).astype(BF16)
            total = total.reshape((4, 2) + total.shape[1:])
            Z[p, 0] = total[:, 0]
            Z[p, 1] = total[:, 1]
            for i in (0, 2, 1):

                @pl.when((z + i + 1) % 2 == p)
                def _():
                    z_copy(i).start()

        def add_z():
            settle(ZR, zr.at[0])
            mine = Z[z % 2, z // 2].astype(F32)
            for i in range(3):
                mine = mine + ZR[i].astype(F32)
            E2[...] = mine.astype(BF16)
            for i in (0, 2, 1):
                x_copy(i).start()

        def add_x():
            settle(XR, xr.at[0])
            mine = E2[x].astype(F32)
            for i in range(3):
                mine = mine + XR[i].astype(F32)
            E[...] = mine.astype(BF16)
            owners_send(E, YR, ys, yr)

        def add_y():
            owners_sum(E, YR, ys, yr, F, FR, fs, fr)

        def finish():
            owners_end(E, YR, ys, yr, F, FR, fs, fr)

        def drain():
            for p in range(2):
                c_copy(p).wait_send()
            settle(ZR, zs.at[0])
            settle(XR, xs.at[0])

        return c_copy, add_cores, add_z, add_x, add_y, finish, drain

    l_core, l_cores, l_z, l_x, l_y, l_finish, l_drain = z_first(
        gl, Cl, Zl, ZRl, El2, XRl, El, YRl, Fl, FRl, cls, clr, zls, zlr, xls, xlr, yls, ylr, fls, flr
    )
    c_core, c_cores, c_z, c_x, c_y, c_finish, c_drain = z_first(
        gc, Cc, Zc, ZRc, Ec2, XRc, Ec, YRc, Fc, FRc, ccs, ccr, zcs, zcr, xcs, xcr, ycs, ycr, fcs, fcr
    )
    last_a = (Ea, YRa, yas, yar)
    more_a = (Fa, FRa, fas, far)

    loads[0].wait()
    loads[1].wait()
    loads[2].wait()
    for cp in loads[3:]:
        cp.start()

    def out_step(t, carry):
        rows = pl.ds(pl.multiple_of(t * 128, 128), 128)
        slope = cot[rows, :].astype(F32) * mg[...].reshape(1, 1280)
        unit = n2[rows, :]
        grad = r2[rows, :] * (slope - unit * jnp.mean(slope * unit, axis=-1, keepdims=True))
        n2[rows, :] = grad
        db[rows, :] = grad.astype(BF16)
        return carry

    lax.fori_loop(0, 4, out_step, 0)
    loads[3].wait()
    dc[...] = lax.dot_general(db[...], wo[...], NT, preferred_element_type=F32).astype(BF16)
    loads[4].wait()

    def wo_step(t, carry):
        cols = pl.ds(pl.multiple_of(t * 640, 128), 640)
        wof[t] = jnp.dot(combt[...], db[:, cols], preferred_element_type=F32)
        return carry

    lax.fori_loop(0, 2, wo_step, 0)
    grad_o = (
        jnp.concatenate([wof[0].reshape(16, 40, 640), wof[1].reshape(16, 40, 640)], axis=1)
        .astype(BF16)
        .reshape(8, 2, 80, 640)
    )
    gl[1] = grad_o[..., :N_LEFT]
    gm[1] = grad_o[..., N_LEFT:]
    met(zp + xp + [core, p1, p2, yhp])
    l_core(1).start()
    m_core(1).start()

    DP[...] = jnp.zeros_like(DP)
    loads[5].wait()

    def value_step(h, carry):
        lanes, mask = head_lanes(h)
        parts = [
            lax.dot_general(
                prob[h, b], dc[pl.ds(128 * b, 128), lanes] * mask, TN, preferred_element_type=F32
            )
            for b in range(4)
        ]
        DP[2, :, lanes] += overlap(parts)
        return carry

    lax.fori_loop(0, 8, value_step, 0)
    loads[7].wait()
    def part_grad(p, first, width):
        cols = slice(first, first + width)
        dpb[p, :, cols] = DP[p, :, cols].astype(BF16)
        grad = jnp.dot(normt[...], dpb[p, :, cols], preferred_element_type=F32)
        return grad.astype(BF16).reshape(8, 2, 80, width)

    gl[0] = part_grad(2, 0, N_LEFT)
    l_core(0).start()
    gm[0] = part_grad(2, N_LEFT, 640 - N_LEFT)
    m_core(0).start()
    l_cores(1)
    m_cores(1)
    loads[6].wait()

    def head_step(h, carry):
        lanes, mask = head_lanes(h)
        slopes = []
        for b in range(4):
            grad = dc[pl.ds(128 * b, 128), lanes] * mask
            wide = prob[h, b].astype(F32)
            slope = lax.dot_general(
                grad, proj[2, pl.ds(KEYS[b], 256), lanes], NT, preferred_element_type=F32
            )
            slope = wide * (slope - jnp.sum(slope * wide, axis=-1, keepdims=True)) * HEAD_DIM ** (-0.5)
            slopes.append(slope.astype(BF16))
        parts = [
            jnp.dot(slopes[b], proj[1, pl.ds(KEYS[b], 256), lanes] * mask, preferred_element_type=F32)
            for b in range(4)
        ]
        DP[0, :, lanes] += jnp.concatenate(parts, axis=0)
        parts = [
            lax.dot_general(
                slopes[b], proj[0, pl.ds(128 * b, 128), lanes] * mask, TN, preferred_element_type=F32
            )
            for b in range(4)
        ]
        DP[1, :, lanes] += overlap(parts)

        @pl.when(h == 0)
        def _():
            l_cores(0)
            m_cores(0)
            m_start()

        @pl.when(h == 3)
        def _():
            for p in range(2):
                ga[p] = part_grad(p, 0, N_X)
                ca_copy(p).start()

        @pl.when(h == 5)
        def _():
            summed_a(0)
            summed_a(1)

        @pl.when(h == 6)
        def _():
            for p in range(2):
                gc[p] = part_grad(p, N_X, N_Z)
                c_core(p).start()

        return carry

    lax.fori_loop(0, 8, head_step, 0)
    for p in range(2):
        gb[p] = part_grad(p, N_X + N_Z, 640 - N_X - N_Z)
        b_core(p).start()
    m_y()
    c_cores(0)
    c_cores(1)

    def input_dot(half):
        total = jnp.zeros((512, 640), F32)
        for p in range(3):
            total += lax.dot_general(
                dpb[p],
                wq[8 * half : 8 * half + 8, :, 640 * p : 640 * p + 640].reshape(640, 640),
                NT,
                preferred_element_type=F32,
            )
        wof[half, 0:512, :] = total

    loads[8].wait()
    input_dot(0)
    b_cores(0)
    b_cores(1)
    b_start()
    l_z()

    for p in range(2):
        settle(XRa.at[:, p], xar.at[p])
        mine = Sa[p, pl.ds(2 * x, 2)].astype(F32)
        for i in range(3):
            mine = mine + XRa[i, p].astype(F32)
        E1[0, p] = mine[0].astype(BF16)
        E1[1, p] = mine[1].astype(BF16)
    for i in (0, 2, 1):
        z2_copy(i).start()
    input_dot(1)
    m_x()
    l_x()

    def input_step(t, carry):
        rows = pl.ds(pl.multiple_of(t * 128, 128), 128)
        slope = jnp.concatenate([wof[0, rows, :], wof[1, rows, :]], axis=1)
        slope = slope.astype(BF16).astype(F32) * ng[...].reshape(1, 1280)
        value = xin[rows, :].astype(F32)
        factor = lax.rsqrt(jnp.mean(value * value, axis=-1, keepdims=True) + EPSILON)
        unit = value * factor
        grad = factor * (slope - unit * jnp.mean(slope * unit, axis=-1, keepdims=True))
        lg[rows, :] = (grad + n2[rows, :]).astype(BF16)
        return carry

    lax.fori_loop(0, 4, input_step, 0)

    c_z()
    b_y()
    settle(ZR2, z2r.at[0])
    mine = E1[z // 2, z % 2].astype(F32)
    for i in range(3):
        mine = mine + ZR2[i].astype(F32)
    Ea[...] = mine.astype(BF16)
    owners_send(*last_a)
    m_z()
    l_y()
    b_x()
    c_x()
    owners_sum(*last_a, *more_a)
    b_z()
    c_y()

    m_finish()
    l_finish()
    pout[:, 1280 : 1280 + N_LEFT] = FRl[0].astype(F32)
    pout[:, 1280 + N_LEFT : 1920] = Fm[0].astype(F32)
    left, right = FRl[1].astype(F32), Fm[1].astype(F32)
    oout[:, 0:N_LEFT] = left[0:40]
    oout[:, N_LEFT:640] = right[0:40]
    oout[:, 640 : 640 + N_LEFT] = left[40:80]
    oout[:, 640 + N_LEFT : 1280] = right[40:80]
    owners_end(*last_a, *more_a)
    c_finish()
    b_finish()
    for p in range(2):
        first = 640 * p
        pout[:, first : first + N_X] = FRa[p].astype(F32)
        pout[:, first + N_X : first + N_X + N_Z] = FRc[p].astype(F32)
        pout[:, first + N_X + N_Z : first + 640] = Fb[p].astype(F32)

    for drain in (m_drain, b_drain, l_drain, c_drain):
        drain()
    for p in range(2):
        ca_copy(p).wait_send()
    settle(XRa, xas.at[0])
    settle(ZR2, z2s.at[0])


def block_grads(cot, wq, wo, normt, proj, prob, combt, n2, r2, xin, ng, mg):
    vm = pl.BlockSpec(memory_space=pltpu.VMEM)
    hbm = pl.BlockSpec(memory_space=pl.ANY)
    dma = pltpu.SemaphoreType.DMA
    tl, tm = (80, N_LEFT), (80, 640 - N_LEFT)
    ta, tc, tb = (80, N_X), (80, N_Z), (80, 640 - N_X - N_Z)
    held = (cot, wq, wo, normt, proj, prob, combt, n2, r2)
    return pl.pallas_call(
        block_kernel,
        name="block",
        out_shape=(
            jax.ShapeDtypeStruct((512, 1280), BF16),
            jax.ShapeDtypeStruct((80, 1920), F32),
            jax.ShapeDtypeStruct((40, 1280), F32),
        ),
        in_specs=[hbm] * 9 + [vm] * 3,
        out_specs=(vm, vm, vm),
        scratch_shapes=[pltpu.VMEM(k.shape, k.dtype) for k in held]
        + [
            pltpu.VMEM((512, 1280), BF16),
            pltpu.VMEM((512, 640), BF16),
            pltpu.VMEM((2, 640, 640), F32),
            pltpu.VMEM((3, 512, 640), F32),
            pltpu.VMEM((3, 512, 640), BF16),
            pltpu.VMEM((2, 8, 2) + ta, BF16),
            pltpu.VMEM((2, 8) + ta, BF16),
            pltpu.VMEM((2, 8) + ta, BF16),
            pltpu.VMEM((3, 2, 2) + ta, BF16),
            pltpu.VMEM((2, 2) + ta, BF16),
            pltpu.VMEM((3,) + ta, BF16),
            pltpu.VMEM(ta, BF16),
            pltpu.VMEM((3,) + ta, BF16),
            pltpu.VMEM(ta, BF16),
            pltpu.VMEM((2,) + ta, BF16),
        ]
        + [
            pltpu.VMEM(lead + t, BF16)
            for t in (tl, tc)
            for lead in ((2, 8, 2), (2, 8), (2, 2, 4), (3, 4), (4,), (3,), (), (3,), (), (2,))
        ]
        + [
            pltpu.VMEM(lead + t, BF16)
            for t in (tm, tb)
            for lead in ((2, 8, 2), (2, 8), (2, 2, 4), (3, 4), (4,), (3,), (4,), (2,))
        ]
        + [dma((9,))]
        + [dma((n,)) for n in (2, 2, 1, 2, 1, 1, 1, 1, 1, 2)]
        + [dma((n,)) for n in (2, 2, 1, 1, 1, 1, 1, 1, 1, 2) * 2]
        + [dma((n,)) for n in (2, 2, 1, 1, 1, 1, 1, 1, 1, 1) * 2],
        compiler_params=pltpu.CompilerParams(
            collective_id=2, has_side_effects=True, vmem_limit_bytes=62 << 20
        ),
        cost_estimate=pl.CostEstimate(flops=8 * 10**9, bytes_accessed=40 * 10**6, transcendentals=0),
    )(cot, wq, wo, normt, proj, prob, combt, n2, r2, xin, ng, mg)


def finish_kernel(a, b, c, out_a, out_b, out_c):
    out_a[...] = a[...]
    out_b[...] = b[...]
    out_c[...] = c[...]


def finish(*arrays):
    vm = pl.BlockSpec(memory_space=pltpu.VMEM)
    return pl.pallas_call(
        finish_kernel,
        name="finish",
        out_shape=tuple(jax.ShapeDtypeStruct(k.shape, k.dtype) for k in arrays),
        in_specs=[vm] * 3,
        out_specs=(vm,) * 3,
    )(*arrays)


def local(
    token_grads,
    token_dest,
    merger_down,
    merger_up,
    merger_pre,
    layer_input,
    window_ids,
    norm_gain,
    merge_gain,
    qkv_weight,
    proj_weight,
):
    kept = merger(
        token_grads, token_dest.reshape(1, 64), merger_down, merger_up, merger_pre, qkv_weight, proj_weight,
        layer_input, window_ids, norm_gain, merge_gain,
    )
    return finish(*block_grads(*kept, layer_input, norm_gain, merge_gain))


def solution(mesh):
    return jax.shard_map(
        local,
        mesh=mesh,
        in_specs=(
            P(("dp", "llm"), None),
            P(("dp", "llm"), None),
            P("llm", None),
            P(None, "llm"),
            P("dp", "llm"),
            P(("dp", "llm"), None),
            P(("dp", "llm"), None),
            P(),
            P(),
            P("dp", None),
            P("dp", None),
        ),
        out_specs=(P(("dp", "llm"), None), P("dp", None), P("dp", None)),
        check_vma=False,
    )
```
